32 devices in a mesh: head: 2 (over y), blk: 16 (over z, x, core).
Axes of the slice: x: 2, y: 2, z: 4, core: 2. Of those that a mesh axis runs over, the one named last changes fastest.
Arguments:
- hidden_in: float32 [8192, 1, 768], P(('head', 'blk')), may hold values from -6 to 6
- w_query: bfloat16 [768, 768], P(('head', 'blk')), may hold values from -0.21875 to 0.21875
- w_key: bfloat16 [768, 768], P(('head', 'blk')), may hold values from -0.21875 to 0.21875
- w_value: bfloat16 [768, 768], P(('head', 'blk')), may hold values from -0.21875 to 0.21875
- w_out: bfloat16 [768, 768], P(('head', 'blk')), may hold values from -6 to 6
- norm_attn: bfloat16 [768], P(('head', 'blk')), may hold values from 0.5 to 1.5
- norm_ffn: bfloat16 [768], P(('head', 'blk')), may hold values from 0.5 to 1.5
- w_router: bfloat16 [768, 16], P(('head', 'blk')), may hold values from -0.21875 to 0.21875
- shared_gate: bfloat16 [768, 2048], P(('head', 'blk')), may hold values from -0.21875 to 0.21875
- shared_up: bfloat16 [768, 2048], P(('head', 'blk')), may hold values from -0.21875 to 0.21875
- shared_down: bfloat16 [2048, 768], P(('head', 'blk')), may hold values from -0.125 to 0.125
- expert_gate: bfloat16 [768, 32768], P(None, ('head', 'blk')), may hold values from -0.21875 to 0.21875
- expert_up: bfloat16 [768, 32768], P(None, ('head', 'blk')), may hold values from -0.21875 to 0.21875
- expert_down: bfloat16 [32768, 768], P(('head', 'blk')), may hold values from -0.125 to 0.125
- teacher: float32 [8192, 1, 768], P(('head', 'blk')), may hold values from -5 to 5
- routes: int32 [8192, 1, 2], P(('head', 'blk')), may hold values from 0 to 15, all different within a row; in each aligned block of 256 rows (0 to 255, 256 to 511, ..., all dimensions but the last counted through in order) at most 64 rows name the same one
- cont_lengths: int32 [1, 8], replicated, may hold values from 256 to 768, as said below
- valid_mask: int32 [8192, 1], P(('head', 'blk')), may hold values from 0 to 1, as said below
Outputs:
- layer_out: float32 [8192, 1, 768], P(('head', 'blk'))
- input_grad: float32 [8192, 1, 768], P(('head', 'blk'))
- loss_value: float32 [], replicated
- grad_query: float32 [768, 768], P(('head', 'blk'))
- grad_key: float32 [768, 768], P(('head', 'blk'))
- grad_value: float32 [768, 768], P(('head', 'blk'))
- grad_out: float32 [768, 768], P(('head', 'blk'))
- grad_norm_attn: float32 [768], P(('head', 'blk'))
- grad_norm_ffn: float32 [768], P(('head', 'blk'))
- grad_router: float32 [768, 16], P(('head', 'blk'))
- grad_shared_gate: float32 [768, 2048], P(('head', 'blk'))
- grad_shared_up: float32 [768, 2048], P(('head', 'blk'))
- grad_shared_down: float32 [2048, 768], P(('head', 'blk'))
- grad_expert_gate: float32 [768, 32768], P(None, ('head', 'blk'))
- grad_expert_up: float32 [768, 32768], P(None, ('head', 'blk'))
- grad_expert_down: float32 [32768, 768], P(('head', 'blk'))
The draws below stay inside these ranges and needn't reach their ends.
Inputs may be any that keep to these rules, and one draw needn't show every extreme that they name: `routes`: the 2 experts of a token differ; among the tokens of one device (aligned blocks of 256 tokens, positions then groups) no expert is named more than 64 times, a bound that some block reaches. `cont_lengths`: a group's prompt fills its positions 0 to 4095 and its 8 continuations follow in order with these lengths, which add up to 4096 in each group. `valid_mask`: position 0 of every group is valid.
All inputs are finite; a program needn't handle non-finite values.
Results may differ from the reference program's by a relative error of at most 0.039.
Values may be sent and summed in bfloat16 or wider, within the bound.
A program may use at most 768 MiB of HBM per device.

```python
import math
import jax
import jax.numpy as jnp
import numpy as np
from jax import lax

D = 768
HEADS = 12
HEAD_DIM = 64
FF = 2048
EXPERTS = 16
TOP = 2
PROMPT = 4096
CONTS = 8
CONT_LEN = 512
TOK_DEV = 256
GROUP_TOK = 8192
GROUPS = 1
CAP = 64
N_HEAD = 2
N_BLK = 16


def draw_teacher(key, part):
    key = jax.random.fold_in(key, 11)
    return jnp.clip(jax.random.normal(key, (GROUP_TOK, GROUPS, D), jnp.float32), -5.0, 5.0)


def draw_cont_lengths(key, part):
    key = jax.random.fold_in(key, 12)
    first_key, second_key, third_key = jax.random.split(key, 3)
    half_len = CONT_LEN // 2
    pair_count = CONTS // 2
    offsets_pair = jax.random.randint(first_key, (GROUPS, pair_count), -half_len, half_len + 1)
    picked_pair = jax.random.randint(second_key, (GROUPS,), 0, pair_count)
    direction = 2 * jax.random.randint(third_key, (GROUPS,), 0, 2) - 1
    pair_ids = jnp.arange(pair_count, dtype=jnp.int32)
    offsets_pair = jnp.where(pair_ids[None, :] == picked_pair[:, None], half_len * direction[:, None], offsets_pair)
    lengths = jnp.stack([CONT_LEN + offsets_pair, CONT_LEN - offsets_pair], axis=-1).reshape(GROUPS, CONTS)
    return lengths.astype(jnp.int32)


def draw_valid_mask(key, part):
    key = jax.random.fold_in(key, 13)
    row_ids = jnp.arange(GROUP_TOK, dtype=jnp.int32)
    threshold = 250 + 500 * row_ids // GROUP_TOK
    lottery = jax.random.randint(key, (GROUP_TOK, GROUPS), 0, 1000)
    chosen = (lottery < threshold[:, None]).astype(jnp.int32)
    return jnp.where(row_ids[:, None] == 0, 1, chosen).astype(jnp.int32)


def levels(own_key, extent, cuts, least, largest):
    def one(axis_at, blocks):
        steps = jax.random.uniform(jax.random.fold_in(jax.random.fold_in(own_key, 6), axis_at), (blocks,), jnp.float32, least / len(cuts), largest / len(cuts))
        return jnp.repeat(jnp.exp(steps), extent[axis_at] // blocks).reshape((-1,) + (1,) * (len(extent) - axis_at - 1))

    gain = one(*cuts[0])
    for cut in cuts[1:]:
        gain = gain * one(*cut)
    return gain


def assign_block(own_key, own, number, rows, count, top, limit, lean):
    sequence = jax.random.permutation(own_key, count)
    packed, ordinary = portions_of(count, rows * top, limit, lean, True), portions_of(count, rows * top, limit, lean, False)
    places = jnp.arange(count)

    def named(tallies, offset_by):
        used = int((tallies > 0).sum())
        fixed = max(1, used // 4)
        shifted = fixed + (places - fixed + offset_by * (used - fixed)) % max(1, count - fixed)
        return jnp.zeros((count,), jnp.int32).at[sequence[jnp.where(places < fixed, places, shifted)]].set(jnp.asarray(tallies, jnp.int32))

    tallies = jnp.where(number % 4 == 0, named(packed, number // 4), named(ordinary, number - number // 4 - 1))
    mixed = jax.random.permutation(jax.random.fold_in(own, 3), count)
    giver, receiver = mixed[0:count // 2 * 2:2], mixed[1:count // 2 * 2:2]
    slack = jnp.minimum(tallies[giver] - 1, limit - tallies[receiver]) // 2
    slack = jnp.where((giver == sequence[0]) | (receiver == sequence[0]) | (tallies[receiver] == 0), 0, jnp.maximum(slack, 0))
    shifted = jax.random.randint(jax.random.fold_in(own, 4), (count // 2,), 0, 1 << 20) % (slack + 1)
    tallies = tallies.at[giver].add(-shifted).at[receiver].add(shifted)
    items = jnp.searchsorted(jnp.cumsum(tallies), jnp.arange(rows * top), side="right").astype(jnp.int32)
    listing = items.reshape(top, rows).T
    listing = listing[jax.random.permutation(jax.random.fold_in(own, 1), rows)]
    offset_by = jax.random.randint(jax.random.fold_in(own, 2), (rows, 1), 0, top)
    return jnp.take_along_axis(listing, (jnp.arange(top)[None, :] + offset_by) % top, axis=1)


def portions_of(count, total, limit, skew, full):
    weights = [(1 << 20) // math.isqrt(grade ** skew) + 1 for grade in range(1, count + 1)]
    largest = limit if full else min(limit, max(-(-total // count), total * weights[0] // sum(weights)))
    least = 1 if total - largest >= count - 1 else 0
    holding, rest = [largest] + [least] * (count - 1), total - largest - least * (count - 1)
    while rest > 0:
        movable = [i for i in range(1, count) if holding[i] < largest] or [i for i in range(1, count) if holding[i] < limit]
        mass, remaining = sum([weights[i] for i in movable]), rest
        for i in movable:
            addition = min(limit - holding[i], max(1, remaining * weights[i] // mass), rest)
            holding[i] = holding[i] + addition
            rest = rest - addition
    return np.array(holding)


def centred(own_key, shape, width, limit, shards=(), kind=jnp.bfloat16):
    level = levels(own_key, shape, shards, -0.22, 0.18) if shards else 1.0
    entries = jax.random.normal(own_key, shape, jnp.float32) * width * level
    return jnp.minimum(jnp.maximum(entries, -limit), limit).astype(kind)


def setup_inputs(seed: int = 0) -> dict:
    splits = jax.random.split(jax.random.key(seed), 19)
    hidden_in = centred(splits[0], (GROUP_TOK, GROUPS, D), 1.0, 6.0, ((0, 32),), jnp.float32)
    w_query = centred(splits[1], (D, D), D ** -0.5, 0.21875, ((0, 32),))
    w_key = centred(splits[2], (D, D), D ** -0.5, 0.21875, ((0, 32),))
    w_value = centred(splits[3], (D, D), D ** -0.5, 0.21875, ((0, 32),))
    w_out = centred(splits[4], (D, D), 1 ** -0.5, 6.0, ((0, 32),))
    norm_attn = jnp.clip(1.0 + 0.1 * jax.random.normal(splits[5], (D,), jnp.float32), 0.5, 1.5).astype(jnp.bfloat16)
    norm_ffn = jnp.clip(1.0 + 0.1 * jax.random.normal(splits[6], (D,), jnp.float32), 0.5, 1.5).astype(jnp.bfloat16)
    w_router = centred(splits[7], (D, EXPERTS), D ** -0.5, 0.21875, ((0, 32),))
    shared_gate = centred(splits[8], (D, FF), D ** -0.5, 0.21875, ((0, 32),))
    shared_up = centred(splits[9], (D, FF), D ** -0.5, 0.21875, ((0, 32),))
    shared_down = centred(splits[10], (FF, D), FF ** -0.5, 0.125, ((0, 32),))
    expert_gate = centred(splits[11], (D, EXPERTS * FF), D ** -0.5, 0.21875, ((1, 32),))
    expert_up = centred(splits[12], (D, EXPERTS * FF), D ** -0.5, 0.21875, ((1, 32),))
    expert_down = centred(splits[13], (EXPERTS * FF, D), FF ** -0.5, 0.125, ((0, 32),))
    teacher = draw_teacher(jax.random.fold_in(splits[18], 71), 0)
    routes_keys = jax.random.split(jax.random.fold_in(splits[15], 1), GROUP_TOK * GROUPS // TOK_DEV)
    routes_turns = jax.random.permutation(jax.random.fold_in(splits[15], 3), GROUP_TOK * GROUPS // TOK_DEV)
    routes = jax.vmap(lambda own, number: assign_block(jax.random.fold_in(splits[15], 2), own, number, TOK_DEV, EXPERTS, TOP, CAP, 1))(routes_keys, routes_turns).reshape((GROUP_TOK, GROUPS, TOP))
    cont_lengths = draw_cont_lengths(jax.random.fold_in(splits[18], 71), 0)
    valid_mask = draw_valid_mask(jax.random.fold_in(splits[18], 71), 0)
    return {"hidden_in": hidden_in, "w_query": w_query, "w_key": w_key, "w_value": w_value, "w_out": w_out, "norm_attn": norm_attn, "norm_ffn": norm_ffn, "w_router": w_router, "shared_gate": shared_gate, "shared_up": shared_up, "shared_down": shared_down, "expert_gate": expert_gate, "expert_up": expert_up, "expert_down": expert_down, "teacher": teacher, "routes": routes, "cont_lengths": cont_lengths, "valid_mask": valid_mask}


@jax.custom_vjp
def low(v):
    return lax.optimization_barrier(v.astype(jnp.bfloat16)).astype(jnp.float32)

@jax.custom_vjp
def low_back(v):
    return v

def low_keep(v):
    return (low(v), None)

def low_pass(kept, grad):
    return (grad,)

def back_keep(v):
    return (v, None)

def back_low(kept, grad):
    return (low(grad),)
low.defvjp(low_keep, low_pass)
low_back.defvjp(back_keep, back_low)
EPSILON = 1e-06
NEGATIVE = -1e+30
HIGHEST = lax.Precision.HIGHEST

def matmul_high(left, right):
    return jnp.dot(left, right, precision=HIGHEST, preferred_element_type=jnp.float32)

def apply_silu(argument):
    return argument * jax.nn.sigmoid(argument)

def root_norm(inputs, gain_vec):
    scaling = lax.rsqrt(lax.optimization_barrier(jnp.mean(inputs * inputs, axis=-1, keepdims=True)) + EPSILON)
    return inputs * scaling * gain_vec

def segment_starts(positions, cont_lengths):
    run_ends = jnp.cumsum(cont_lengths, axis=1).astype(jnp.int32)
    begins = (PROMPT + run_ends - cont_lengths).astype(jnp.int32)
    passed = begins[None, :, :] <= positions[:, None, None]
    return lax.optimization_barrier(jnp.max(jnp.where(passed, begins[None], 0), axis=-1)).astype(jnp.int32)

def rotary_tables(positions, run_begin):
    relative = jnp.where(positions[:, None] < PROMPT, positions[:, None], PROMPT + positions[:, None] - run_begin)
    angle_pos = relative.astype(jnp.float32)
    half_dim = HEAD_DIM // 2
    frequency = jnp.exp(jnp.arange(half_dim, dtype=jnp.int32).astype(jnp.float32) * (-2.0 * math.log(10000.0) / HEAD_DIM))
    angles = angle_pos[:, :, None, None] * frequency
    return (jnp.cos(angles), jnp.sin(angles))

def rotate(inputs, cosine_table, sine_table):
    half_dim = inputs.shape[-1] // 2
    first_half = inputs[..., :half_dim]
    second_half = inputs[..., half_dim:]
    return jnp.concatenate([first_half * cosine_table - second_half * sine_table, second_half * cosine_table + first_half * sine_table], axis=-1)

def attend_block(block_queries, group_keys, group_values, block_pos, block_begin, score_scale):
    scores = low_back(jnp.einsum('hqd,hkd->hqk', block_queries, group_keys, precision=HIGHEST) * score_scale)
    key_pos = jnp.arange(GROUP_TOK, dtype=jnp.int32)
    allowed = (key_pos[None, :] <= block_pos[:, None]) & ((key_pos[None, :] < PROMPT) | (key_pos[None, :] >= block_begin[:, None]))
    scores = jnp.where(allowed[None], scores, NEGATIVE)
    row_top = lax.optimization_barrier(jnp.max(scores, axis=-1, keepdims=True))
    weights = jnp.where(allowed[None], jnp.exp(scores - row_top), 0.0)
    row_total = lax.optimization_barrier(jnp.sum(weights, axis=-1, keepdims=True))
    return jnp.einsum('hqk,hkd->hqd', low(weights), group_values, precision=HIGHEST) / row_total

def expert_slots(per_device, devices):
    onehot = (per_device[:, :, None] == jnp.arange(EXPERTS, dtype=jnp.int32)).astype(jnp.int32)
    ranking = lax.optimization_barrier(jnp.sum((jnp.cumsum(onehot, axis=1) - 1) * onehot, axis=-1))
    device_ids = jnp.arange(devices, dtype=jnp.int32)[:, None]
    flat_slot = (per_device * (devices * CAP) + device_ids * CAP + ranking).astype(jnp.int32).reshape(-1)
    owners = (jnp.arange(flat_slot.shape[0], dtype=jnp.int32) // TOP).astype(jnp.int32)
    slot_table = jnp.full((EXPERTS * devices * CAP,), owners.shape[0] // TOP, jnp.int32).at[flat_slot].set(owners)
    return (flat_slot.reshape(-1, TOP), slot_table)

def reference(hidden_in, w_query, w_key, w_value, w_out, norm_attn, norm_ffn, w_router, shared_gate, shared_up, shared_down, expert_gate, expert_up, expert_down, teacher, routes, cont_lengths, valid_mask):
    token_count = GROUP_TOK * GROUPS
    devices = N_HEAD * N_BLK
    positions = jnp.arange(GROUP_TOK, dtype=jnp.int32)
    run_begin = segment_starts(positions, cont_lengths)
    cosine_table, sine_table = rotary_tables(positions, run_begin)
    slot_index, slot_table = expert_slots(routes.reshape(devices, TOK_DEV * TOP), devices)
    route_flat = routes.reshape(token_count, TOP).astype(jnp.int32)
    block_rows = min(512, GROUP_TOK)
    block_count = GROUP_TOK // block_rows
    score_scale = HEAD_DIM ** (-0.5)

    def forward(inputs, query_mat, key_mat, value_mat, out_mat, gain_attn, gain_ffn, route_mat, share_gate, share_up, share_down, gate_cols, up_cols, down_rows):
        flat_in = inputs.reshape(token_count, D)
        normed_attn = low(root_norm(flat_in, gain_attn))
        head_shape = (GROUP_TOK, GROUPS, HEADS, HEAD_DIM)
        query_raw = low_back(matmul_high(normed_attn, query_mat)).reshape(head_shape)
        key_raw = low_back(matmul_high(normed_attn, key_mat)).reshape(head_shape)
        value_rows = low_back(low(matmul_high(normed_attn, value_mat))).reshape(head_shape)
        query_rows = low_back(low(rotate(query_raw, cosine_table, sine_table)))
        key_rows = low_back(low(rotate(key_raw, cosine_table, sine_table)))
        query_heads = query_rows.transpose(1, 2, 0, 3)
        key_heads = key_rows.transpose(1, 2, 0, 3)
        value_heads = value_rows.transpose(1, 2, 0, 3)

        def one_block(block_index):
            group_id = block_index // block_count
            block_id = block_index % block_count
            first_row = block_id * block_rows
            group_queries = lax.dynamic_index_in_dim(query_heads, group_id, 0, keepdims=False)
            block_queries = lax.dynamic_slice_in_dim(group_queries, first_row, block_rows, 1)
            group_keys = lax.dynamic_index_in_dim(key_heads, group_id, 0, keepdims=False)
            group_values = lax.dynamic_index_in_dim(value_heads, group_id, 0, keepdims=False)
            begin_col = lax.dynamic_index_in_dim(run_begin, group_id, 1, keepdims=False)
            block_begin = lax.dynamic_slice_in_dim(begin_col, first_row, block_rows, 0)
            block_pos = (first_row + jnp.arange(block_rows, dtype=jnp.int32)).astype(jnp.int32)
            return attend_block(block_queries, group_keys, group_values, block_pos, block_begin, score_scale)
        attended = lax.map(jax.checkpoint(one_block), jnp.arange(GROUPS * block_count, dtype=jnp.int32))
        attended = attended.reshape(GROUPS, block_count, HEADS, block_rows, HEAD_DIM).transpose(1, 3, 0, 2, 4).reshape(token_count, D)
        attended = low_back(low(attended))
        residual_mid = flat_in + low_back(matmul_high(attended, out_mat))
        normed_ffn = low(root_norm(residual_mid, gain_ffn))
        logits = low_back(matmul_high(normed_ffn, route_mat))
        chosen = jnp.take_along_axis(logits, route_flat, axis=1)
        gate_probs = jax.nn.softmax(chosen, axis=1)
        shared_gate_in = low_back(matmul_high(normed_ffn, share_gate))
        shared_up_in = low_back(matmul_high(normed_ffn, share_up))
        shared_out = low_back(matmul_high(low(apply_silu(shared_gate_in) * shared_up_in), share_down))
        padded = jnp.concatenate([normed_ffn, jnp.zeros((1, D), jnp.float32)], axis=0)
        gate_stack = gate_cols.reshape(D, EXPERTS, FF).transpose(1, 0, 2)
        up_stack = up_cols.reshape(D, EXPERTS, FF).transpose(1, 0, 2)
        down_stack = down_rows.reshape(EXPERTS, FF, D)

        def one_expert(operands):
            table_row, gate_part, up_part, down_part = operands
            picked = jnp.take(padded, table_row, axis=0)
            inner_gate = low_back(matmul_high(picked, gate_part))
            inner_up = low_back(matmul_high(picked, up_part))
            return matmul_high(low(apply_silu(inner_gate) * inner_up), down_part)
        expert_out = lax.map(jax.checkpoint(one_expert), (slot_table.reshape(EXPERTS, -1), gate_stack, up_stack, down_stack)).reshape(-1, D)
        routed_first = low_back(jnp.take(expert_out, slot_index[:, 0], axis=0))
        routed_second = low_back(jnp.take(expert_out, slot_index[:, 1], axis=0))
        mixture = gate_probs[:, 0:1] * routed_first + gate_probs[:, 1:2] * routed_second
        return (residual_mid + shared_out + mixture).reshape(GROUP_TOK, GROUPS, D)
    layer_out, pullback = jax.vjp(forward, hidden_in, w_query.astype(jnp.float32), w_key.astype(jnp.float32), w_value.astype(jnp.float32), w_out.astype(jnp.float32), norm_attn.astype(jnp.float32), norm_ffn.astype(jnp.float32), w_router.astype(jnp.float32), shared_gate.astype(jnp.float32), shared_up.astype(jnp.float32), shared_down.astype(jnp.float32), expert_gate.astype(jnp.float32), expert_up.astype(jnp.float32), expert_down.astype(jnp.float32))
    valid_total = jnp.sum(valid_mask).astype(jnp.float32)
    keep_rows = valid_mask.astype(jnp.float32)[..., None]
    deviation = layer_out - teacher
    loss_value = jnp.sum(keep_rows * deviation * deviation) / (valid_total * D)
    cotangent = keep_rows * deviation * (token_count / valid_total)
    gradients = pullback(cotangent)
    return (layer_out, gradients[0], loss_value, gradients[1], gradients[2], gradients[3], gradients[4], gradients[5], gradients[6], gradients[7], gradients[8], gradients[9], gradients[10], gradients[11], gradients[12], gradients[13])
```

```python
import functools
import math

import jax
import jax.numpy as jnp
from jax import lax
from jax.experimental import pallas as pl
from jax.experimental.pallas import tpu as pltpu
from jax.sharding import PartitionSpec as P

HEADS = 12
HEAD_DIM = 64
EXPERTS = 16
TOP = 2
PROMPT = 4096
LONGEST = 768
CAP = 64

EPSILON = 1e-06
NEGATIVE = -1e30
SCORE_SCALE = HEAD_DIM ** (-0.5)
EXP_SCALE = SCORE_SCALE * math.log2(math.e)

TILE = 256
FWD_WIDE, FWD_MASK = 8, 4
BWD_WIDE, BWD_MASK = 4, 2

MESH_ID = pl.DeviceIdType.MESH
AXES = ("head", "blk")


def apply_silu(argument):
    return argument * jax.nn.sigmoid(argument)


def silu_slope(argument):
    sigmoid_val = jax.nn.sigmoid(argument)
    return sigmoid_val * (1.0 + argument * (1.0 - sigmoid_val))


def root_norm(inputs, gain_vec):
    scaling = lax.rsqrt(jnp.mean(inputs * inputs, axis=-1, keepdims=True) + EPSILON)
    return (inputs * scaling * gain_vec, scaling)


def root_norm_back(inputs, scaling, gain_vec, upstream):
    weighted = gain_vec * upstream
    through = scaling * weighted - inputs * scaling**3 * jnp.mean(
        weighted * inputs, axis=-1, keepdims=True
    )
    return (through, jnp.sum(upstream * inputs * scaling, axis=0))


def segment_starts(positions, cont_lengths):
    run_ends = jnp.cumsum(cont_lengths, axis=1)
    begins = PROMPT + run_ends - cont_lengths
    passed = begins[None, :, :] <= positions[:, None, None]
    return jnp.max(jnp.where(passed, begins[None], 0), axis=-1)


def rotary_tables(positions, run_begin):
    relative = jnp.where(
        positions[:, None] < PROMPT, positions[:, None], PROMPT + positions[:, None] - run_begin
    )
    angle_pos = relative.astype(jnp.float32).reshape(1, -1)
    half_dim = HEAD_DIM // 2
    frequency = jnp.exp(
        jnp.arange(half_dim, dtype=jnp.int32).astype(jnp.float32)
        * (-2.0 * math.log(10000.0) / HEAD_DIM)
    )
    angles = angle_pos * frequency[:, None]
    return (jnp.cos(angles), jnp.sin(angles))


def flat_index(cols):
    return lax.axis_index("head") * cols + lax.axis_index("blk")


def coords(flat, cols):
    return (lax.div(flat, cols), lax.rem(flat, cols))


def greet(flat, cols):
    pl.semaphore_signal(
        pltpu.get_barrier_semaphore(),
        inc=1,
        device_id=coords(flat, cols),
        device_id_type=MESH_ID,
    )


def remote(source, target, send_sem, recv_sem, flat, cols):
    return pltpu.make_async_remote_copy(
        src_ref=source,
        dst_ref=target,
        send_sem=send_sem,
        recv_sem=recv_sem,
        device_id=coords(flat, cols),
        device_id_type=MESH_ID,
    )


def loop(first, last, body):
    def step(index, carry):
        body(index)
        return carry

    lax.fori_loop(first, last, step, 0)


def greet_partners(cols, size, partners):
    me = flat_index(cols)
    mine, group = lax.rem(me, size), lax.div(me, size)
    loop(1, partners, lambda s: greet(lax.rem(group + s, partners) * size + mine, cols))
    for t in range(1, size):
        greet(group * size + lax.rem(mine + t, size), cols)
    pl.semaphore_wait(pltpu.get_barrier_semaphore(), partners + size - 2)
    return mine, group


class Work:
    def __init__(self, arrays, out_shape, body, reuse=None):
        self.arrays, self.out_shape, self.body = list(arrays), list(out_shape), body
        self.reuse = reuse or {}

    def own_buffers(self):
        return [i for i in range(len(self.out_shape)) if i not in self.reuse]

    def scratch(self):
        held = self.arrays + [self.out_shape[i] for i in self.own_buffers()]
        total = len(self.arrays) + len(self.out_shape)
        return [pltpu.VMEM(a.shape, a.dtype) for a in held] + [pltpu.SemaphoreType.DMA((total,))]

    def bind(self, refs):
        count, total = len(self.arrays), len(self.arrays) + len(self.out_shape)
        inputs, outputs = refs[:count], refs[count:total]
        held_in, rest, sems = refs[total : total + count], refs[total + count : -1], refs[-1]
        held_out = [None] * len(outputs)
        for buffer, i in zip(rest, self.own_buffers()):
            held_out[i] = buffer
        for i, source in self.reuse.items():
            held_out[i] = held_in[source]
        loads = [
            pltpu.make_async_copy(inputs[i], held_in[i], sems.at[i]) for i in range(count)
        ]
        stores = [
            pltpu.make_async_copy(held_out[i], outputs[i], sems.at[count + i])
            for i in range(len(outputs))
        ]

        def begin():
            for copy in loads:
                copy.start()

        def run():
            for copy in loads:
                copy.wait()
            self.body(held_in, held_out, [copy.start for copy in stores])

        def end():
            for copy in stores:
                copy.wait()

        return begin, run, end


def split_refs(refs, count, work):
    extra_in = len(work.arrays) if work else 0
    extra_out = len(work.out_shape) if work else 0
    inputs, refs = refs[:count], refs[count:]
    work_in, refs = refs[:extra_in], refs[extra_in:]
    outputs, refs = refs[:count], refs[count:]
    work_out, refs = refs[:extra_out], refs[extra_out:]
    if not work:
        return inputs, outputs, refs, (lambda: None,) * 3
    held = extra_in + len(work.own_buffers()) + 1
    return inputs, outputs, refs[:-held], work.bind(work_in + work_out + refs[-held:])


def spread_kernel(cols, size, partners, work, count, *refs):
    inputs, outputs, sems, (begin, run, end) = split_refs(refs, count, work)
    begin()
    mine, group = greet_partners(cols, size, partners)

    def far(i, s):
        send, recv = sems[5 * i], sems[5 * i + 1]
        other = lax.rem(group + s, partners)
        return remote(
            inputs[i].at[other], outputs[i].at[mine, group], send.at[s], recv.at[s], other * size + mine, cols
        )

    def near(i, s, t):
        send, recv = sems[5 * i + 2], sems[5 * i + 3]
        block = outputs[i].at[mine, lax.rem(group - s + partners, partners)]
        target = group * size + lax.rem(mine + t, size)
        return remote(block, block, send.at[s, t], recv.at[s, t], target, cols)

    def own(i):
        return pltpu.make_async_copy(inputs[i].at[group], outputs[i].at[mine, group], sems[5 * i + 4])

    def each(action):
        for i in range(count):
            action(i)

    def near_all(s, action):
        for i in range(count):
            for t in range(1, size):
                action(near(i, s, t))

    each(lambda i: own(i).start())
    loop(1, partners, lambda s: each(lambda i: far(i, s).start()))
    each(lambda i: own(i).wait())
    near_all(0, lambda copy: copy.start())
    run()

    def relay(s):
        each(lambda i: far(i, s).wait_recv())
        near_all(s, lambda copy: copy.start())

    loop(1, partners, relay)
    loop(1, partners, lambda s: each(lambda i: far(i, s).wait_send()))
    loop(0, partners, lambda s: near_all(s, lambda copy: copy.wait()))
    end()


def spread(arrays, cols, size, partners, collective_id, work=None):
    count = len(arrays)
    out_shape, scratch = [], []
    for array in arrays:
        block = array.shape[1:]
        out_shape.append(jax.ShapeDtypeStruct((size, partners) + block, array.dtype))
        scratch += [
            pltpu.SemaphoreType.DMA((partners,)),
            pltpu.SemaphoreType.DMA((partners,)),
            pltpu.SemaphoreType.DMA((partners, size)),
            pltpu.SemaphoreType.DMA((partners, size)),
            pltpu.SemaphoreType.DMA,
        ]
    extra = []
    if work:
        extra, out_shape, scratch = work.arrays, out_shape + work.out_shape, scratch + work.scratch()
    return pl.pallas_call(
        functools.partial(spread_kernel, cols, size, partners, work, count),
        out_shape=out_shape,
        in_specs=[pl.BlockSpec(memory_space=pl.ANY)] * (count + len(extra)),
        out_specs=[pl.BlockSpec(memory_space=pl.ANY)] * len(out_shape),
        scratch_shapes=scratch,
        compiler_params=pltpu.CompilerParams(
            collective_id=collective_id, has_side_effects=True, vmem_limit_bytes=52 * 2**20
        ),
    )(*arrays, *extra)


def collect_kernel(cols, size, partners, work, count, *refs):
    inputs, outputs, scratch, (begin, run, end) = split_refs(refs, count, work)
    begin()
    mine, group = greet_partners(cols, size, partners)

    def near(i, s, t):
        inbox, send, recv = scratch[7 * i + 1], scratch[7 * i + 2], scratch[7 * i + 3]
        other = lax.rem(group + s, partners)
        member = lax.rem(mine + t, size)
        return remote(
            inputs[i].at[member, other],
            inbox.at[t - 1, other],
            send.at[s, t],
            recv.at[s, t],
            group * size + member,
            cols,
        )

    def far(i, s):
        stage, send, recv = scratch[7 * i], scratch[7 * i + 4], scratch[7 * i + 5]
        other = lax.rem(group + s, partners)
        return remote(
            stage.at[other], outputs[i].at[group], send.at[s], recv.at[s], other * size + mine, cols
        )

    def own(i):
        return pltpu.make_async_copy(
            scratch[7 * i].at[group], outputs[i].at[group], scratch[7 * i + 6]
        )

    def each(action):
        for i in range(count):
            action(i)

    def near_all(s, action):
        for i in range(count):
            for t in range(1, size):
                action(near(i, s, t))

    def add(s):
        other = lax.rem(group + s, partners)
        for i in range(count):
            stage, inbox = scratch[7 * i], scratch[7 * i + 1]
            total = inputs[i][mine, other].astype(jnp.float32)
            for t in range(1, size):
                total = total + inbox[t - 1, other].astype(jnp.float32)
            stage[other] = total.astype(stage.dtype)

    loop(1, partners, lambda s: near_all(s, lambda copy: copy.start()))
    near_all(0, lambda copy: copy.start())

    def relay(s):
        near_all(s, lambda copy: copy.wait_recv())
        add(s)
        each(lambda i: far(i, s).start())

    loop(1, partners, relay)
    near_all(0, lambda copy: copy.wait_recv())
    add(0)
    each(lambda i: own(i).start())
    run()
    loop(0, partners, lambda s: near_all(s, lambda copy: copy.wait_send()))
    loop(1, partners, lambda s: each(lambda i: far(i, s).wait()))
    each(lambda i: own(i).wait())
    end()


def collect(arrays, cols, collective_id, work=None):
    count = len(arrays)
    size, partners = arrays[0].shape[:2]
    out_shape, scratch = [], []
    for array in arrays:
        block = array.shape[2:]
        out_shape.append(jax.ShapeDtypeStruct((partners,) + block, array.dtype))
        scratch += [
            pltpu.VMEM((partners,) + block, array.dtype),
            pltpu.VMEM((size - 1, partners) + block, array.dtype),
            pltpu.SemaphoreType.DMA((partners, size)),
            pltpu.SemaphoreType.DMA((partners, size)),
            pltpu.SemaphoreType.DMA((partners,)),
            pltpu.SemaphoreType.DMA((partners,)),
            pltpu.SemaphoreType.DMA,
        ]
    extra = []
    if work:
        extra, out_shape, scratch = work.arrays, out_shape + work.out_shape, scratch + work.scratch()
    return pl.pallas_call(
        functools.partial(collect_kernel, cols, size, partners, work, count),
        out_shape=out_shape,
        in_specs=[pl.BlockSpec(memory_space=pltpu.VMEM)] * count
        + [pl.BlockSpec(memory_space=pl.ANY)] * len(extra),
        out_specs=[pl.BlockSpec(memory_space=pl.ANY)] * len(out_shape),
        scratch_shapes=scratch,
        compiler_params=pltpu.CompilerParams(
            collective_id=collective_id, has_side_effects=True, vmem_limit_bytes=52 * 2**20
        ),
    )(*arrays, *extra)


def spot():
    column = lax.axis_index("blk")
    return (
        lax.axis_index("head"),
        lax.div(column, 4),
        lax.rem(lax.div(column, 2), 2),
        lax.rem(column, 2),
    )


def at_spot(head, depth, x, core):
    return (head, depth * 4 + x * 2 + core)


def push(source, target, send_sem, recv_sem, device):
    return pltpu.make_async_remote_copy(
        src_ref=source,
        dst_ref=target,
        send_sem=send_sem,
        recv_sem=recv_sem,
        device_id=device,
        device_id_type=MESH_ID,
    )


def greet_mesh(depths):
    head, depth, x, core = spot()
    barrier = pltpu.get_barrier_semaphore()

    def signal(device):
        pl.semaphore_signal(barrier, inc=1, device_id=device, device_id_type=MESH_ID)

    loop(1, depths, lambda s: signal(at_spot(head, lax.rem(depth + s, depths), x, core)))
    signal(at_spot(head, depth, 1 - x, core))
    signal(at_spot(1 - head, depth, x, core))
    signal(at_spot(head, depth, x, 1 - core))
    pl.semaphore_wait(barrier, depths + 2)


GATHER_SEMS = 13


def gather_sems(depths):
    row, square = pltpu.SemaphoreType.DMA((depths,)), pltpu.SemaphoreType.DMA((4, depths))
    return [row] * 10 + [square] * 2 + [pltpu.SemaphoreType.DMA]


class Gather:
    def __init__(self, source, result, sems, depths, cut):
        self.source, self.result, self.sems = source, result, sems
        self.depths, self.cut = depths, cut
        self.width = source.shape[-1]

    def along(self, s):
        head, depth, x, core = spot()
        device = at_spot(head, lax.rem(depth + s, self.depths), x, core)
        target = self.result.at[head, depth, x, core]
        return push(self.source, target, self.sems[0].at[s], self.sems[1].at[s], device)

    def block(self, s, far_head, far_x):
        head, depth, x, core = spot()
        return self.result.at[
            1 - head if far_head else head,
            lax.rem(depth - s + self.depths, self.depths),
            1 - x if far_x else x,
            core,
        ]

    def hop(self, kind, s):
        head, depth, x, core = spot()
        if kind in (0, 3):
            device = at_spot(head, depth, 1 - x, core)
        else:
            device = at_spot(1 - head, depth, x, core)
        view = self.block(s, kind == 3, kind == 2)
        if kind == 2:
            view = view.at[:, pl.ds(0, self.cut)]
        if kind == 3:
            view = view.at[:, pl.ds(self.cut, self.width - self.cut)]
        sems = self.sems
        return push(view, view, sems[2 + 2 * kind].at[s], sems[3 + 2 * kind].at[s], device)

    def kinds(self):
        return (2, 3) if self.cut < self.width else (2,)

    def share(self, part, s):
        head, depth, x, core = spot()
        view = self.block(s, part // 2 == 1, part % 2 == 1)
        device = at_spot(head, depth, x, 1 - core)
        return push(view, view, self.sems[10].at[part, s], self.sems[11].at[part, s], device)

    def own(self):
        return pltpu.make_async_copy(self.source, self.result.at[spot()], self.sems[12])

    def start(self):
        self.own().start()
        loop(1, self.depths, lambda s: self.along(s).start())

    def begin_near(self, s):
        self.hop(0, s).start()
        self.hop(1, s).start()
        self.share(0, s).start()

    def start_own(self):
        self.own().wait()
        self.begin_near(0)

    def spread_near(self):
        def step(s):
            self.along(s).wait_recv()
            self.begin_near(s)

        loop(1, self.depths, step)

    def spread_far(self):
        def step(s):
            self.hop(0, s).wait_recv()
            self.hop(2, s).start()
            self.share(1, s).start()
            self.hop(1, s).wait_recv()
            if self.cut < self.width:
                self.hop(3, s).start()
            self.share(2, s).start()

        loop(0, self.depths, step)

    def settle(self):
        def step(s):
            for kind in self.kinds():
                self.hop(kind, s).wait_recv()
            self.share(3, s).start()

        loop(0, self.depths, step)

    def finish(self):
        loop(1, self.depths, lambda s: self.along(s).wait_send())

        def step(s):
            for kind in (0, 1) + self.kinds():
                self.hop(kind, s).wait_send()
            for part in range(4):
                self.share(part, s).wait()

        loop(0, self.depths, step)


def cut_of(width):
    return width // 256 * 128 if width >= 256 else width


def gathered_shape(shard, depths):
    return jax.ShapeDtypeStruct((2, depths, 2, 2) + shard.shape, shard.dtype)


def gather_kernel(depths, count, *refs):
    gathers = gathers_of(refs[:count], refs[count : 2 * count], refs[2 * count :], depths)
    greet_mesh(depths)
    for step in ("start", "start_own", "spread_near", "spread_far", "settle", "finish"):
        for gather in gathers:
            getattr(gather, step)()


def gather_all(arrays, cols, collective_id):
    depths, count = cols // 4, len(arrays)
    return pl.pallas_call(
        functools.partial(gather_kernel, depths, count),
        out_shape=[gathered_shape(array, depths) for array in arrays],
        in_specs=[pl.BlockSpec(memory_space=pl.ANY)] * count,
        out_specs=[pl.BlockSpec(memory_space=pl.ANY)] * count,
        scratch_shapes=gather_sems(depths) * count,
        compiler_params=pltpu.CompilerParams(collective_id=collective_id, has_side_effects=True),
    )(*arrays)


REDUCE_SCRATCH = 20


class Reduce:
    def __init__(self, parts, total, scratch, depths, cut):
        self.parts, self.total = parts, total
        self.sums, self.core_in, self.a1, self.b1, self.a2, self.b2, self.z_in = scratch[:7]
        self.sems = scratch[7:]
        self.depths, self.cut = depths, cut
        self.width = parts.shape[-1]
        self.two = cut < self.width
        self.first = pl.ds(0, cut)
        self.rest = pl.ds(cut, self.width - cut)

    def goal(self, s):
        return lax.rem(spot()[1] + s, self.depths)

    def to_core(self, s):
        head, depth, x, core = spot()
        goal = self.goal(s)
        return push(
            self.parts.at[:, goal, :, 1 - core],
            self.core_in.at[:, goal],
            self.sems[0].at[s],
            self.sems[1].at[s],
            at_spot(head, depth, x, 1 - core),
        )

    def hop(self, kind, s):
        head, depth, x, core = spot()
        goal = self.goal(s)
        over_x = at_spot(head, depth, 1 - x, core)
        over_head = at_spot(1 - head, depth, x, core)
        if kind == 0:
            view = self.sums.at[1 - head, goal, :, :, self.first]
            target, device = self.a1.at[goal], over_head
        elif kind == 1:
            view = self.sums.at[:, goal, 1 - x, :, self.rest]
            target, device = self.b1.at[goal], over_x
        elif kind == 2:
            view = self.sums.at[head, goal, 1 - x, :, self.first]
            target, device = self.a2.at[goal], over_x
        else:
            view = self.sums.at[1 - head, goal, x, :, self.rest]
            target, device = self.b2.at[goal], over_head
        send, recv = self.sems[2 + 2 * kind], self.sems[3 + 2 * kind]
        return push(view, target, send.at[s], recv.at[s], device)

    def along(self, s):
        head, depth, x, core = spot()
        goal = self.goal(s)
        return push(
            self.sums.at[head, goal, x],
            self.z_in.at[s],
            self.sems[10].at[s],
            self.sems[11].at[s],
            at_spot(head, goal, x, core),
        )

    def own(self, s):
        goal = self.goal(s)
        return pltpu.make_async_copy(
            self.parts.at[:, goal, :, spot()[3]], self.sums.at[:, goal], self.sems[12].at[s]
        )

    def start(self):
        def step(s):
            self.to_core(s).start()
            self.own(s).start()

        self.each(step, 0, self.depths)

    def each(self, step, first, last):
        loop(first, last, lambda i: step(lax.rem(i + 1, self.depths)))

    def add(self, where, columns, arrived):
        place = where + (slice(None), columns)
        self.sums[place] = self.sums[place] + arrived

    def near(self, first, last):
        def step(s):
            goal = self.goal(s)
            self.own(s).wait()
            self.to_core(s).wait_recv()
            whole = pl.ds(0, self.width)
            for k in range(4):
                self.add((k // 2, goal, k % 2), whole, self.core_in[k // 2, goal, k % 2])
            self.hop(0, s).start()
            if self.two:
                self.hop(1, s).start()

        self.each(step, first, last)

    def middle(self, first, last):
        head, _, x, _ = spot()

        def step(s):
            goal = self.goal(s)
            self.hop(0, s).wait_recv()
            for k in range(2):
                self.add((head, goal, k), self.first, self.a1[goal, k])
            self.hop(2, s).start()
            if self.two:
                self.hop(1, s).wait_recv()
                for k in range(2):
                    self.add((k, goal, x), self.rest, self.b1[goal, k])
                self.hop(3, s).start()

        self.each(step, first, last)

    def far(self, first, last):
        head, _, x, _ = spot()

        def step(s):
            goal = self.goal(s)
            self.hop(2, s).wait_recv()
            self.add((head, goal, x), self.first, self.a2[goal])
            if self.two:
                self.hop(3, s).wait_recv()
                self.add((head, goal, x), self.rest, self.b2[goal])
            pl.when(s > 0)(lambda: self.along(s).start())

        self.each(step, first, last)

    def finish(self):
        head, depth, x, _ = spot()
        self.total[...] = self.sums[head, depth, x].astype(jnp.float32)

        def step(s):
            self.along(s).wait_recv()
            self.total[...] += self.z_in[s].astype(jnp.float32)

        loop(1, self.depths, step)

        def sent(s):
            self.to_core(s).wait_send()
            for kind in (0, 1, 2, 3) if self.two else (0, 2):
                self.hop(kind, s).wait_send()

        loop(0, self.depths, sent)
        loop(1, self.depths, lambda s: self.along(s).wait_send())


def reduce_scratch(shape, dtype, depths, cut):
    rows, width = shape[-2:]
    rest = max(width - cut, 128)
    row = pltpu.SemaphoreType.DMA((depths,))
    return [
        pltpu.VMEM((2, depths, 2, rows, width), dtype),
        pltpu.VMEM((2, depths, 2, rows, width), dtype),
        pltpu.VMEM((depths, 2, rows, cut), dtype),
        pltpu.VMEM((depths, 2, rows, rest), dtype),
        pltpu.VMEM((depths, rows, cut), dtype),
        pltpu.VMEM((depths, rows, rest), dtype),
        pltpu.VMEM((depths, rows, width), dtype),
    ] + [row] * 13


def reduces_of(parts, totals, scratch, depths):
    return [
        Reduce(
            part,
            totals[i],
            scratch[REDUCE_SCRATCH * i : REDUCE_SCRATCH * (i + 1)],
            depths,
            cut_of(part.shape[-1]),
        )
        for i, part in enumerate(parts)
    ]


def reduce_kernel(depths, count, *refs):
    reduces = reduces_of(refs[:count], refs[count : 2 * count], refs[2 * count :], depths)
    greet_mesh(depths)
    for reduce in reduces:
        reduce.start()
    for step in ("near", "middle", "far"):
        for reduce in reduces:
            getattr(reduce, step)(0, depths)
    for reduce in reduces:
        reduce.finish()


def all_reduce_scratch(arrays, depths):
    scratch = []
    for array in arrays:
        scratch += reduce_scratch(array.shape, array.dtype, depths, cut_of(array.shape[-1]))
    return scratch


def reduce_all(arrays, cols, collective_id):
    depths, count = cols // 4, len(arrays)
    return pl.pallas_call(
        functools.partial(reduce_kernel, depths, count),
        out_shape=[jax.ShapeDtypeStruct(array.shape[-2:], jnp.float32) for array in arrays],
        in_specs=[pl.BlockSpec(memory_space=pl.ANY)] * count,
        out_specs=[pl.BlockSpec(memory_space=pltpu.VMEM)] * count,
        scratch_shapes=all_reduce_scratch(arrays, depths),
        compiler_params=pltpu.CompilerParams(
            collective_id=collective_id, has_side_effects=True, vmem_limit_bytes=52 * 2**20
        ),
    )(*arrays)


def unit_place(pair):
    return lax.rem(pair, 4) != 3, lax.div(pair, 4) * 3 + lax.rem(pair, 4)


def greet_units(cols, pairs, sibling, to_units):
    me = flat_index(cols)
    core, pair = lax.rem(me, 2), lax.div(me, 2)
    holds, unit = unit_place(pair)
    barrier = pltpu.get_barrier_semaphore()
    units = pairs // 4 * 3
    extra = 1 if sibling else 0
    if sibling:
        pl.when(holds)(lambda: greet(me + 1 - 2 * core, cols))
    if to_units:

        @pl.when(holds)
        def _():
            loop(1, pairs, lambda s: greet(lax.rem(pair + s, pairs) * 2 + core, cols))
            pl.semaphore_wait(barrier, units - 1 + extra)

        pl.when(jnp.logical_not(holds))(lambda: pl.semaphore_wait(barrier, units))
    else:

        def to_unit(s):
            other = lax.rem(pair + s, pairs)
            pl.when(unit_place(other)[0])(lambda: greet(other * 2 + core, cols))

        loop(1, pairs, to_unit)
        pl.when(holds)(lambda: pl.semaphore_wait(barrier, pairs - 1 + extra))
    return me, core, pair, holds, unit


def to_units_kernel(cols, pairs, with_kv, *refs):
    if with_kv:
        source, q_out, kv_out, send, recv, own_sem, kv_send, kv_recv, fwd_send, fwd_recv = refs
    else:
        source, q_out, send, recv, own_sem = refs
    me, core, pair, holds, _ = greet_units(cols, pairs, with_kv, True)
    q_rows = pl.ds(0, HEAD_DIM)
    kv_rows = pl.ds(HEAD_DIM, 2 * HEAD_DIM)

    def far(s):
        other = lax.rem(pair + s, pairs)
        unit = unit_place(other)[1]
        target = other * 2 + core
        copies = [
            remote(
                source.at[unit, q_rows] if with_kv else source.at[unit],
                q_out.at[pair],
                send.at[s],
                recv.at[s],
                target,
                cols,
            )
        ]
        if with_kv:
            copies.append(
                remote(
                    source.at[unit, kv_rows],
                    kv_out.at[me],
                    kv_send.at[s],
                    kv_recv.at[s],
                    target,
                    cols,
                )
            )
        return copies

    def own():
        unit = unit_place(pair)[1]
        copies = [
            pltpu.make_async_copy(
                source.at[unit, q_rows] if with_kv else source.at[unit],
                q_out.at[pair],
                own_sem.at[0],
            )
        ]
        if with_kv:
            copies.append(
                pltpu.make_async_copy(source.at[unit, kv_rows], kv_out.at[me], own_sem.at[1])
            )
        return copies

    def forward(s):
        block = kv_out.at[lax.rem(pair - s + pairs, pairs) * 2 + core]
        return remote(block, block, fwd_send.at[s], fwd_recv.at[s], me + 1 - 2 * core, cols)

    def sends(s, action):
        def run():
            for copy in far(s):
                action(copy)

        pl.when(unit_place(lax.rem(pair + s, pairs))[0])(run)

    loop(1, pairs, lambda s: sends(s, lambda copy: copy.start()))

    @pl.when(holds)
    def _():
        for copy in own():
            copy.start()
        for copy in own():
            copy.wait()
        if with_kv:
            forward(0).start()

        def take(s):
            for copy in far(s):
                copy.wait_recv()
            if with_kv:
                forward(s).start()

        loop(1, pairs, take)
        if with_kv:
            loop(0, pairs, lambda s: forward(s).wait())

    loop(1, pairs, lambda s: sends(s, lambda copy: copy.wait_send()))


def to_units(blocks, cols, with_kv, collective_id):
    units, rows, width = blocks.shape
    pairs = units // 3 * 4
    out_shape = [jax.ShapeDtypeStruct((pairs, HEAD_DIM, width), blocks.dtype)]
    scratch = [
        pltpu.SemaphoreType.DMA((pairs,)),
        pltpu.SemaphoreType.DMA((pairs,)),
        pltpu.SemaphoreType.DMA((2,)),
    ]
    if with_kv:
        out_shape.append(jax.ShapeDtypeStruct((2 * pairs, 2 * HEAD_DIM, width), blocks.dtype))
        scratch += [pltpu.SemaphoreType.DMA((pairs,))] * 4
    return pl.pallas_call(
        functools.partial(to_units_kernel, cols, pairs, with_kv),
        out_shape=out_shape,
        in_specs=[pl.BlockSpec(memory_space=pl.ANY)],
        out_specs=[pl.BlockSpec(memory_space=pl.ANY)] * len(out_shape),
        scratch_shapes=scratch,
        compiler_params=pltpu.CompilerParams(collective_id=collective_id, has_side_effects=True),
    )(blocks)


def project_kernel(
    cols, x_ref, gain_ref, w_ref, cos_ref, sin_ref, normed_ref, scale_ref, q_out, kv_out,
    stage, q_send, q_recv, kv_send, kv_recv, fwd_send, fwd_recv, own_sem,
):
    me = flat_index(cols)
    core, pair = lax.rem(me, 2), lax.div(me, 2)
    holds, unit = unit_place(pair)
    sibling = me + 1 - 2 * core
    pairs, heads = q_out.shape[0], stage.shape[0]
    barrier = pltpu.get_barrier_semaphore()
    width = heads * HEAD_DIM

    @pl.when(holds)
    def _():
        loop(1, pairs, lambda s: greet(lax.rem(pair + s, pairs) * 2 + core, cols))
        greet(sibling, cols)

    rows = x_ref[...]
    scale = lax.rsqrt(jnp.mean(rows * rows, axis=-1, keepdims=True) + EPSILON)
    normed = (rows * scale * gain_ref[...]).astype(jnp.bfloat16)
    scale_ref[...] = scale
    normed_ref[...] = normed
    cosine, sine = cos_ref[...], sin_ref[...]
    half = HEAD_DIM // 2
    q_rows, kv_rows = pl.ds(0, HEAD_DIM), pl.ds(HEAD_DIM, 2 * HEAD_DIM)

    def q_far(u, holder):
        return remote(
            stage.at[u, q_rows], q_out.at[pair], q_send.at[u], q_recv.at[pair], holder * 2 + core,
            cols,
        )

    def kv_far(u, holder):
        return remote(
            stage.at[u, kv_rows], kv_out.at[me], kv_send.at[u], kv_recv.at[pair],
            holder * 2 + core, cols,
        )

    q_own = pltpu.make_async_copy(stage.at[unit, q_rows], q_out.at[pair], own_sem.at[0])
    kv_own = pltpu.make_async_copy(stage.at[unit, kv_rows], kv_out.at[me], own_sem.at[1])

    def forward(source):
        block = kv_out.at[source * 2 + core]
        return remote(block, block, fwd_send.at[source], fwd_recv.at[source], sibling, cols)

    per = TILE // HEAD_DIM
    for group in range(heads // per):
        for part in range(3):
            at = pl.ds(part * width + group * TILE, TILE)
            turned = dot(normed, w_ref[:, at], (1, 0)).T
            for k in range(per):
                head = group * per + k
                low = part * HEAD_DIM
                block = turned[k * HEAD_DIM : (k + 1) * HEAD_DIM]
                if part < 2:
                    first, second = block[:half], block[half:]
                    block = jnp.concatenate(
                        [first * cosine - second * sine, second * cosine + first * sine], axis=0
                    )
                stage[head, low : low + HEAD_DIM, :] = block.astype(jnp.bfloat16)
        if group == 0:
            pl.when(holds)(lambda: pl.semaphore_wait(barrier, heads))
            pl.when(jnp.logical_not(holds))(lambda: pl.semaphore_wait(barrier, heads))
        for k in range(per):
            u = group * per + k
            holder = u // 3 * 4 + u % 3

            @pl.when(pair != holder)
            def _(u=u, holder=holder):
                kv_far(u, holder).start()
                q_far(u, holder).start()

            @pl.when(pair == holder)
            def _():
                kv_own.start()
                q_own.start()

    @pl.when(holds)
    def _():
        kv_own.wait()
        forward(pair).start()

        def take(s):
            source = lax.rem(pair - s + pairs, pairs)
            arrival = remote(
                stage.at[unit, kv_rows], kv_out.at[source * 2 + core], kv_send.at[unit],
                kv_recv.at[source], source * 2 + core, cols,
            )
            arrival.wait_recv()
            forward(source).start()

        loop(1, pairs, take)

        def take_q(s):
            source = lax.rem(pair - s + pairs, pairs)
            remote(
                stage.at[unit, q_rows], q_out.at[source], q_send.at[unit], q_recv.at[source],
                source * 2 + core, cols,
            ).wait_recv()

        loop(1, pairs, take_q)
        loop(0, pairs, lambda source: forward(source).wait())
        q_own.wait()

    def sent(u, holder):
        kv_far(u, holder).wait_send()
        q_far(u, holder).wait_send()

    other_units(pairs, pair, sent)


def project(rows, gain, weights, cosine, sine, cols, collective_id):
    tokens, width = rows.shape
    heads = width // HEAD_DIM
    pairs = heads // 3 * 4
    by_pair, by_unit = pltpu.SemaphoreType.DMA((pairs,)), pltpu.SemaphoreType.DMA((heads,))
    vmem = pl.BlockSpec(memory_space=pltpu.VMEM)
    everywhere = pl.BlockSpec(memory_space=pl.ANY)
    return pl.pallas_call(
        functools.partial(project_kernel, cols),
        out_shape=[
            jax.ShapeDtypeStruct((tokens, width), jnp.bfloat16),
            jax.ShapeDtypeStruct((tokens, 1), jnp.float32),
            jax.ShapeDtypeStruct((pairs, HEAD_DIM, tokens), jnp.bfloat16),
            jax.ShapeDtypeStruct((2 * pairs, 2 * HEAD_DIM, tokens), jnp.bfloat16),
        ],
        in_specs=[vmem] * 5,
        out_specs=[vmem, vmem, everywhere, everywhere],
        scratch_shapes=[
            pltpu.VMEM((heads, 3 * HEAD_DIM, tokens), jnp.bfloat16),
            by_unit,
            by_pair,
            by_unit,
            by_pair,
            by_pair,
            by_pair,
            pltpu.SemaphoreType.DMA((2,)),
        ],
        compiler_params=pltpu.CompilerParams(
            collective_id=collective_id, has_side_effects=True, vmem_limit_bytes=40 * 2**20
        ),
    )(rows, gain.reshape(1, width), weights, cosine, sine)


def to_tokens_kernel(cols, pairs, with_kv, *refs):
    if with_kv:
        q_in, kv_in, q_out, kv_out, send, recv, own_sem = refs[:7]
        stage, inbox, kv_send, kv_recv, near_send, near_recv = refs[7:]
    else:
        q_in, q_out, send, recv, own_sem = refs
    me, core, pair, holds, unit = greet_units(cols, pairs, with_kv, False)

    def far(s):
        other = lax.rem(pair + s, pairs)
        target = other * 2 + core
        copies = [remote(q_in.at[other], q_out.at[unit], send.at[s], recv.at[s], target, cols)]
        if with_kv:
            copies.append(
                remote(
                    stage.at[other], kv_out.at[unit], kv_send.at[s], kv_recv.at[s], target, cols
                )
            )
        return copies

    def own():
        copies = [pltpu.make_async_copy(q_in.at[pair], q_out.at[unit], own_sem.at[0])]
        if with_kv:
            copies.append(pltpu.make_async_copy(stage.at[pair], kv_out.at[unit], own_sem.at[1]))
        return copies

    def near(s):
        other = lax.rem(pair + s, pairs)
        return remote(
            kv_in.at[other * 2 + 1 - core],
            inbox.at[other],
            near_send.at[s],
            near_recv.at[s],
            me + 1 - 2 * core,
            cols,
        )

    def add(s):
        other = lax.rem(pair + s, pairs)
        total = kv_in[other * 2 + core].astype(jnp.float32) + inbox[other].astype(jnp.float32)
        stage[other] = total.astype(stage.dtype)

    @pl.when(holds)
    def _():
        if with_kv:
            loop(1, pairs, lambda s: near(s).start())
            near(0).start()

        def give(s):
            if with_kv:
                near(s).wait_recv()
                add(s)
            for copy in far(s):
                copy.start()

        loop(1, pairs, give)
        if with_kv:
            near(0).wait_recv()
            add(0)
        for copy in own():
            copy.start()
        for copy in own():
            copy.wait()

    def take(s):
        def run():
            for copy in far(s):
                copy.wait_recv()

        pl.when(unit_place(lax.rem(pair - s + pairs, pairs))[0])(run)

    loop(1, pairs, take)

    @pl.when(holds)
    def _():
        def sent(s):
            for copy in far(s):
                copy.wait_send()

        loop(1, pairs, sent)
        if with_kv:
            loop(0, pairs, lambda s: near(s).wait_send())


def to_tokens(arrays, cols, collective_id):
    with_kv = len(arrays) == 2
    pairs, _, width = arrays[0].shape
    units = pairs // 4 * 3
    out_shape = [jax.ShapeDtypeStruct((units, HEAD_DIM, width), arrays[0].dtype)]
    in_specs = [pl.BlockSpec(memory_space=pl.ANY)]
    scratch = [
        pltpu.SemaphoreType.DMA((pairs,)),
        pltpu.SemaphoreType.DMA((pairs,)),
        pltpu.SemaphoreType.DMA((2,)),
    ]
    if with_kv:
        out_shape.append(jax.ShapeDtypeStruct((units, 2 * HEAD_DIM, width), arrays[1].dtype))
        in_specs.append(pl.BlockSpec(memory_space=pltpu.VMEM))
        scratch += [pltpu.VMEM((pairs, 2 * HEAD_DIM, width), arrays[1].dtype)] * 2
        scratch += [pltpu.SemaphoreType.DMA((pairs,))] * 4
    return pl.pallas_call(
        functools.partial(to_tokens_kernel, cols, pairs, with_kv),
        out_shape=out_shape,
        in_specs=in_specs,
        out_specs=[pl.BlockSpec(memory_space=pl.ANY)] * len(out_shape),
        scratch_shapes=scratch,
        compiler_params=pltpu.CompilerParams(
            collective_id=collective_id, has_side_effects=True, vmem_limit_bytes=48 * 2**20
        ),
    )(*arrays)


def wide_of(first, blocks):
    return pl.ds(pl.multiple_of(first * TILE, TILE), blocks * TILE)


def in_reach(first, shape, place, run):
    key_pos = first * TILE + lax.broadcasted_iota(jnp.int32, shape, 0)
    return (key_pos <= place) & (key_pos >= run)


def tile_reach(tile, core, width, wide, masked, blocks):
    joined = TILE // width
    low = (2 * tile * joined + core) * width
    high = low + (2 * joined - 1) * width - 1
    prompt = low < PROMPT
    full = jnp.where(prompt, low // (TILE * wide), PROMPT // (TILE * wide))
    back = jnp.maximum((low - LONGEST + 1) // TILE, PROMPT // TILE)
    first = jnp.where(prompt, full * wide, back)
    steps = (high // TILE + masked - first) // masked
    first = jnp.minimum(first, blocks - steps * masked)
    lane = lax.broadcasted_iota(jnp.int32, (1, TILE), 1)
    place = low + lane + lane // width * width
    return full, first, steps, place


CHUNK = 64


def fill_rows(kv_ref, first_row, rows):
    def fill(b):
        rows[wide_of(b, 1), :] = kv_ref[b, first_row : first_row + HEAD_DIM, :].T

    loop(0, kv_ref.shape[0], fill)


def forward_tile(tile, core, width, queries, run, kv_ref, key_rows, kept):
    full, start, steps, place = tile_reach(
        tile, core, width, FWD_WIDE, FWD_MASK, kv_ref.shape[0]
    )

    def by_eight(value):
        return value.reshape(-1, 8, TILE)

    def fold(blocks, first, state, masked):
        top, total, gathered = state
        base = pl.multiple_of(first * TILE, TILE)
        highest = top
        for c in range(blocks * TILE // CHUNK):
            scores = jnp.dot(
                key_rows[pl.ds(base + c * CHUNK, CHUNK), :],
                queries,
                preferred_element_type=jnp.float32,
            )
            if masked:
                key_pos = base + c * CHUNK + lax.broadcasted_iota(jnp.int32, scores.shape, 0)
                scores = jnp.where((key_pos <= place) & (key_pos >= run), scores, NEGATIVE)
            kept[c * CHUNK : (c + 1) * CHUNK, :] = scores
            highest = jnp.maximum(highest, jnp.max(by_eight(scores), axis=0))
        new_top = jnp.broadcast_to(jnp.max(highest, axis=0, keepdims=True), (8, TILE))
        shrink = jnp.exp2((top - new_top) * EXP_SCALE)
        total = total * shrink
        gathered = (by_eight(gathered) * shrink[None]).reshape(HEAD_DIM, TILE)
        for j in range(blocks):
            low = []
            for c in range(j * TILE // CHUNK, (j + 1) * TILE // CHUNK):
                scores = by_eight(kept[c * CHUNK : (c + 1) * CHUNK, :])
                weights = jnp.exp2((scores - new_top[None]) * EXP_SCALE)
                total = total + jnp.sum(weights, axis=0)
                low.append(weights.reshape(CHUNK, TILE).astype(jnp.bfloat16))
            gathered = gathered + jnp.dot(
                kv_ref[first + j, HEAD_DIM : 2 * HEAD_DIM, :],
                jnp.concatenate(low, axis=0),
                preferred_element_type=jnp.float32,
            )
        return (new_top, total, gathered)

    state = (
        jnp.full((8, TILE), NEGATIVE, jnp.float32),
        jnp.zeros((8, TILE), jnp.float32),
        jnp.zeros((HEAD_DIM, TILE), jnp.float32),
    )
    state = lax.fori_loop(0, full, lambda b, s: fold(FWD_WIDE, b * FWD_WIDE, s, False), state)
    top, total, gathered = lax.fori_loop(
        0, steps, lambda b, s: fold(FWD_MASK, start + b * FWD_MASK, s, True), state
    )
    total = jnp.sum(total, axis=0, keepdims=True)
    exact = gathered / total
    return exact, exact.astype(jnp.bfloat16), top[0:1] * EXP_SCALE + jnp.log2(total)


def forward_scratch(blocks):
    return [
        pltpu.VMEM((blocks * TILE, HEAD_DIM), jnp.bfloat16),
        pltpu.VMEM((max(FWD_WIDE, FWD_MASK) * TILE, TILE), jnp.float32),
    ]


def my_unit():
    me = flat_index(lax.axis_size("blk"))
    pair = lax.div(me, 2)
    holds, unit = unit_place(pair)
    return me, lax.rem(me, 2), pair, holds, unit


def forward_kernel(width, q_ref, kv_ref, run_ref, o_ref, ob_ref, lse_ref, key_rows, kept):
    tile = pl.program_id(0)
    _, core, _, holds, _ = my_unit()

    @pl.when(holds & (tile == 0))
    def _():
        fill_rows(kv_ref, 0, key_rows)

    @pl.when(holds)
    def _():
        o_ref[0], ob_ref[0], lse_ref[0] = forward_tile(
            tile, core, width, q_ref[0], run_ref[0], kv_ref, key_rows, kept
        )


def tile_spec(rows):
    return pl.BlockSpec((1, rows, TILE), lambda i: (i, 0, 0))


def attend(queries, keys_values, run, width):
    tiles = queries.shape[0]
    held = pl.BlockSpec(keys_values.shape, lambda i: (0, 0, 0))
    return pl.pallas_call(
        functools.partial(forward_kernel, width),
        grid=(tiles,),
        in_specs=[tile_spec(HEAD_DIM), held, tile_spec(1)],
        out_specs=[tile_spec(HEAD_DIM), tile_spec(HEAD_DIM), tile_spec(1)],
        scratch_shapes=forward_scratch(keys_values.shape[0]),
        out_shape=[
            jax.ShapeDtypeStruct((tiles, HEAD_DIM, TILE), jnp.float32),
            jax.ShapeDtypeStruct((tiles, HEAD_DIM, TILE), jnp.bfloat16),
            jax.ShapeDtypeStruct((tiles, 1, TILE), jnp.float32),
        ],
        compiler_params=pltpu.CompilerParams(vmem_limit_bytes=48 * 2**20),
    )(queries, keys_values, run)


def other_units(pairs, pair, action):
    def one(u):
        holder = lax.div(u, 3) * 4 + lax.rem(u, 3)
        pl.when(holder != pair)(lambda: action(u, holder))

    loop(0, pairs // 4 * 3, one)


def gathers_of(sources, results, sems, depths):
    return [
        Gather(
            source,
            results[i],
            sems[GATHER_SEMS * i : GATHER_SEMS * (i + 1)],
            depths,
            cut_of(source.shape[-1]),
        )
        for i, source in enumerate(sources)
    ]


GATHER_AT = {"start": 0, "start_own": 0, "spread_near": 7, "spread_far": 10, "settle": 13}


def forward_home_kernel(cols, count, *refs):
    q_ref, kv_ref, run_ref = refs[:3]
    sources, refs = refs[3 : 3 + count], refs[3 + count :]
    o_ref, lse_ref, home = refs[:3]
    results, refs = refs[3 : 3 + count], refs[3 + count :]
    key_rows, kept, low, send, recv, own_sem = refs[:6]
    gathers = gathers_of(sources, results, refs[6:], cols // 4)
    tile, tiles = pl.program_id(0), tiles_of(kv_ref)
    me, core, pair, holds, unit = my_unit()

    @pl.when(tile == 0)
    def _():
        loop(1, tiles, lambda s: greet(lax.rem(pair + s, tiles) * 2 + core, cols))
        greet(me + 1 - 2 * core, cols)

    @pl.when(holds & (tile == 0))
    def _():
        fill_rows(kv_ref, 0, key_rows)

    @pl.when(tile == 0)
    def _():
        pl.semaphore_wait(pltpu.get_barrier_semaphore(), tiles)

    for name, place_at in GATHER_AT.items():

        @pl.when(tile == place_at)
        def _(name=name):
            for gather in gathers:
                getattr(gather, name)()

    def away(t):
        return remote(
            low.at[t], home.at[unit], send.at[t], recv.at[unit], t * 2 + core, cols
        )

    stays = pltpu.make_async_copy(low.at[pair], home.at[unit], own_sem)

    @pl.when(holds)
    def _():
        o_ref[0], low[tile], lse_ref[0] = forward_tile(
            tile, core, TILE, q_ref[0], run_ref[0], kv_ref, key_rows, kept
        )
        pl.when(tile != pair)(lambda: away(tile).start())
        pl.when(tile == pair)(lambda: stays.start())

    @pl.when(tile == tiles - 1)
    def _():
        for gather in gathers:
            gather.finish()

        def arrived(u, holder):
            remote(
                low.at[pair], home.at[u], send.at[pair], recv.at[u], holder * 2 + core, cols
            ).wait_recv()

        other_units(tiles, pair, arrived)

        @pl.when(holds)
        def _():
            def sent(t):
                pl.when(t != pair)(lambda: away(t).wait_send())

            loop(0, tiles, sent)
            stays.wait()


def tiles_of(kv_ref):
    return kv_ref.shape[0] // 2


def attend_home(queries, keys_values, run, shards, cols, collective_id):
    tiles, units, depths = queries.shape[0], queries.shape[0] // 4 * 3, cols // 4
    held = pl.BlockSpec(keys_values.shape, lambda i: (0, 0, 0))
    everywhere = pl.BlockSpec(memory_space=pl.ANY)
    return pl.pallas_call(
        functools.partial(forward_home_kernel, cols, len(shards)),
        grid=(tiles,),
        in_specs=[tile_spec(HEAD_DIM), held, tile_spec(1)] + [everywhere] * len(shards),
        out_specs=[tile_spec(HEAD_DIM), tile_spec(1), everywhere] + [everywhere] * len(shards),
        scratch_shapes=forward_scratch(keys_values.shape[0])
        + [
            pltpu.VMEM((tiles, HEAD_DIM, TILE), jnp.bfloat16),
            pltpu.SemaphoreType.DMA((tiles,)),
            pltpu.SemaphoreType.DMA((units,)),
            pltpu.SemaphoreType.DMA,
        ]
        + gather_sems(depths) * len(shards),
        out_shape=[
            jax.ShapeDtypeStruct((tiles, HEAD_DIM, TILE), jnp.float32),
            jax.ShapeDtypeStruct((tiles, 1, TILE), jnp.float32),
            jax.ShapeDtypeStruct((units, HEAD_DIM, TILE), jnp.bfloat16),
        ]
        + [gathered_shape(shard, depths) for shard in shards],
        compiler_params=pltpu.CompilerParams(
            collective_id=collective_id, has_side_effects=True, vmem_limit_bytes=48 * 2**20
        ),
    )(queries, keys_values, run, *shards)


def backward_tile(
    tile, core, width, queries, grads, exact, lse, run,
    kv_ref, key_rows, value_rows, dk_sum, dv_sum,
):
    full, start, steps, place = tile_reach(
        tile, core, width, BWD_WIDE, BWD_MASK, kv_ref.shape[0]
    )
    delta = jnp.sum(grads.astype(jnp.float32) * exact, axis=0, keepdims=True)
    over_queries = (((1,), (1,)), ((), ()))

    def fold(blocks, first, dq, masked):
        rows = wide_of(first, blocks)
        scores = jnp.dot(key_rows[rows, :], queries, preferred_element_type=jnp.float32)
        probs = jnp.exp2(scores * EXP_SCALE - lse)
        if masked:
            probs = jnp.where(in_reach(first, scores.shape, place, run), probs, 0.0)
        dp = jnp.dot(value_rows[rows, :], grads, preferred_element_type=jnp.float32)
        ds = (probs * (dp - delta)).astype(jnp.bfloat16)
        low = probs.astype(jnp.bfloat16)
        for j in range(blocks):
            part = slice(j * TILE, (j + 1) * TILE)
            dv_sum[first + j] += lax.dot_general(
                grads, low[part], over_queries, preferred_element_type=jnp.float32
            )
            dk_sum[first + j] += lax.dot_general(
                queries, ds[part], over_queries, preferred_element_type=jnp.float32
            )
            dq = dq + jnp.dot(
                kv_ref[first + j, 0:HEAD_DIM, :], ds[part], preferred_element_type=jnp.float32
            )
        return dq

    dq = jnp.zeros((HEAD_DIM, TILE), jnp.float32)
    dq = lax.fori_loop(0, full, lambda b, s: fold(BWD_WIDE, b * BWD_WIDE, s, False), dq)
    dq = lax.fori_loop(0, steps, lambda b, s: fold(BWD_MASK, start + b * BWD_MASK, s, True), dq)
    return (dq * SCORE_SCALE).astype(jnp.bfloat16)


def backward_begin(kv_ref, key_rows, value_rows, dk_sum, dv_sum):
    fill_rows(kv_ref, 0, key_rows)
    fill_rows(kv_ref, HEAD_DIM, value_rows)

    def clear(b):
        dk_sum[b] = jnp.zeros((HEAD_DIM, TILE), jnp.float32)
        dv_sum[b] = jnp.zeros((HEAD_DIM, TILE), jnp.float32)

    loop(0, kv_ref.shape[0], clear)


def backward_end(dk_sum, dv_sum, dkv, first, last):
    def drain(b):
        dkv[b, 0:HEAD_DIM, :] = (dk_sum[b] * SCORE_SCALE).astype(jnp.bfloat16)
        dkv[b, HEAD_DIM : 2 * HEAD_DIM, :] = dv_sum[b].astype(jnp.bfloat16)

    loop(first, last, drain)


def backward_scratch(blocks):
    return [pltpu.VMEM((blocks * TILE, HEAD_DIM), jnp.bfloat16)] * 2 + [
        pltpu.VMEM((blocks, HEAD_DIM, TILE), jnp.float32)
    ] * 2


NEAR_AT, MIDDLE_AT, FAR_AT = (0, 2, 4, 6), (2, 4, 6, 8), (3, 5, 7, 9)


def reduce_at(step, reduces, depths):
    quarter = depths // 4
    for name, places in (("far", FAR_AT), ("middle", MIDDLE_AT), ("near", NEAR_AT)):
        for part, place_at in enumerate(places):

            @pl.when(step == place_at)
            def _(name=name, part=part):
                for reduce in reduces:
                    getattr(reduce, name)(part * quarter, (part + 1) * quarter)


def backward_kernel(width, depths, count, *refs):
    q_ref, kv_ref, do_ref, o_ref, lse_ref, run_ref = refs[:6]
    parts, refs = refs[6 : 6 + count], refs[6 + count :]
    dq_ref, dkv_ref = refs[:2]
    totals, refs = refs[2 : 2 + count], refs[2 + count :]
    held = refs[:4]
    reduces = reduces_of(parts, totals, refs[4:], depths)
    tile, tiles = pl.program_id(0), pl.num_programs(0)
    _, core, _, holds, _ = my_unit()

    @pl.when(tile == 0)
    def _():
        greet_mesh(depths)
        for reduce in reduces:
            reduce.start()

    reduce_at(tile, reduces, depths)

    @pl.when(holds & (tile == 0))
    def _():
        backward_begin(kv_ref, *held)

    @pl.when(holds)
    def _():
        dq_ref[0] = backward_tile(
            tile, core, width, q_ref[0], do_ref[0], o_ref[0], lse_ref[0], run_ref[0],
            kv_ref, *held,
        )

    @pl.when(holds & (tile == tiles - 1))
    def _():
        backward_end(held[2], held[3], dkv_ref, 0, dkv_ref.shape[0])

    @pl.when(tile == tiles - 1)
    def _():
        for reduce in reduces:
            reduce.finish()


def attend_back(queries, keys_values, grads, exact, lse, run, width, parts, cols, collective_id):
    tiles, blocks = queries.shape[0], keys_values.shape[0]
    held = pl.BlockSpec(keys_values.shape, lambda i: (0, 0, 0))
    wide, flat = tile_spec(HEAD_DIM), tile_spec(1)
    depths = cols // 4
    return pl.pallas_call(
        functools.partial(backward_kernel, width, depths, len(parts)),
        grid=(tiles,),
        in_specs=[wide, held, wide, wide, flat, flat]
        + [pl.BlockSpec(memory_space=pl.ANY)] * len(parts),
        out_specs=[wide, held]
        + [pl.BlockSpec(part.shape[-2:], lambda i: (0, 0)) for part in parts],
        scratch_shapes=backward_scratch(blocks) + all_reduce_scratch(parts, depths),
        out_shape=[
            jax.ShapeDtypeStruct(queries.shape, jnp.bfloat16),
            jax.ShapeDtypeStruct(keys_values.shape, jnp.bfloat16),
        ]
        + [jax.ShapeDtypeStruct(part.shape[-2:], jnp.float32) for part in parts],
        compiler_params=pltpu.CompilerParams(
            collective_id=collective_id, has_side_effects=True, vmem_limit_bytes=52 * 2**20
        ),
    )(queries, keys_values, grads, exact, lse, run, *parts)


def backward_home_kernel(cols, depths, count, *refs):
    q_ref, kv_ref, o_ref, lse_ref, run_ref, do_source = refs[:6]
    parts, refs = refs[6 : 6 + count], refs[6 + count :]
    q_home, kv_home = refs[:2]
    totals, refs = refs[2 : 2 + count], refs[2 + count :]
    held, refs = refs[:4], refs[4:]
    grads, low, dkv, inbox, refs = refs[0], refs[1], refs[2], refs[3], refs[4:]
    in_send, in_recv, q_send, q_recv, kv_send, kv_recv, near_send, near_recv, own_sem = refs[:9]
    reduces = reduces_of(parts, totals, refs[9:], depths)
    step, pairs = pl.program_id(0), tiles_of(kv_ref)
    tile = pairs - 1 - step
    me, core, pair, holds, unit = my_unit()
    sibling = me + 1 - 2 * core
    last = tile == 0

    def do_out(u, holder):
        return remote(
            do_source.at[u], grads.at[pair], in_send.at[u], in_recv.at[pair], holder * 2 + core, cols
        )

    def do_in(t):
        return remote(
            do_source.at[unit], grads.at[t], in_send.at[unit], in_recv.at[t], t * 2 + core, cols
        )

    def q_away(t):
        return remote(low.at[t], q_home.at[unit], q_send.at[t], q_recv.at[unit], t * 2 + core, cols)

    def kv_away(t):
        return remote(
            inbox.at[t], kv_home.at[unit], kv_send.at[t], kv_recv.at[unit], t * 2 + core, cols
        )

    def near(t):
        return remote(
            dkv.at[t * 2 + 1 - core], inbox.at[t], near_send.at[t], near_recv.at[t], sibling, cols
        )

    do_own = pltpu.make_async_copy(do_source.at[unit], grads.at[pair], own_sem.at[0])
    q_stays = pltpu.make_async_copy(low.at[pair], q_home.at[unit], own_sem.at[1])
    kv_stays = pltpu.make_async_copy(inbox.at[pair], kv_home.at[unit], own_sem.at[2])

    def give(t):
        near(t).wait_recv()
        inbox[t] = dkv[t * 2 + core] + inbox[t]
        pl.when(t != pair)(lambda: kv_away(t).start())
        pl.when(t == pair)(lambda: kv_stays.start())

    @pl.when(step == 0)
    def _():
        loop(1, pairs, lambda s: greet(lax.rem(pair + s, pairs) * 2 + core, cols))
        greet(sibling, cols)
        pl.semaphore_wait(pltpu.get_barrier_semaphore(), pairs)
        other_units(pairs, pair, lambda u, holder: do_out(u, holder).start())
        pl.when(holds)(lambda: do_own.start())
        for reduce in reduces:
            reduce.start()

    @pl.when(holds & (step == 0))
    def _():
        backward_begin(kv_ref, *held)

    reduce_at(step, reduces, depths)

    @pl.when(holds)
    def _():
        pl.when(tile != pair)(lambda: do_in(tile).wait_recv())
        pl.when(tile == pair)(lambda: do_own.wait())
        low[tile] = backward_tile(
            tile, core, TILE, q_ref[0], grads[tile], o_ref[0], lse_ref[0], run_ref[0],
            kv_ref, *held,
        )
        pl.when(tile != pair)(lambda: q_away(tile).start())
        pl.when(tile == pair)(lambda: q_stays.start())
        backward_end(held[2], held[3], dkv, 2 * tile, 2 * tile + 2)
        near(tile).start()
        pl.when(step > 0)(lambda: give(tile + 1))
        pl.when(last)(lambda: give(tile))

    @pl.when(last)
    def _():
        for reduce in reduces:
            reduce.finish()

        def arrived(u, holder):
            target = holder * 2 + core
            remote(
                low.at[pair], q_home.at[u], q_send.at[pair], q_recv.at[u], target, cols
            ).wait_recv()
            remote(
                inbox.at[pair], kv_home.at[u], kv_send.at[pair], kv_recv.at[u], target, cols
            ).wait_recv()

        other_units(pairs, pair, arrived)
        other_units(pairs, pair, lambda u, holder: do_out(u, holder).wait_send())

        @pl.when(holds)
        def _():
            def sent(t):
                near(t).wait_send()

                @pl.when(t != pair)
                def _():
                    q_away(t).wait_send()
                    kv_away(t).wait_send()

            loop(0, pairs, sent)
            q_stays.wait()
            kv_stays.wait()


def attend_back_home(queries, keys_values, do_blocks, exact, lse, run, parts, cols, collective_id):
    tiles, blocks = queries.shape[0], keys_values.shape[0]
    units, depths = do_blocks.shape[0], cols // 4
    held = pl.BlockSpec(keys_values.shape, lambda i: (0, 0, 0))
    wide = pl.BlockSpec((1, HEAD_DIM, TILE), lambda i: (tiles - 1 - i, 0, 0))
    flat = pl.BlockSpec((1, 1, TILE), lambda i: (tiles - 1 - i, 0, 0))
    everywhere = pl.BlockSpec(memory_space=pl.ANY)
    by_tile, by_unit = pltpu.SemaphoreType.DMA((tiles,)), pltpu.SemaphoreType.DMA((units,))
    tile_rows = pltpu.VMEM((tiles, HEAD_DIM, TILE), jnp.bfloat16)
    return pl.pallas_call(
        functools.partial(backward_home_kernel, cols, depths, len(parts)),
        grid=(tiles,),
        in_specs=[wide, held, wide, flat, flat, everywhere] + [everywhere] * len(parts),
        out_specs=[everywhere, everywhere]
        + [pl.BlockSpec(part.shape[-2:], lambda i: (0, 0)) for part in parts],
        scratch_shapes=backward_scratch(blocks)
        + [
            tile_rows,
            tile_rows,
            pltpu.VMEM((blocks, 2 * HEAD_DIM, TILE), jnp.bfloat16),
            pltpu.VMEM((tiles, 2 * HEAD_DIM, TILE), jnp.bfloat16),
            by_unit,
            by_tile,
            by_tile,
            by_unit,
            by_tile,
            by_unit,
            by_tile,
            by_tile,
            pltpu.SemaphoreType.DMA((3,)),
        ]
        + all_reduce_scratch(parts, depths),
        out_shape=[
            jax.ShapeDtypeStruct((units, HEAD_DIM, TILE), jnp.bfloat16),
            jax.ShapeDtypeStruct((units, 2 * HEAD_DIM, TILE), jnp.bfloat16),
        ]
        + [jax.ShapeDtypeStruct(part.shape[-2:], jnp.float32) for part in parts],
        compiler_params=pltpu.CompilerParams(
            collective_id=collective_id, has_side_effects=True, vmem_limit_bytes=52 * 2**20
        ),
    )(queries, keys_values, exact, lse, run, do_blocks, *parts)


def to_tiles(blocks):
    count, rows, width = blocks.shape
    if width == TILE:
        return blocks
    joined = TILE // width
    return (
        blocks.reshape(count // joined, joined, rows, width)
        .transpose(0, 2, 1, 3)
        .reshape(count // joined, rows, TILE)
    )


def from_tiles(tiles, width):
    count, rows, _ = tiles.shape
    if width == TILE:
        return tiles
    joined = TILE // width
    return (
        tiles.reshape(count, rows, joined, width)
        .transpose(0, 2, 1, 3)
        .reshape(count * joined, rows, width)
    )


def dot(left, right, over):
    return lax.dot_general(
        left, right, (((over[0],), (over[1],)), ((), ())), preferred_element_type=jnp.float32
    )


STRIP = 512


def strips(total, body):
    width = min(total, STRIP)
    loop(0, total // width, lambda j: body(pl.ds(pl.multiple_of(j * width, width), width)))


def shared_forward(ins, outs, done):
    normed, wide, down = ins
    gate_in, up_in, hidden_low, total = outs
    hidden = down.shape[0]

    def strip(at):
        after = pl.ds(at.start + hidden, at.size)
        gate = dot(normed[...], wide[:, at], (1, 0))
        up = dot(normed[...], wide[:, after], (1, 0))
        gate_in[:, at] = gate.astype(jnp.bfloat16)
        up_in[:, at] = up.astype(jnp.bfloat16)
        hidden_low[:, at] = (apply_silu(gate) * up).astype(jnp.bfloat16)

    strips(hidden, strip)
    for start in done[:3]:
        start()
    total[...] = dot(hidden_low[...], down[...], (1, 0))
    done[3]()


def shared_backward(ins, outs, done):
    grads, normed, gate_in, up_in, hidden_low, wide, down = ins
    grad_wide, grad_down, back = outs
    hidden = down.shape[0]
    normed_t = normed[...].T
    back[...] = jnp.zeros_like(back)

    def strip(at):
        after = pl.ds(at.start + hidden, at.size)
        upstream = dot(grads[...], down[at, :], (1, 1))
        gate, up = gate_in[:, at].astype(jnp.float32), up_in[:, at].astype(jnp.float32)
        low_gate = (upstream * up * silu_slope(gate)).astype(jnp.bfloat16)
        low_up = (upstream * apply_silu(gate)).astype(jnp.bfloat16)
        back[...] += dot(low_gate, wide[:, at], (1, 1)) + dot(low_up, wide[:, after], (1, 1))
        grad_wide[:, at] = dot(normed_t, low_gate, (1, 0)).astype(jnp.bfloat16)
        grad_wide[:, after] = dot(normed_t, low_up, (1, 0)).astype(jnp.bfloat16)
        grad_down[at, :] = dot(hidden_low[:, at].T, grads[...], (1, 0)).astype(jnp.bfloat16)

    strips(hidden, strip)
    for start in done:
        start()


QUARTERS = 4


def quarter_order(pair, per):
    own = lax.div(pair, per)
    outer, inner = lax.div(own, 2), lax.rem(own, 2)
    return [own, (1 - outer) * 2 + inner, outer * 2 + 1 - inner, (1 - outer) * 2 + 1 - inner]


def expert_kernel(cols, step, final, work_first, work, shapes, *refs):
    held_in, held_out, extra = shapes
    sending, refs = refs[0], refs[1:]
    inputs, refs = refs[:held_in], refs[held_in:]
    extra_in = len(work.arrays)
    work_in, refs = refs[:extra_in], refs[extra_in:]
    returned, refs = refs[0], refs[1:]
    outputs, refs = refs[:held_out], refs[held_out:]
    work_out, refs = refs[: len(work.out_shape)], refs[len(work.out_shape) :]
    land, partial, inbox, refs = refs[0], refs[1], refs[2], refs[3:]
    send, recv, share_send, share_recv, near_send, near_recv, refs = refs[:6] + (refs[6:],)
    back_send, back_recv, own_sem, load_sem, refs = refs[:4] + (refs[4:],)
    held, refs = refs[:held_in], refs[held_in:]
    scratch, refs = refs[:extra], refs[extra:]
    begin, run, end = work.bind(work_in + work_out + refs)

    me = flat_index(cols)
    core, pair = lax.rem(me, 2), lax.div(me, 2)
    pairs = sending.shape[0]
    per = pairs // QUARTERS
    sibling = me + 1 - 2 * core
    order = quarter_order(pair, per)

    loads = [pltpu.make_async_copy(inputs[i], held[i], load_sem.at[i]) for i in range(held_in)]
    for copy in loads:
        copy.start()
    begin()

    loop(1, pairs, lambda s: greet(lax.rem(pair + s, pairs) * 2 + core, cols))
    greet(sibling, cols)
    pl.semaphore_wait(pltpu.get_barrier_semaphore(), pairs)

    def out(e):
        return remote(
            sending.at[e], land.at[pair, core], send.at[e], recv.at[pair], e * 2 + core, cols
        )

    def arrival(e):
        return remote(
            sending.at[e], land.at[e, core], send.at[e], recv.at[e], e * 2 + core, cols
        )

    def share(e):
        block = land.at[e, core]
        return remote(block, block, share_send.at[e], share_recv.at[e], sibling, cols)

    def near(quarter):
        rows = pl.ds(quarter * per, per)
        return remote(
            partial.at[rows, 1 - core],
            inbox.at[rows],
            near_send.at[quarter],
            near_recv.at[quarter],
            sibling,
            cols,
        )

    def back(e):
        return remote(
            inbox.at[e], returned.at[pair], back_send.at[e], back_recv.at[pair], e * 2 + core, cols
        )

    def back_arrival(e):
        return remote(
            inbox.at[e], returned.at[e], back_send.at[e], back_recv.at[e], e * 2 + core, cols
        )

    def others(quarter, action):
        def one(k):
            e = quarter * per + k
            pl.when(e != pair)(lambda: action(e))

        loop(0, per, one)

    own_in = pltpu.make_async_copy(sending.at[pair], land.at[pair, core], own_sem.at[0])
    own_back = pltpu.make_async_copy(inbox.at[pair], returned.at[pair], own_sem.at[1])

    for quarter in (order[2], order[0], order[1], order[3]):
        others(quarter, lambda e: out(e).start())
    own_in.start()
    own_in.wait()
    share(pair).start()
    if work_first:
        run()
    for copy in loads:
        copy.wait()

    def take(quarter):
        def one(e):
            arrival(e).wait_recv()
            share(e).start()

        others(quarter, one)
        loop(0, per, lambda k: share(quarter * per + k).wait_recv())
        step(quarter, per, land, partial, held, scratch)
        near(quarter).start()

    def give(quarter):
        near(quarter).wait_recv()

        def one(k):
            e = quarter * per + k
            inbox[e] = partial[e, core] + inbox[e]
            pl.when(e != pair)(lambda: back(e).start())

        loop(0, per, one)

    take(order[0])
    take(order[1])
    give(order[0])
    give(order[1])
    own_back.start()
    take(order[2])
    give(order[2])
    take(order[3])
    give(order[3])
    if not work_first:
        run()
    final(land, held, scratch, outputs)
    for quarter in order:
        others(quarter, lambda e: out(e).wait_send())
        others(quarter, lambda e: back(e).wait_send())
        others(quarter, lambda e: back_arrival(e).wait_recv())
        loop(0, per, lambda k: share(quarter * per + k).wait_send())
        near(quarter).wait_send()
    own_back.wait()
    end()


def expert_pass(sending, held, out_shape, extra, step, final, work, work_first, cols, collective_id):
    pairs, slots, width = sending.shape
    block = (pairs, slots, width)
    both = (pairs, 2, slots, width)
    sems = pltpu.SemaphoreType.DMA((pairs,))
    scratch = [
        pltpu.VMEM(both, sending.dtype),
        pltpu.VMEM(both, sending.dtype),
        pltpu.VMEM(block, sending.dtype),
    ]
    scratch += [sems] * 8 + [pltpu.SemaphoreType.DMA((2,)), pltpu.SemaphoreType.DMA((len(held),))]
    scratch += [pltpu.VMEM(a.shape, a.dtype) for a in held] + extra + work.scratch()
    out_shape = [jax.ShapeDtypeStruct(block, sending.dtype)] + out_shape
    shapes = (len(held), len(out_shape) - 1, len(extra))
    everywhere = pl.BlockSpec(memory_space=pl.ANY)
    return pl.pallas_call(
        functools.partial(expert_kernel, cols, step, final, work_first, work, shapes),
        out_shape=out_shape + work.out_shape,
        in_specs=[everywhere] * (1 + len(held) + len(work.arrays)),
        out_specs=[everywhere] * (len(out_shape) + len(work.out_shape)),
        scratch_shapes=scratch,
        compiler_params=pltpu.CompilerParams(
            collective_id=collective_id, has_side_effects=True, vmem_limit_bytes=52 * 2**20
        ),
    )(sending, *held, *work.arrays)


def forward_step(quarter, per, land, partial, held, scratch):
    gate, up, down = held
    gate_kept, up_kept, hidden_kept = scratch[:3]
    rows = land[pl.ds(quarter * per, per)].reshape(-1, land.shape[-1])

    def strip(at):
        inner_gate = dot(rows, gate[:, at], (1, 0))
        inner_up = dot(rows, up[:, at], (1, 0))
        gate_kept[quarter, :, at] = inner_gate.astype(jnp.bfloat16)
        up_kept[quarter, :, at] = inner_up.astype(jnp.bfloat16)
        hidden_kept[quarter, :, at] = (apply_silu(inner_gate) * inner_up).astype(jnp.bfloat16)

    strips(gate.shape[1], strip)
    total = dot(hidden_kept[quarter], down[...], (1, 0)).astype(jnp.bfloat16)
    partial[pl.ds(quarter * per, per)] = total.reshape((per,) + partial.shape[1:])


def forward_final(land, held, scratch, outputs):
    sems = scratch[3]
    copies = [
        pltpu.make_async_copy(source, outputs[i], sems.at[i])
        for i, source in enumerate((land,) + tuple(scratch[:3]))
    ]
    for copy in copies:
        copy.start()
    for copy in copies:
        copy.wait()


def expert_forward(sending, gate, up, down, work, cols, collective_id):
    pairs, slots, width = sending.shape
    kept = (QUARTERS, 2 * pairs * slots // QUARTERS, gate.shape[1])
    out_shape = [jax.ShapeDtypeStruct((pairs, 2, slots, width), sending.dtype)]
    out_shape += [jax.ShapeDtypeStruct(kept, sending.dtype)] * 3
    extra = [pltpu.VMEM(kept, sending.dtype)] * 3 + [pltpu.SemaphoreType.DMA((4,))]
    return expert_pass(
        sending, [gate, up, down], out_shape, extra, forward_step, forward_final, work, False,
        cols, collective_id,
    )


def backward_step(quarter, per, land, partial, held, scratch):
    gate, up, down, _, gate_kept, up_kept, _ = held
    grads = land[pl.ds(quarter * per, per)].reshape(-1, land.shape[-1])

    def strip(at):
        upstream = dot(grads, down[at, :], (1, 1))
        inner_gate = gate_kept[quarter, :, at].astype(jnp.float32)
        inner_up = up_kept[quarter, :, at].astype(jnp.float32)
        gate_kept[quarter, :, at] = (upstream * inner_up * silu_slope(inner_gate)).astype(
            jnp.bfloat16
        )
        up_kept[quarter, :, at] = (upstream * apply_silu(inner_gate)).astype(jnp.bfloat16)

    strips(gate.shape[1], strip)
    total = dot(gate_kept[quarter], gate[...], (1, 1)) + dot(up_kept[quarter], up[...], (1, 1))
    partial[pl.ds(quarter * per, per)] = total.astype(jnp.bfloat16).reshape(
        (per,) + partial.shape[1:]
    )


GRAD_STRIP = 256


def backward_final(land, held, scratch, outputs):
    _, _, _, rows, low_gate, low_up, hidden = held
    buffers, sems = scratch
    width, inner = land.shape[-1], hidden.shape[-1]
    row_count = low_gate.shape[0] * low_gate.shape[1]
    started = {}

    def flat(ref):
        return ref[...].reshape(row_count, ref.shape[-1])

    def turned(ref, at):
        lead = ref.shape[:-1]
        return ref[(slice(None),) * len(lead) + (at,)].reshape(row_count, GRAD_STRIP).T

    def store(slot, part, value, target):
        if (slot, part) in started:
            started[slot, part].wait()
        view = buffers.at[slot, part, :, pl.ds(0, value.shape[1])]
        buffers[slot, part, :, 0 : value.shape[1]] = value
        copy = pltpu.make_async_copy(view, target, sems.at[slot, part])
        copy.start()
        started[slot, part] = copy

    for j in range(width // GRAD_STRIP):
        at = slice(j * GRAD_STRIP, (j + 1) * GRAD_STRIP)
        left = turned(rows, at)
        store(j % 2, 0, dot(left, flat(low_gate), (1, 0)), outputs[0].at[at])
        store(j % 2, 1, dot(left, flat(low_up), (1, 0)), outputs[1].at[at])
    for j in range(inner // GRAD_STRIP):
        at = slice(j * GRAD_STRIP, (j + 1) * GRAD_STRIP)
        value = dot(turned(hidden, at), land[...].reshape(row_count, width), (1, 0))
        store(j % 2, j // 2 % 2, value, outputs[2].at[at])
    for copy in started.values():
        copy.wait()


def expert_backward(sending, gate, up, down, kept, work, cols, collective_id):
    out_shape = [jax.ShapeDtypeStruct(w.shape, jnp.float32) for w in (gate, up, down)]
    widest = max(gate.shape[1], down.shape[1])
    extra = [
        pltpu.VMEM((2, 2, GRAD_STRIP, widest), jnp.float32),
        pltpu.SemaphoreType.DMA((2, 2)),
    ]
    return expert_pass(
        sending, [gate, up, down] + list(kept), out_shape, extra, backward_step, backward_final,
        work, True, cols, collective_id,
    )


def on_device(
    hidden_in,
    w_query,
    w_key,
    w_value,
    w_out,
    norm_attn,
    norm_ffn,
    w_router,
    shared_gate,
    shared_up,
    shared_down,
    expert_gate,
    expert_up,
    expert_down,
    teacher,
    routes,
    cont_lengths,
    valid_mask,
):
    rows_dev, groups, model_width = hidden_in.shape
    tokens = rows_dev * groups
    head_count = lax.axis_size("head")
    cols = lax.axis_size("blk")
    devices = head_count * cols
    slices = devices // EXPERTS
    pairs = devices // 2
    shard = w_query.shape[0]
    hidden = shared_gate.shape[1]
    bf16, f32 = jnp.bfloat16, jnp.float32
    me = flat_index(cols)
    core, pair = lax.rem(me, 2), lax.div(me, 2)
    holds, unit = unit_place(pair)

    packed = jnp.concatenate([w_query, w_key, w_value], axis=1)
    router_size = shard * EXPERTS
    router_rows = -(-router_size // 128)
    router_pad = router_rows * 128 - router_size

    def in_rows(gains_first, gains_second, scalar, router):
        count = gains_first.shape[0]
        pieces = [
            jnp.pad(gains_first.astype(f32), ((0, 0), (0, 128 - shard))),
            jnp.pad(gains_second.astype(f32), ((0, 0), (0, 128 - shard))),
            jnp.broadcast_to(scalar, (count, 128)),
            jnp.pad(router.astype(f32), ((0, 0), (0, router_pad + (5 - router_rows) * 128))),
        ]
        return jnp.concatenate(pieces, axis=1).reshape(count, 8, 128)

    small = in_rows(
        norm_attn[None],
        norm_ffn[None],
        jnp.sum(valid_mask.astype(f32)),
        w_router.reshape(1, router_size),
    )[0]
    all_packed, all_small = gather_all([packed, small], cols, 0)
    proj_mat = all_packed.reshape(model_width, 3 * model_width)
    all_small = all_small.reshape(devices, 8, 128)
    gain_attn = all_small[:, 0, :shard].reshape(model_width)
    gain_ffn = all_small[:, 1, :shard].reshape(model_width)
    valid_total = jnp.sum(all_small[:, 2, 0])
    route_mat = (
        all_small[:, 3 : 3 + router_rows]
        .reshape(devices, router_rows * 128)[:, :router_size]
        .reshape(model_width, EXPERTS)
        .astype(bf16)
    )

    wide = jnp.concatenate([shared_gate, shared_up], axis=1)
    share_wide = lax.all_gather(wide, AXES, axis=0, tiled=True)

    local_pos = me * rows_dev + jnp.arange(rows_dev, dtype=jnp.int32)
    local_begin = segment_starts(local_pos, cont_lengths)
    cosine, sine = rotary_tables(local_pos, local_begin)
    flat_in = hidden_in.reshape(tokens, model_width)
    def rotated(halves, sine_now):
        first, second = halves[:, 0], halves[:, 1]
        return jnp.concatenate(
            [first * cosine - second * sine_now, second * cosine + first * sine_now], axis=1
        )

    def by_unit(blocks):
        rows = blocks.shape[1]
        return (
            blocks.reshape(HEADS, rows, rows_dev, groups)
            .transpose(3, 0, 1, 2)
            .reshape(groups * HEADS, rows, rows_dev)
        )

    def by_head(blocks):
        rows = blocks.shape[1]
        return (
            blocks.reshape(groups, HEADS, rows, rows_dev)
            .transpose(1, 2, 3, 0)
            .reshape(HEADS, rows, tokens)
        )

    at_home = rows_dev == TILE and groups == 1
    if at_home:
        normed_attn, scaling_attn, q_blocks, kv_blocks = project(
            flat_in, gain_attn, proj_mat, cosine, sine, cols, 1
        )
    else:
        normed_exact, scaling_attn = root_norm(flat_in, gain_attn)
        normed_attn = normed_exact.astype(bf16)
        projected = dot(proj_mat, normed_attn, (0, 1)).reshape(
            3, HEADS, 2, HEAD_DIM // 2, tokens
        )
        qkv_blocks = jnp.concatenate(
            [
                rotated(projected[0], sine),
                rotated(projected[1], sine),
                projected[2].reshape(HEADS, HEAD_DIM, tokens),
            ],
            axis=1,
        ).astype(bf16)
        q_blocks, kv_blocks = to_units(by_unit(qkv_blocks), cols, True, 1)

    unit_lengths = lax.dynamic_slice_in_dim(
        cont_lengths, jnp.minimum(unit // HEADS, groups - 1), 1, axis=0
    )
    place = (
        (2 * jnp.arange(pairs, dtype=jnp.int32) + core)[:, None] * rows_dev
        + jnp.arange(rows_dev, dtype=jnp.int32)
    ).reshape(-1)
    run = segment_starts(place, unit_lengths).reshape(-1, 1, TILE)
    queries, keys_values = to_tiles(q_blocks), to_tiles(kv_blocks)
    if at_home:
        exact, lse, attended, out_mat, share_down = attend_home(
            queries, keys_values, run, [w_out, shared_down], cols, 2
        )
    else:
        exact, low, lse = attend(queries, keys_values, run, rows_dev)
        (attended,) = to_tokens([from_tiles(low, rows_dev)], cols, 2)
        out_mat, share_down = gather_all([w_out, shared_down], cols, 11)
    out_mat = out_mat.reshape(model_width, model_width)
    share_down = share_down.reshape(hidden, model_width)
    attended = by_head(attended).reshape(model_width, tokens)

    residual_mid = flat_in + dot(attended, out_mat, (0, 0))
    normed_mid, scaling_ffn = root_norm(residual_mid, gain_ffn)
    normed_ffn = normed_mid.astype(bf16)

    route_flat = routes.reshape(tokens, TOP)
    route_onehot = (route_flat[:, :, None] == jnp.arange(EXPERTS, dtype=jnp.int32)).astype(f32)
    flat_routes = route_flat.reshape(-1)
    route_hits = (flat_routes[:, None] == jnp.arange(EXPERTS, dtype=jnp.int32)).astype(bf16)
    order = jnp.arange(tokens * TOP, dtype=jnp.int32)
    before = dot((order[None, :] < order[:, None]).astype(bf16), route_hits, (1, 0))
    ranking = jnp.sum(before * route_hits.astype(f32), axis=1).astype(jnp.int32)
    slot_of = (flat_routes * CAP + ranking).reshape(tokens, TOP)
    slot_ids = jnp.arange(EXPERTS * CAP, dtype=jnp.int32)
    place_first = (slot_ids[:, None] == slot_of[None, :, 0]).astype(bf16)
    place_second = (slot_ids[:, None] == slot_of[None, :, 1]).astype(bf16)

    sending = dot(place_first + place_second, normed_ffn, (1, 0)).astype(bf16)
    sending = sending.reshape(EXPERTS, CAP, model_width)

    logits = dot(normed_ffn, route_mat, (1, 0))
    chosen = jnp.sum(route_onehot * logits[:, None, :], axis=-1)
    gate_probs = jax.nn.softmax(chosen, axis=1)
    out = jax.ShapeDtypeStruct
    shared_work = Work(
        [normed_ffn, share_wide, share_down],
        [
            out((tokens, hidden), bf16),
            out((tokens, hidden), bf16),
            out((tokens, hidden), bf16),
            out((tokens, model_width), f32),
        ],
        shared_forward,
    )
    if slices == 2:
        passed = expert_forward(
            sending, expert_gate, expert_up, expert_down, shared_work, cols, 3
        )
        returned, kept, shared_results = passed[0], passed[1:5], passed[5:]
    else:
        (arrived,) = spread([sending], cols, slices, EXPERTS, 3)
        arrived = arrived.reshape(devices * CAP, model_width)
        inner_gate = dot(arrived, expert_gate, (1, 0))
        inner_up = dot(arrived, expert_up, (1, 0))
        inner_hidden = (apply_silu(inner_gate) * inner_up).astype(bf16)
        partial_out = dot(inner_hidden, expert_down, (1, 0)).astype(bf16)
        returned, *shared_results = collect(
            [partial_out.reshape(slices, EXPERTS, CAP, model_width)], cols, 4, shared_work
        )
    shared_gate_in, shared_up_in, shared_hidden, shared_out = shared_results
    expert_rows = returned.reshape(EXPERTS * CAP, model_width)
    routed_first = dot(place_first, expert_rows, (0, 0))
    routed_second = dot(place_second, expert_rows, (0, 0))
    mixture = gate_probs[:, 0:1] * routed_first + gate_probs[:, 1:2] * routed_second
    layer_flat = residual_mid + shared_out + mixture

    keep_rows = valid_mask.reshape(tokens).astype(f32)[:, None]
    deviation = layer_flat - teacher.reshape(tokens, model_width)
    loss_local = jnp.sum(keep_rows * deviation * deviation)
    grad_rows = keep_rows * deviation * (tokens * devices / valid_total)
    back_first = (gate_probs[:, 0:1] * grad_rows).astype(bf16)
    back_second = (gate_probs[:, 1:2] * grad_rows).astype(bf16)
    back_send = (
        dot(place_first, back_first, (1, 0)) + dot(place_second, back_second, (1, 0))
    ).astype(bf16)
    shared_work = Work(
        [
            grad_rows.astype(bf16),
            normed_ffn,
            shared_gate_in,
            shared_up_in,
            shared_hidden,
            share_wide,
            share_down,
        ],
        [
            out(share_wide.shape, bf16),
            out(share_down.shape, bf16),
            out((tokens, model_width), f32),
        ],
        shared_backward,
        {0: 5, 1: 6},
    )
    back_send = back_send.reshape(EXPERTS, CAP, model_width)
    if slices == 2:
        passed = expert_backward(
            back_send, expert_gate, expert_up, expert_down, kept, shared_work, cols, 5
        )
        back_returned, grad_expert_gate, grad_expert_up, grad_expert_down = passed[:4]
        grad_share_wide, grad_share_down, shared_back = passed[4:]
    else:
        back_arrived, grad_share_wide, grad_share_down, shared_back = spread(
            [back_send], cols, slices, EXPERTS, 5, shared_work
        )
        back_arrived = back_arrived.reshape(devices * CAP, model_width)
        grad_inner = dot(back_arrived, expert_down, (1, 1))
        grad_inner_gate = (grad_inner * inner_up * silu_slope(inner_gate)).astype(bf16)
        grad_inner_up = (grad_inner * apply_silu(inner_gate)).astype(bf16)
        back_partial = (
            dot(grad_inner_gate, expert_gate, (1, 1)) + dot(grad_inner_up, expert_up, (1, 1))
        ).astype(bf16)
        (back_returned,) = collect(
            [back_partial.reshape(slices, EXPERTS, CAP, model_width)], cols, 6
        )
        grad_expert_down = dot(inner_hidden, back_arrived, (0, 0))
        grad_expert_gate = dot(arrived, grad_inner_gate, (0, 0))
        grad_expert_up = dot(arrived, grad_inner_up, (0, 0))

    grad_gate = jnp.stack(
        [jnp.sum(grad_rows * routed_first, axis=-1), jnp.sum(grad_rows * routed_second, axis=-1)],
        axis=1,
    )
    grad_chosen = gate_probs * (grad_gate - jnp.sum(gate_probs * grad_gate, axis=1, keepdims=True))
    grad_logits = jnp.sum(route_onehot * grad_chosen[:, :, None], axis=1).astype(bf16)
    grad_route_mat = dot(normed_ffn, grad_logits, (0, 0))

    back_rows = back_returned.reshape(EXPERTS * CAP, model_width)
    grad_normed = (
        dot(place_first + place_second, back_rows, (0, 0))
        + dot(grad_logits, route_mat, (1, 1))
        + shared_back
    )

    grad_mid_norm, grad_gain_ffn = root_norm_back(residual_mid, scaling_ffn, gain_ffn, grad_normed)
    grad_mid = grad_rows + grad_mid_norm
    grad_mid_low = grad_mid.astype(bf16)
    grad_attended = dot(out_mat, grad_mid_low, (1, 1)).astype(bf16)
    grad_out_mat = dot(attended, grad_mid_low, (1, 0))
    grad_blocks = by_unit(grad_attended.reshape(HEADS, HEAD_DIM, tokens))
    spots = (2, cols // 4, 2, 2)
    parts = [
        grad_share_wide.reshape(spots + (shard, 2 * hidden)),
        grad_share_down.reshape(spots + shared_down.shape),
        grad_out_mat.astype(bf16).reshape(spots + (shard, model_width)),
    ]
    if at_home:
        dq, dkv, share_sums, grad_share_down, grad_out_sum = attend_back_home(
            queries, keys_values, grad_blocks, exact, lse, run, parts, cols, 10
        )
    else:
        (grad_blocks,) = to_units(grad_blocks, cols, False, 7)
        dq, dkv, share_sums, grad_share_down, grad_out_sum = attend_back(
            queries, keys_values, to_tiles(grad_blocks), exact, lse, run, rows_dev, parts, cols, 10
        )
        dq, dkv = to_tokens([from_tiles(dq, rows_dev), from_tiles(dkv, rows_dev)], cols, 8)
    dq, dkv = by_head(dq).astype(f32), by_head(dkv)

    def halves_of(rows):
        return rows.reshape(HEADS, 2, HEAD_DIM // 2, tokens)

    grad_proj = jnp.concatenate(
        [
            rotated(halves_of(dq), -sine).astype(bf16).reshape(model_width, tokens),
            rotated(halves_of(dkv[:, :HEAD_DIM].astype(f32)), -sine)
            .astype(bf16)
            .reshape(model_width, tokens),
            dkv[:, HEAD_DIM:].reshape(model_width, tokens),
        ],
        axis=0,
    )
    grad_normed_attn = dot(grad_proj, proj_mat, (0, 1))
    grad_in_norm, grad_gain_attn = root_norm_back(
        flat_in, scaling_attn, gain_attn, grad_normed_attn
    )
    input_grad = (grad_mid + grad_in_norm).reshape(rows_dev, groups, model_width)

    grad_attn = dot(normed_attn, grad_proj, (0, 1)).astype(bf16)
    tail = in_rows(
        grad_gain_attn.reshape(devices, shard),
        grad_gain_ffn.reshape(devices, shard),
        loss_local,
        grad_route_mat.reshape(devices, router_size),
    )
    attn_sums, tail_sums = reduce_all(
        [grad_attn.reshape(spots + (shard, 3 * model_width)), tail.reshape(spots + (8, 128))],
        cols,
        9,
    )
    loss_value = tail_sums[2, 0] / (valid_total * model_width)
    return (
        layer_flat.reshape(rows_dev, groups, model_width),
        input_grad,
        loss_value,
        attn_sums[:, :model_width],
        attn_sums[:, model_width : 2 * model_width],
        attn_sums[:, 2 * model_width :],
        grad_out_sum,
        tail_sums[0, :shard],
        tail_sums[1, :shard],
        tail_sums[3 : 3 + router_rows].reshape(-1)[:router_size].reshape(shard, EXPERTS),
        share_sums[:, :hidden],
        share_sums[:, hidden:],
        grad_share_down,
        grad_expert_gate,
        grad_expert_up,
        grad_expert_down,
    )


def solution(mesh):
    placed = (
        P(("head", "blk"), None, None),
        P(("head", "blk"), None),
        P(("head", "blk"), None),
        P(("head", "blk"), None),
        P(("head", "blk"), None),
        P(("head", "blk")),
        P(("head", "blk")),
        P(("head", "blk"), None),
        P(("head", "blk"), None),
        P(("head", "blk"), None),
        P(("head", "blk"), None),
        P(None, ("head", "blk")),
        P(None, ("head", "blk")),
        P(("head", "blk"), None),
        P(("head", "blk"), None, None),
        P(("head", "blk"), None, None),
        P(),
        P(("head", "blk"), None),
    )
    return jax.shard_map(
        on_device,
        mesh=mesh,
        in_specs=placed,
        out_specs=(
            P(("head", "blk"), None, None),
            P(("head", "blk"), None, None),
            P(),
            P(("head", "blk"), None),
            P(("head", "blk"), None),
            P(("head", "blk"), None),
            P(("head", "blk"), None),
            P(("head", "blk")),
            P(("head", "blk")),
            P(("head", "blk"), None),
            P(("head", "blk"), None),
            P(("head", "blk"), None),
            P(("head", "blk"), None),
            P(None, ("head", "blk")),
            P(None, ("head", "blk")),
            P(("head", "blk"), None),
        ),
        check_vma=False,
    )
```

```python
import functools
import math

import jax
import jax.numpy as jnp
from jax import lax
from jax.experimental import pallas as pl
from jax.experimental.pallas import tpu as pltpu
from jax.sharding import PartitionSpec as P

HEADS = 12
HEAD_DIM = 64
EXPERTS = 16
TOP = 2
PROMPT = 4096
LONGEST = 768
CAP = 64

EPSILON = 1e-06
NEGATIVE = -1e30
SCORE_SCALE = HEAD_DIM ** (-0.5)
EXP_SCALE = SCORE_SCALE * math.log2(math.e)

TILE = 256
FWD_WIDE, FWD_MASK = 8, 4
BWD_WIDE, BWD_MASK = 4, 2

MESH_ID = pl.DeviceIdType.MESH
AXES = ("head", "blk")


def apply_silu(argument):
    return argument * jax.nn.sigmoid(argument)


def silu_slope(argument):
    sigmoid_val = jax.nn.sigmoid(argument)
    return sigmoid_val * (1.0 + argument * (1.0 - sigmoid_val))


def root_norm(inputs, gain_vec):
    scaling = lax.rsqrt(jnp.mean(inputs * inputs, axis=-1, keepdims=True) + EPSILON)
    return (inputs * scaling * gain_vec, scaling)


def root_norm_back(inputs, scaling, gain_vec, upstream):
    weighted = gain_vec * upstream
    through = scaling * weighted - inputs * scaling**3 * jnp.mean(
        weighted * inputs, axis=-1, keepdims=True
    )
    return (through, jnp.sum(upstream * inputs * scaling, axis=0))


def segment_starts(positions, cont_lengths):
    count = cont_lengths.shape[1]
    earlier = jnp.arange(count)[None, :] < jnp.arange(count)[:, None]
    begins = PROMPT + jnp.sum(jnp.where(earlier, cont_lengths[:, None, :], 0), axis=2)
    passed = begins[None, :, :] <= positions[:, None, None]
    return jnp.max(jnp.where(passed, begins[None], 0), axis=-1)


def rotary_tables(positions, run_begin):
    relative = jnp.where(
        positions[:, None] < PROMPT, positions[:, None], PROMPT + positions[:, None] - run_begin
    )
    angle_pos = relative.astype(jnp.float32).reshape(1, -1)
    half_dim = HEAD_DIM // 2
    frequency = jnp.exp(
        jnp.arange(half_dim, dtype=jnp.int32).astype(jnp.float32)
        * (-2.0 * math.log(10000.0) / HEAD_DIM)
    )
    angles = angle_pos * frequency[:, None]
    return (jnp.cos(angles), jnp.sin(angles))


def flat_index(cols):
    return lax.axis_index("head") * cols + lax.axis_index("blk")


def coords(flat, cols):
    return (lax.div(flat, cols), lax.rem(flat, cols))


def greet(flat, cols):
    pl.semaphore_signal(
        pltpu.get_barrier_semaphore(),
        inc=1,
        device_id=coords(flat, cols),
        device_id_type=MESH_ID,
    )


def remote(source, target, send_sem, recv_sem, flat, cols):
    return pltpu.make_async_remote_copy(
        src_ref=source,
        dst_ref=target,
        send_sem=send_sem,
        recv_sem=recv_sem,
        device_id=coords(flat, cols),
        device_id_type=MESH_ID,
    )


def loop(first, last, body):
    def step(index, carry):
        body(index)
        return carry

    lax.fori_loop(first, last, step, 0)


def greet_partners(cols, size, partners):
    me = flat_index(cols)
    mine, group = lax.rem(me, size), lax.div(me, size)
    loop(1, partners, lambda s: greet(lax.rem(group + s, partners) * size + mine, cols))
    for t in range(1, size):
        greet(group * size + lax.rem(mine + t, size), cols)
    pl.semaphore_wait(pltpu.get_barrier_semaphore(), partners + size - 2)
    return mine, group


class Work:
    def __init__(self, arrays, out_shape, body, reuse=None):
        self.arrays, self.out_shape, self.body = list(arrays), list(out_shape), body
        self.reuse = reuse or {}

    def own_buffers(self):
        return [i for i in range(len(self.out_shape)) if i not in self.reuse]

    def scratch(self):
        held = self.arrays + [self.out_shape[i] for i in self.own_buffers()]
        total = len(self.arrays) + len(self.out_shape)
        return [pltpu.VMEM(a.shape, a.dtype) for a in held] + [pltpu.SemaphoreType.DMA((total,))]

    def bind(self, refs):
        count, total = len(self.arrays), len(self.arrays) + len(self.out_shape)
        inputs, outputs = refs[:count], refs[count:total]
        held_in, rest, sems = refs[total : total + count], refs[total + count : -1], refs[-1]
        held_out = [None] * len(outputs)
        for buffer, i in zip(rest, self.own_buffers()):
            held_out[i] = buffer
        for i, source in self.reuse.items():
            held_out[i] = held_in[source]
        loads = [
            pltpu.make_async_copy(inputs[i], held_in[i], sems.at[i]) for i in range(count)
        ]
        stores = [
            pltpu.make_async_copy(held_out[i], outputs[i], sems.at[count + i])
            for i in range(len(outputs))
        ]

        def begin():
            for copy in loads:
                copy.start()

        def run():
            for copy in loads:
                copy.wait()
            self.body(held_in, held_out, [copy.start for copy in stores])

        def end():
            for copy in stores:
                copy.wait()

        return begin, run, end


def split_refs(refs, count, work):
    extra_in = len(work.arrays) if work else 0
    extra_out = len(work.out_shape) if work else 0
    inputs, refs = refs[:count], refs[count:]
    work_in, refs = refs[:extra_in], refs[extra_in:]
    outputs, refs = refs[:count], refs[count:]
    work_out, refs = refs[:extra_out], refs[extra_out:]
    if not work:
        return inputs, outputs, refs, (lambda: None,) * 3
    held = extra_in + len(work.own_buffers()) + 1
    return inputs, outputs, refs[:-held], work.bind(work_in + work_out + refs[-held:])


def spread_kernel(cols, size, partners, work, count, *refs):
    inputs, outputs, sems, (begin, run, end) = split_refs(refs, count, work)
    begin()
    mine, group = greet_partners(cols, size, partners)

    def far(i, s):
        send, recv = sems[5 * i], sems[5 * i + 1]
        other = lax.rem(group + s, partners)
        return remote(
            inputs[i].at[other], outputs[i].at[mine, group], send.at[s], recv.at[s], other * size + mine, cols
        )

    def near(i, s, t):
        send, recv = sems[5 * i + 2], sems[5 * i + 3]
        block = outputs[i].at[mine, lax.rem(group - s + partners, partners)]
        target = group * size + lax.rem(mine + t, size)
        return remote(block, block, send.at[s, t], recv.at[s, t], target, cols)

    def own(i):
        return pltpu.make_async_copy(inputs[i].at[group], outputs[i].at[mine, group], sems[5 * i + 4])

    def each(action):
        for i in range(count):
            action(i)

    def near_all(s, action):
        for i in range(count):
            for t in range(1, size):
                action(near(i, s, t))

    each(lambda i: own(i).start())
    loop(1, partners, lambda s: each(lambda i: far(i, s).start()))
    each(lambda i: own(i).wait())
    near_all(0, lambda copy: copy.start())
    run()

    def relay(s):
        each(lambda i: far(i, s).wait_recv())
        near_all(s, lambda copy: copy.start())

    loop(1, partners, relay)
    loop(1, partners, lambda s: each(lambda i: far(i, s).wait_send()))
    loop(0, partners, lambda s: near_all(s, lambda copy: copy.wait()))
    end()


def spread(arrays, cols, size, partners, collective_id, work=None):
    count = len(arrays)
    out_shape, scratch = [], []
    for array in arrays:
        block = array.shape[1:]
        out_shape.append(jax.ShapeDtypeStruct((size, partners) + block, array.dtype))
        scratch += [
            pltpu.SemaphoreType.DMA((partners,)),
            pltpu.SemaphoreType.DMA((partners,)),
            pltpu.SemaphoreType.DMA((partners, size)),
            pltpu.SemaphoreType.DMA((partners, size)),
            pltpu.SemaphoreType.DMA,
        ]
    extra = []
    if work:
        extra, out_shape, scratch = work.arrays, out_shape + work.out_shape, scratch + work.scratch()
    return pl.pallas_call(
        functools.partial(spread_kernel, cols, size, partners, work, count),
        out_shape=out_shape,
        in_specs=[pl.BlockSpec(memory_space=pl.ANY)] * (count + len(extra)),
        out_specs=[pl.BlockSpec(memory_space=pl.ANY)] * len(out_shape),
        scratch_shapes=scratch,
        compiler_params=pltpu.CompilerParams(
            collective_id=collective_id, has_side_effects=True, vmem_limit_bytes=52 * 2**20
        ),
    )(*arrays, *extra)


def collect_kernel(cols, size, partners, work, count, *refs):
    inputs, outputs, scratch, (begin, run, end) = split_refs(refs, count, work)
    begin()
    mine, group = greet_partners(cols, size, partners)

    def near(i, s, t):
        inbox, send, recv = scratch[7 * i + 1], scratch[7 * i + 2], scratch[7 * i + 3]
        other = lax.rem(group + s, partners)
        member = lax.rem(mine + t, size)
        return remote(
            inputs[i].at[member, other],
            inbox.at[t - 1, other],
            send.at[s, t],
            recv.at[s, t],
            group * size + member,
            cols,
        )

    def far(i, s):
        stage, send, recv = scratch[7 * i], scratch[7 * i + 4], scratch[7 * i + 5]
        other = lax.rem(group + s, partners)
        return remote(
            stage.at[other], outputs[i].at[group], send.at[s], recv.at[s], other * size + mine, cols
        )

    def own(i):
        return pltpu.make_async_copy(
            scratch[7 * i].at[group], outputs[i].at[group], scratch[7 * i + 6]
        )

    def each(action):
        for i in range(count):
            action(i)

    def near_all(s, action):
        for i in range(count):
            for t in range(1, size):
                action(near(i, s, t))

    def add(s):
        other = lax.rem(group + s, partners)
        for i in range(count):
            stage, inbox = scratch[7 * i], scratch[7 * i + 1]
            total = inputs[i][mine, other].astype(jnp.float32)
            for t in range(1, size):
                total = total + inbox[t - 1, other].astype(jnp.float32)
            stage[other] = total.astype(stage.dtype)

    loop(1, partners, lambda s: near_all(s, lambda copy: copy.start()))
    near_all(0, lambda copy: copy.start())

    def relay(s):
        near_all(s, lambda copy: copy.wait_recv())
        add(s)
        each(lambda i: far(i, s).start())

    loop(1, partners, relay)
    near_all(0, lambda copy: copy.wait_recv())
    add(0)
    each(lambda i: own(i).start())
    run()
    loop(0, partners, lambda s: near_all(s, lambda copy: copy.wait_send()))
    loop(1, partners, lambda s: each(lambda i: far(i, s).wait()))
    each(lambda i: own(i).wait())
    end()


def collect(arrays, cols, collective_id, work=None):
    count = len(arrays)
    size, partners = arrays[0].shape[:2]
    out_shape, scratch = [], []
    for array in arrays:
        block = array.shape[2:]
        out_shape.append(jax.ShapeDtypeStruct((partners,) + block, array.dtype))
        scratch += [
            pltpu.VMEM((partners,) + block, array.dtype),
            pltpu.VMEM((size - 1, partners) + block, array.dtype),
            pltpu.SemaphoreType.DMA((partners, size)),
            pltpu.SemaphoreType.DMA((partners, size)),
            pltpu.SemaphoreType.DMA((partners,)),
            pltpu.SemaphoreType.DMA((partners,)),
            pltpu.SemaphoreType.DMA,
        ]
    extra = []
    if work:
        extra, out_shape, scratch = work.arrays, out_shape + work.out_shape, scratch + work.scratch()
    return pl.pallas_call(
        functools.partial(collect_kernel, cols, size, partners, work, count),
        out_shape=out_shape,
        in_specs=[pl.BlockSpec(memory_space=pltpu.VMEM)] * count
        + [pl.BlockSpec(memory_space=pl.ANY)] * len(extra),
        out_specs=[pl.BlockSpec(memory_space=pl.ANY)] * len(out_shape),
        scratch_shapes=scratch,
        compiler_params=pltpu.CompilerParams(
            collective_id=collective_id, has_side_effects=True, vmem_limit_bytes=52 * 2**20
        ),
    )(*arrays, *extra)


def spot():
    column = lax.axis_index("blk")
    return (
        lax.axis_index("head"),
        lax.div(column, 4),
        lax.rem(lax.div(column, 2), 2),
        lax.rem(column, 2),
    )


def at_spot(head, depth, x, core):
    return (head, depth * 4 + x * 2 + core)


def push(source, target, send_sem, recv_sem, device):
    return pltpu.make_async_remote_copy(
        src_ref=source,
        dst_ref=target,
        send_sem=send_sem,
        recv_sem=recv_sem,
        device_id=device,
        device_id_type=MESH_ID,
    )


def greet_mesh(depths):
    head, depth, x, core = spot()
    barrier = pltpu.get_barrier_semaphore()

    def signal(device):
        pl.semaphore_signal(barrier, inc=1, device_id=device, device_id_type=MESH_ID)

    loop(1, depths, lambda s: signal(at_spot(head, lax.rem(depth + s, depths), x, core)))
    signal(at_spot(head, depth, 1 - x, core))
    signal(at_spot(1 - head, depth, x, core))
    signal(at_spot(head, depth, x, 1 - core))
    pl.semaphore_wait(barrier, depths + 2)


GATHER_SEMS = 13


def gather_sems(depths):
    row, square = pltpu.SemaphoreType.DMA((depths,)), pltpu.SemaphoreType.DMA((4, depths))
    return [row] * 10 + [square] * 2 + [pltpu.SemaphoreType.DMA]


class Gather:
    def __init__(self, source, result, sems, depths, cut):
        self.source, self.result, self.sems = source, result, sems
        self.depths, self.cut = depths, cut
        self.width = source.shape[-1]

    def along(self, s):
        head, depth, x, core = spot()
        device = at_spot(head, lax.rem(depth + s, self.depths), x, core)
        target = self.result.at[head, depth, x, core]
        return push(self.source, target, self.sems[0].at[s], self.sems[1].at[s], device)

    def block(self, s, far_head, far_x):
        head, depth, x, core = spot()
        return self.result.at[
            1 - head if far_head else head,
            lax.rem(depth - s + self.depths, self.depths),
            1 - x if far_x else x,
            core,
        ]

    def hop(self, kind, s):
        head, depth, x, core = spot()
        if kind in (0, 3):
            device = at_spot(head, depth, 1 - x, core)
        else:
            device = at_spot(1 - head, depth, x, core)
        view = self.block(s, kind == 3, kind == 2)
        if kind == 2:
            view = view.at[:, pl.ds(0, self.cut)]
        if kind == 3:
            view = view.at[:, pl.ds(self.cut, self.width - self.cut)]
        sems = self.sems
        return push(view, view, sems[2 + 2 * kind].at[s], sems[3 + 2 * kind].at[s], device)

    def kinds(self):
        return (2, 3) if self.cut < self.width else (2,)

    def share(self, part, s):
        head, depth, x, core = spot()
        view = self.block(s, part // 2 == 1, part % 2 == 1)
        device = at_spot(head, depth, x, 1 - core)
        return push(view, view, self.sems[10].at[part, s], self.sems[11].at[part, s], device)

    def own(self):
        return pltpu.make_async_copy(self.source, self.result.at[spot()], self.sems[12])

    def start(self):
        self.own().start()
        loop(1, self.depths, lambda s: self.along(s).start())

    def begin_near(self, s):
        self.hop(0, s).start()
        self.hop(1, s).start()
        self.share(0, s).start()

    def start_own(self):
        self.own().wait()
        self.begin_near(0)

    def spread_near(self):
        def step(s):
            self.along(s).wait_recv()
            self.begin_near(s)

        loop(1, self.depths, step)

    def spread_far(self):
        def step(s):
            self.hop(0, s).wait_recv()
            self.hop(2, s).start()
            self.share(1, s).start()
            self.hop(1, s).wait_recv()
            if self.cut < self.width:
                self.hop(3, s).start()
            self.share(2, s).start()

        loop(0, self.depths, step)

    def settle(self):
        def step(s):
            for kind in self.kinds():
                self.hop(kind, s).wait_recv()
            self.share(3, s).start()

        loop(0, self.depths, step)

    def finish(self):
        loop(1, self.depths, lambda s: self.along(s).wait_send())

        def step(s):
            for kind in (0, 1) + self.kinds():
                self.hop(kind, s).wait_send()
            for part in range(4):
                self.share(part, s).wait()

        loop(0, self.depths, step)


def cut_of(width):
    return width // 256 * 128 if width >= 256 else width


def gathered_shape(shard, depths):
    return jax.ShapeDtypeStruct((2, depths, 2, 2) + shard.shape, shard.dtype)


def gather_kernel(depths, count, *refs):
    gathers = gathers_of(refs[:count], refs[count : 2 * count], refs[2 * count :], depths)
    greet_mesh(depths)
    for step in ("start", "start_own", "spread_near", "spread_far", "settle", "finish"):
        for gather in gathers:
            getattr(gather, step)()


def gather_all(arrays, cols, collective_id):
    depths, count = cols // 4, len(arrays)
    return pl.pallas_call(
        functools.partial(gather_kernel, depths, count),
        out_shape=[gathered_shape(array, depths) for array in arrays],
        in_specs=[pl.BlockSpec(memory_space=pl.ANY)] * count,
        out_specs=[pl.BlockSpec(memory_space=pl.ANY)] * count,
        scratch_shapes=gather_sems(depths) * count,
        compiler_params=pltpu.CompilerParams(collective_id=collective_id, has_side_effects=True),
    )(*arrays)


REDUCE_SCRATCH = 20


class Reduce:
    def __init__(self, parts, total, scratch, depths, cut):
        self.parts, self.total = parts, total
        self.sums, self.core_in, self.a1, self.b1, self.a2, self.b2, self.z_in = scratch[:7]
        self.sems = scratch[7:]
        self.depths, self.cut = depths, cut
        self.width = parts.shape[-1]
        self.two = cut < self.width
        self.first = pl.ds(0, cut)
        self.rest = pl.ds(cut, self.width - cut)

    def goal(self, s):
        return lax.rem(spot()[1] + s, self.depths)

    def to_core(self, s):
        head, depth, x, core = spot()
        goal = self.goal(s)
        return push(
            self.parts.at[:, goal, :, 1 - core],
            self.core_in.at[:, goal],
            self.sems[0].at[s],
            self.sems[1].at[s],
            at_spot(head, depth, x, 1 - core),
        )

    def hop(self, kind, s):
        head, depth, x, core = spot()
        goal = self.goal(s)
        over_x = at_spot(head, depth, 1 - x, core)
        over_head = at_spot(1 - head, depth, x, core)
        if kind == 0:
            view = self.sums.at[1 - head, goal, :, :, self.first]
            target, device = self.a1.at[goal], over_head
        elif kind == 1:
            view = self.sums.at[:, goal, 1 - x, :, self.rest]
            target, device = self.b1.at[goal], over_x
        elif kind == 2:
            view = self.sums.at[head, goal, 1 - x, :, self.first]
            target, device = self.a2.at[goal], over_x
        else:
            view = self.sums.at[1 - head, goal, x, :, self.rest]
            target, device = self.b2.at[goal], over_head
        send, recv = self.sems[2 + 2 * kind], self.sems[3 + 2 * kind]
        return push(view, target, send.at[s], recv.at[s], device)

    def along(self, s):
        head, depth, x, core = spot()
        goal = self.goal(s)
        return push(
            self.sums.at[head, goal, x],
            self.z_in.at[s],
            self.sems[10].at[s],
            self.sems[11].at[s],
            at_spot(head, goal, x, core),
        )

    def own(self, s):
        goal = self.goal(s)
        return pltpu.make_async_copy(
            self.parts.at[:, goal, :, spot()[3]], self.sums.at[:, goal], self.sems[12].at[s]
        )

    def start(self):
        def step(s):
            self.to_core(s).start()
            self.own(s).start()

        self.each(step, 0, self.depths)

    def each(self, step, first, last):
        loop(first, last, lambda i: step(lax.rem(i + 1, self.depths)))

    def add(self, where, columns, arrived):
        place = where + (slice(None), columns)
        self.sums[place] = self.sums[place] + arrived

    def near(self, first, last):
        def step(s):
            goal = self.goal(s)
            self.own(s).wait()
            self.to_core(s).wait_recv()
            whole = pl.ds(0, self.width)
            for k in range(4):
                self.add((k // 2, goal, k % 2), whole, self.core_in[k // 2, goal, k % 2])
            self.hop(0, s).start()
            if self.two:
                self.hop(1, s).start()

        self.each(step, first, last)

    def middle(self, first, last):
        head, _, x, _ = spot()

        def step(s):
            goal = self.goal(s)
            self.hop(0, s).wait_recv()
            for k in range(2):
                self.add((head, goal, k), self.first, self.a1[goal, k])
            self.hop(2, s).start()
            if self.two:
                self.hop(1, s).wait_recv()
                for k in range(2):
                    self.add((k, goal, x), self.rest, self.b1[goal, k])
                self.hop(3, s).start()

        self.each(step, first, last)

    def far(self, first, last):
        head, _, x, _ = spot()

        def step(s):
            goal = self.goal(s)
            self.hop(2, s).wait_recv()
            self.add((head, goal, x), self.first, self.a2[goal])
            if self.two:
                self.hop(3, s).wait_recv()
                self.add((head, goal, x), self.rest, self.b2[goal])
            pl.when(s > 0)(lambda: self.along(s).start())

        self.each(step, first, last)

    def finish(self):
        head, depth, x, _ = spot()
        self.total[...] = self.sums[head, depth, x].astype(jnp.float32)

        def step(s):
            self.along(s).wait_recv()
            self.total[...] += self.z_in[s].astype(jnp.float32)

        loop(1, self.depths, step)

        def sent(s):
            self.to_core(s).wait_send()
            for kind in (0, 1, 2, 3) if self.two else (0, 2):
                self.hop(kind, s).wait_send()

        loop(0, self.depths, sent)
        loop(1, self.depths, lambda s: self.along(s).wait_send())


def reduce_scratch(shape, dtype, depths, cut):
    rows, width = shape[-2:]
    rest = max(width - cut, 128)
    row = pltpu.SemaphoreType.DMA((depths,))
    return [
        pltpu.VMEM((2, depths, 2, rows, width), dtype),
        pltpu.VMEM((2, depths, 2, rows, width), dtype),
        pltpu.VMEM((depths, 2, rows, cut), dtype),
        pltpu.VMEM((depths, 2, rows, rest), dtype),
        pltpu.VMEM((depths, rows, cut), dtype),
        pltpu.VMEM((depths, rows, rest), dtype),
        pltpu.VMEM((depths, rows, width), dtype),
    ] + [row] * 13


def reduces_of(parts, totals, scratch, depths):
    return [
        Reduce(
            part,
            totals[i],
            scratch[REDUCE_SCRATCH * i : REDUCE_SCRATCH * (i + 1)],
            depths,
            cut_of(part.shape[-1]),
        )
        for i, part in enumerate(parts)
    ]


def reduce_kernel(depths, count, *refs):
    reduces = reduces_of(refs[:count], refs[count : 2 * count], refs[2 * count :], depths)
    greet_mesh(depths)
    for reduce in reduces:
        reduce.start()
    for step in ("near", "middle", "far"):
        for reduce in reduces:
            getattr(reduce, step)(0, depths)
    for reduce in reduces:
        reduce.finish()


def all_reduce_scratch(arrays, depths):
    scratch = []
    for array in arrays:
        scratch += reduce_scratch(array.shape, array.dtype, depths, cut_of(array.shape[-1]))
    return scratch


def reduce_all(arrays, cols, collective_id):
    depths, count = cols // 4, len(arrays)
    return pl.pallas_call(
        functools.partial(reduce_kernel, depths, count),
        out_shape=[jax.ShapeDtypeStruct(array.shape[-2:], jnp.float32) for array in arrays],
        in_specs=[pl.BlockSpec(memory_space=pl.ANY)] * count,
        out_specs=[pl.BlockSpec(memory_space=pltpu.VMEM)] * count,
        scratch_shapes=all_reduce_scratch(arrays, depths),
        compiler_params=pltpu.CompilerParams(
            collective_id=collective_id, has_side_effects=True, vmem_limit_bytes=52 * 2**20
        ),
    )(*arrays)


def unit_place(pair):
    return lax.rem(pair, 4) != 3, lax.div(pair, 4) * 3 + lax.rem(pair, 4)


def greet_units(cols, pairs, sibling, to_units):
    me = flat_index(cols)
    core, pair = lax.rem(me, 2), lax.div(me, 2)
    holds, unit = unit_place(pair)
    barrier = pltpu.get_barrier_semaphore()
    units = pairs // 4 * 3
    extra = 1 if sibling else 0
    if sibling:
        pl.when(holds)(lambda: greet(me + 1 - 2 * core, cols))
    if to_units:

        @pl.when(holds)
        def _():
            loop(1, pairs, lambda s: greet(lax.rem(pair + s, pairs) * 2 + core, cols))
            pl.semaphore_wait(barrier, units - 1 + extra)

        pl.when(jnp.logical_not(holds))(lambda: pl.semaphore_wait(barrier, units))
    else:

        def to_unit(s):
            other = lax.rem(pair + s, pairs)
            pl.when(unit_place(other)[0])(lambda: greet(other * 2 + core, cols))

        loop(1, pairs, to_unit)
        pl.when(holds)(lambda: pl.semaphore_wait(barrier, pairs - 1 + extra))
    return me, core, pair, holds, unit


def to_units_kernel(cols, pairs, with_kv, *refs):
    if with_kv:
        source, q_out, kv_out, send, recv, own_sem, kv_send, kv_recv, fwd_send, fwd_recv = refs
    else:
        source, q_out, send, recv, own_sem = refs
    me, core, pair, holds, _ = greet_units(cols, pairs, with_kv, True)
    q_rows = pl.ds(0, HEAD_DIM)
    kv_rows = pl.ds(HEAD_DIM, 2 * HEAD_DIM)

    def far(s):
        other = lax.rem(pair + s, pairs)
        unit = unit_place(other)[1]
        target = other * 2 + core
        copies = [
            remote(
                source.at[unit, q_rows] if with_kv else source.at[unit],
                q_out.at[pair],
                send.at[s],
                recv.at[s],
                target,
                cols,
            )
        ]
        if with_kv:
            copies.append(
                remote(
                    source.at[unit, kv_rows],
                    kv_out.at[me],
                    kv_send.at[s],
                    kv_recv.at[s],
                    target,
                    cols,
                )
            )
        return copies

    def own():
        unit = unit_place(pair)[1]
        copies = [
            pltpu.make_async_copy(
                source.at[unit, q_rows] if with_kv else source.at[unit],
                q_out.at[pair],
                own_sem.at[0],
            )
        ]
        if with_kv:
            copies.append(
                pltpu.make_async_copy(source.at[unit, kv_rows], kv_out.at[me], own_sem.at[1])
            )
        return copies

    def forward(s):
        block = kv_out.at[lax.rem(pair - s + pairs, pairs) * 2 + core]
        return remote(block, block, fwd_send.at[s], fwd_recv.at[s], me + 1 - 2 * core, cols)

    def sends(s, action):
        def run():
            for copy in far(s):
                action(copy)

        pl.when(unit_place(lax.rem(pair + s, pairs))[0])(run)

    loop(1, pairs, lambda s: sends(s, lambda copy: copy.start()))

    @pl.when(holds)
    def _():
        for copy in own():
            copy.start()
        for copy in own():
            copy.wait()
        if with_kv:
            forward(0).start()

        def take(s):
            for copy in far(s):
                copy.wait_recv()
            if with_kv:
                forward(s).start()

        loop(1, pairs, take)
        if with_kv:
            loop(0, pairs, lambda s: forward(s).wait())

    loop(1, pairs, lambda s: sends(s, lambda copy: copy.wait_send()))


def to_units(blocks, cols, with_kv, collective_id):
    units, rows, width = blocks.shape
    pairs = units // 3 * 4
    out_shape = [jax.ShapeDtypeStruct((pairs, HEAD_DIM, width), blocks.dtype)]
    scratch = [
        pltpu.SemaphoreType.DMA((pairs,)),
        pltpu.SemaphoreType.DMA((pairs,)),
        pltpu.SemaphoreType.DMA((2,)),
    ]
    if with_kv:
        out_shape.append(jax.ShapeDtypeStruct((2 * pairs, 2 * HEAD_DIM, width), blocks.dtype))
        scratch += [pltpu.SemaphoreType.DMA((pairs,))] * 4
    return pl.pallas_call(
        functools.partial(to_units_kernel, cols, pairs, with_kv),
        out_shape=out_shape,
        in_specs=[pl.BlockSpec(memory_space=pl.ANY)],
        out_specs=[pl.BlockSpec(memory_space=pl.ANY)] * len(out_shape),
        scratch_shapes=scratch,
        compiler_params=pltpu.CompilerParams(collective_id=collective_id, has_side_effects=True),
    )(blocks)


def project_kernel(
    cols, x_ref, gain_ref, w_ref, cos_ref, sin_ref, normed_ref, scale_ref, q_out, kv_out,
    stage, q_send, q_recv, kv_send, kv_recv, fwd_send, fwd_recv, own_sem,
):
    me = flat_index(cols)
    core, pair = lax.rem(me, 2), lax.div(me, 2)
    holds, unit = unit_place(pair)
    sibling = me + 1 - 2 * core
    pairs, heads = q_out.shape[0], stage.shape[0]
    barrier = pltpu.get_barrier_semaphore()
    width = heads * HEAD_DIM

    @pl.when(holds)
    def _():
        loop(1, pairs, lambda s: greet(lax.rem(pair + s, pairs) * 2 + core, cols))
        greet(sibling, cols)

    rows = x_ref[...]
    scale = lax.rsqrt(jnp.mean(rows * rows, axis=-1, keepdims=True) + EPSILON)
    normed = (rows * scale * gain_ref[...]).astype(jnp.bfloat16)
    scale_ref[...] = scale
    normed_ref[...] = normed
    cosine, sine = cos_ref[...], sin_ref[...]
    half = HEAD_DIM // 2
    q_rows, kv_rows = pl.ds(0, HEAD_DIM), pl.ds(HEAD_DIM, 2 * HEAD_DIM)

    def q_far(u, holder):
        return remote(
            stage.at[u, q_rows], q_out.at[pair], q_send.at[u], q_recv.at[pair], holder * 2 + core,
            cols,
        )

    def kv_far(u, holder):
        return remote(
            stage.at[u, kv_rows], kv_out.at[me], kv_send.at[u], kv_recv.at[pair],
            holder * 2 + core, cols,
        )

    q_own = pltpu.make_async_copy(stage.at[unit, q_rows], q_out.at[pair], own_sem.at[0])
    kv_own = pltpu.make_async_copy(stage.at[unit, kv_rows], kv_out.at[me], own_sem.at[1])

    def forward(source):
        block = kv_out.at[source * 2 + core]
        return remote(block, block, fwd_send.at[source], fwd_recv.at[source], sibling, cols)

    per = TILE // HEAD_DIM
    for group in range(heads // per):
        for part in range(3):
            at = pl.ds(part * width + group * TILE, TILE)
            turned = dot(normed, w_ref[:, at], (1, 0)).T
            for k in range(per):
                head = group * per + k
                low = part * HEAD_DIM
                block = turned[k * HEAD_DIM : (k + 1) * HEAD_DIM]
                if part < 2:
                    first, second = block[:half], block[half:]
                    block = jnp.concatenate(
                        [first * cosine - second * sine, second * cosine + first * sine], axis=0
                    )
                stage[head, low : low + HEAD_DIM, :] = block.astype(jnp.bfloat16)
        if group == 0:
            pl.when(holds)(lambda: pl.semaphore_wait(barrier, heads))
            pl.when(jnp.logical_not(holds))(lambda: pl.semaphore_wait(barrier, heads))
        for k in range(per):
            u = group * per + k
            holder = u // 3 * 4 + u % 3

            @pl.when(pair != holder)
            def _(u=u, holder=holder):
                kv_far(u, holder).start()
                q_far(u, holder).start()

            @pl.when(pair == holder)
            def _():
                kv_own.start()
                q_own.start()

    @pl.when(holds)
    def _():
        kv_own.wait()
        forward(pair).start()

        def take(s):
            source = lax.rem(pair - s + pairs, pairs)
            arrival = remote(
                stage.at[unit, kv_rows], kv_out.at[source * 2 + core], kv_send.at[unit],
                kv_recv.at[source], source * 2 + core, cols,
            )
            arrival.wait_recv()
            forward(source).start()

        loop(1, pairs, take)

        def take_q(s):
            source = lax.rem(pair - s + pairs, pairs)
            remote(
                stage.at[unit, q_rows], q_out.at[source], q_send.at[unit], q_recv.at[source],
                source * 2 + core, cols,
            ).wait_recv()

        loop(1, pairs, take_q)
        loop(0, pairs, lambda source: forward(source).wait())
        q_own.wait()

    def sent(u, holder):
        kv_far(u, holder).wait_send()
        q_far(u, holder).wait_send()

    other_units(pairs, pair, sent)


def project(rows, gain, weights, cosine, sine, cols, collective_id):
    tokens, width = rows.shape
    heads = width // HEAD_DIM
    pairs = heads // 3 * 4
    by_pair, by_unit = pltpu.SemaphoreType.DMA((pairs,)), pltpu.SemaphoreType.DMA((heads,))
    vmem = pl.BlockSpec(memory_space=pltpu.VMEM)
    everywhere = pl.BlockSpec(memory_space=pl.ANY)
    return pl.pallas_call(
        functools.partial(project_kernel, cols),
        out_shape=[
            jax.ShapeDtypeStruct((tokens, width), jnp.bfloat16),
            jax.ShapeDtypeStruct((tokens, 1), jnp.float32),
            jax.ShapeDtypeStruct((pairs, HEAD_DIM, tokens), jnp.bfloat16),
            jax.ShapeDtypeStruct((2 * pairs, 2 * HEAD_DIM, tokens), jnp.bfloat16),
        ],
        in_specs=[vmem] * 5,
        out_specs=[vmem, vmem, everywhere, everywhere],
        scratch_shapes=[
            pltpu.VMEM((heads, 3 * HEAD_DIM, tokens), jnp.bfloat16),
            by_unit,
            by_pair,
            by_unit,
            by_pair,
            by_pair,
            by_pair,
            pltpu.SemaphoreType.DMA((2,)),
        ],
        compiler_params=pltpu.CompilerParams(
            collective_id=collective_id, has_side_effects=True, vmem_limit_bytes=40 * 2**20
        ),
    )(rows, gain.reshape(1, width), weights, cosine, sine)


def to_tokens_kernel(cols, pairs, with_kv, *refs):
    if with_kv:
        q_in, kv_in, q_out, kv_out, send, recv, own_sem = refs[:7]
        stage, inbox, kv_send, kv_recv, near_send, near_recv = refs[7:]
    else:
        q_in, q_out, send, recv, own_sem = refs
    me, core, pair, holds, unit = greet_units(cols, pairs, with_kv, False)

    def far(s):
        other = lax.rem(pair + s, pairs)
        target = other * 2 + core
        copies = [remote(q_in.at[other], q_out.at[unit], send.at[s], recv.at[s], target, cols)]
        if with_kv:
            copies.append(
                remote(
                    stage.at[other], kv_out.at[unit], kv_send.at[s], kv_recv.at[s], target, cols
                )
            )
        return copies

    def own():
        copies = [pltpu.make_async_copy(q_in.at[pair], q_out.at[unit], own_sem.at[0])]
        if with_kv:
            copies.append(pltpu.make_async_copy(stage.at[pair], kv_out.at[unit], own_sem.at[1]))
        return copies

    def near(s):
        other = lax.rem(pair + s, pairs)
        return remote(
            kv_in.at[other * 2 + 1 - core],
            inbox.at[other],
            near_send.at[s],
            near_recv.at[s],
            me + 1 - 2 * core,
            cols,
        )

    def add(s):
        other = lax.rem(pair + s, pairs)
        total = kv_in[other * 2 + core].astype(jnp.float32) + inbox[other].astype(jnp.float32)
        stage[other] = total.astype(stage.dtype)

    @pl.when(holds)
    def _():
        if with_kv:
            loop(1, pairs, lambda s: near(s).start())
            near(0).start()

        def give(s):
            if with_kv:
                near(s).wait_recv()
                add(s)
            for copy in far(s):
                copy.start()

        loop(1, pairs, give)
        if with_kv:
            near(0).wait_recv()
            add(0)
        for copy in own():
            copy.start()
        for copy in own():
            copy.wait()

    def take(s):
        def run():
            for copy in far(s):
                copy.wait_recv()

        pl.when(unit_place(lax.rem(pair - s + pairs, pairs))[0])(run)

    loop(1, pairs, take)

    @pl.when(holds)
    def _():
        def sent(s):
            for copy in far(s):
                copy.wait_send()

        loop(1, pairs, sent)
        if with_kv:
            loop(0, pairs, lambda s: near(s).wait_send())


def to_tokens(arrays, cols, collective_id):
    with_kv = len(arrays) == 2
    pairs, _, width = arrays[0].shape
    units = pairs // 4 * 3
    out_shape = [jax.ShapeDtypeStruct((units, HEAD_DIM, width), arrays[0].dtype)]
    in_specs = [pl.BlockSpec(memory_space=pl.ANY)]
    scratch = [
        pltpu.SemaphoreType.DMA((pairs,)),
        pltpu.SemaphoreType.DMA((pairs,)),
        pltpu.SemaphoreType.DMA((2,)),
    ]
    if with_kv:
        out_shape.append(jax.ShapeDtypeStruct((units, 2 * HEAD_DIM, width), arrays[1].dtype))
        in_specs.append(pl.BlockSpec(memory_space=pltpu.VMEM))
        scratch += [pltpu.VMEM((pairs, 2 * HEAD_DIM, width), arrays[1].dtype)] * 2
        scratch += [pltpu.SemaphoreType.DMA((pairs,))] * 4
    return pl.pallas_call(
        functools.partial(to_tokens_kernel, cols, pairs, with_kv),
        out_shape=out_shape,
        in_specs=in_specs,
        out_specs=[pl.BlockSpec(memory_space=pl.ANY)] * len(out_shape),
        scratch_shapes=scratch,
        compiler_params=pltpu.CompilerParams(
            collective_id=collective_id, has_side_effects=True, vmem_limit_bytes=48 * 2**20
        ),
    )(*arrays)


def wide_of(first, blocks):
    return pl.ds(pl.multiple_of(first * TILE, TILE), blocks * TILE)


def in_reach(first, shape, place, run):
    key_pos = first * TILE + lax.broadcasted_iota(jnp.int32, shape, 0)
    return (key_pos <= place) & (key_pos >= run)


def tile_reach(tile, core, width, wide, masked, blocks):
    joined = TILE // width
    low = (2 * tile * joined + core) * width
    high = low + (2 * joined - 1) * width - 1
    prompt = low < PROMPT
    full = jnp.where(prompt, low // (TILE * wide), PROMPT // (TILE * wide))
    back = jnp.maximum((low - LONGEST + 1) // TILE, PROMPT // TILE)
    first = jnp.where(prompt, full * wide, back)
    steps = (high // TILE + masked - first) // masked
    first = jnp.minimum(first, blocks - steps * masked)
    lane = lax.broadcasted_iota(jnp.int32, (1, TILE), 1)
    place = low + lane + lane // width * width
    return full, first, steps, place


CHUNK = 64


def fill_rows(kv_ref, first_row, rows):
    def fill(b):
        rows[wide_of(b, 1), :] = kv_ref[b, first_row : first_row + HEAD_DIM, :].T

    loop(0, kv_ref.shape[0], fill)


def forward_tile(tile, core, width, queries, run, kv_ref, key_rows, kept):
    full, start, steps, place = tile_reach(
        tile, core, width, FWD_WIDE, FWD_MASK, kv_ref.shape[0]
    )

    def by_eight(value):
        return value.reshape(-1, 8, TILE)

    def fold(blocks, first, state, masked):
        top, total, gathered = state
        base = pl.multiple_of(first * TILE, TILE)
        highest = top
        for c in range(blocks * TILE // CHUNK):
            scores = jnp.dot(
                key_rows[pl.ds(base + c * CHUNK, CHUNK), :],
                queries,
                preferred_element_type=jnp.float32,
            )
            if masked:
                key_pos = base + c * CHUNK + lax.broadcasted_iota(jnp.int32, scores.shape, 0)
                scores = jnp.where((key_pos <= place) & (key_pos >= run), scores, NEGATIVE)
            kept[c * CHUNK : (c + 1) * CHUNK, :] = scores
            highest = jnp.maximum(highest, jnp.max(by_eight(scores), axis=0))
        new_top = jnp.broadcast_to(jnp.max(highest, axis=0, keepdims=True), (8, TILE))
        shrink = jnp.exp2((top - new_top) * EXP_SCALE)
        total = total * shrink
        gathered = (by_eight(gathered) * shrink[None]).reshape(HEAD_DIM, TILE)
        for j in range(blocks):
            low = []
            for c in range(j * TILE // CHUNK, (j + 1) * TILE // CHUNK):
                scores = by_eight(kept[c * CHUNK : (c + 1) * CHUNK, :])
                weights = jnp.exp2((scores - new_top[None]) * EXP_SCALE)
                total = total + jnp.sum(weights, axis=0)
                low.append(weights.reshape(CHUNK, TILE).astype(jnp.bfloat16))
            gathered = gathered + jnp.dot(
                kv_ref[first + j, HEAD_DIM : 2 * HEAD_DIM, :],
                jnp.concatenate(low, axis=0),
                preferred_element_type=jnp.float32,
            )
        return (new_top, total, gathered)

    state = (
        jnp.full((8, TILE), NEGATIVE, jnp.float32),
        jnp.zeros((8, TILE), jnp.float32),
        jnp.zeros((HEAD_DIM, TILE), jnp.float32),
    )
    state = lax.fori_loop(0, full, lambda b, s: fold(FWD_WIDE, b * FWD_WIDE, s, False), state)
    top, total, gathered = lax.fori_loop(
        0, steps, lambda b, s: fold(FWD_MASK, start + b * FWD_MASK, s, True), state
    )
    total = jnp.sum(total, axis=0, keepdims=True)
    exact = gathered / total
    return exact, exact.astype(jnp.bfloat16), top[0:1] * EXP_SCALE + jnp.log2(total)


def forward_scratch(blocks):
    return [
        pltpu.VMEM((blocks * TILE, HEAD_DIM), jnp.bfloat16),
        pltpu.VMEM((max(FWD_WIDE, FWD_MASK) * TILE, TILE), jnp.float32),
    ]


def my_unit():
    me = flat_index(lax.axis_size("blk"))
    pair = lax.div(me, 2)
    holds, unit = unit_place(pair)
    return me, lax.rem(me, 2), pair, holds, unit


def forward_kernel(width, q_ref, kv_ref, run_ref, o_ref, ob_ref, lse_ref, key_rows, kept):
    tile = pl.program_id(0)
    _, core, _, holds, _ = my_unit()

    @pl.when(holds & (tile == 0))
    def _():
        fill_rows(kv_ref, 0, key_rows)

    @pl.when(holds)
    def _():
        o_ref[0], ob_ref[0], lse_ref[0] = forward_tile(
            tile, core, width, q_ref[0], run_ref[0], kv_ref, key_rows, kept
        )


def tile_spec(rows):
    return pl.BlockSpec((1, rows, TILE), lambda i: (i, 0, 0))


def attend(queries, keys_values, run, width):
    tiles = queries.shape[0]
    held = pl.BlockSpec(keys_values.shape, lambda i: (0, 0, 0))
    return pl.pallas_call(
        functools.partial(forward_kernel, width),
        grid=(tiles,),
        in_specs=[tile_spec(HEAD_DIM), held, tile_spec(1)],
        out_specs=[tile_spec(HEAD_DIM), tile_spec(HEAD_DIM), tile_spec(1)],
        scratch_shapes=forward_scratch(keys_values.shape[0]),
        out_shape=[
            jax.ShapeDtypeStruct((tiles, HEAD_DIM, TILE), jnp.float32),
            jax.ShapeDtypeStruct((tiles, HEAD_DIM, TILE), jnp.bfloat16),
            jax.ShapeDtypeStruct((tiles, 1, TILE), jnp.float32),
        ],
        compiler_params=pltpu.CompilerParams(vmem_limit_bytes=48 * 2**20),
    )(queries, keys_values, run)


def other_units(pairs, pair, action):
    def one(u):
        holder = lax.div(u, 3) * 4 + lax.rem(u, 3)
        pl.when(holder != pair)(lambda: action(u, holder))

    loop(0, pairs // 4 * 3, one)


def gathers_of(sources, results, sems, depths):
    return [
        Gather(
            source,
            results[i],
            sems[GATHER_SEMS * i : GATHER_SEMS * (i + 1)],
            depths,
            cut_of(source.shape[-1]),
        )
        for i, source in enumerate(sources)
    ]


GATHER_AT = {"start": 0, "start_own": 0, "spread_near": 8, "spread_far": 11, "settle": 14}


def forward_home_kernel(cols, count, *refs):
    q_ref, kv_ref, run_ref = refs[:3]
    sources, refs = refs[3 : 3 + count], refs[3 + count :]
    o_ref, lse_ref, home = refs[:3]
    results, refs = refs[3 : 3 + count], refs[3 + count :]
    key_rows, kept, low, send, recv, own_sem = refs[:6]
    gathers = gathers_of(sources, results, refs[6:], cols // 4)
    tile, tiles = pl.program_id(0), tiles_of(kv_ref)
    me, core, pair, holds, unit = my_unit()

    @pl.when(tile == 0)
    def _():
        loop(1, tiles, lambda s: greet(lax.rem(pair + s, tiles) * 2 + core, cols))
        greet(me + 1 - 2 * core, cols)

    @pl.when(holds & (tile == 0))
    def _():
        fill_rows(kv_ref, 0, key_rows)

    @pl.when(tile == 0)
    def _():
        pl.semaphore_wait(pltpu.get_barrier_semaphore(), tiles)

    for name, place_at in GATHER_AT.items():

        @pl.when(tile == place_at)
        def _(name=name):
            for gather in gathers:
                getattr(gather, name)()

    def away(t):
        return remote(
            low.at[t], home.at[unit], send.at[t], recv.at[unit], t * 2 + core, cols
        )

    stays = pltpu.make_async_copy(low.at[pair], home.at[unit], own_sem)

    @pl.when(holds)
    def _():
        o_ref[0], low[tile], lse_ref[0] = forward_tile(
            tile, core, TILE, q_ref[0], run_ref[0], kv_ref, key_rows, kept
        )
        pl.when(tile != pair)(lambda: away(tile).start())
        pl.when(tile == pair)(lambda: stays.start())

    @pl.when(tile == tiles - 1)
    def _():
        for gather in gathers:
            gather.finish()

        def arrived(u, holder):
            remote(
                low.at[pair], home.at[u], send.at[pair], recv.at[u], holder * 2 + core, cols
            ).wait_recv()

        other_units(tiles, pair, arrived)

        @pl.when(holds)
        def _():
            def sent(t):
                pl.when(t != pair)(lambda: away(t).wait_send())

            loop(0, tiles, sent)
            stays.wait()


def tiles_of(kv_ref):
    return kv_ref.shape[0] // 2


def attend_home(queries, keys_values, run, shards, cols, collective_id):
    tiles, units, depths = queries.shape[0], queries.shape[0] // 4 * 3, cols // 4
    held = pl.BlockSpec(keys_values.shape, lambda i: (0, 0, 0))
    everywhere = pl.BlockSpec(memory_space=pl.ANY)
    return pl.pallas_call(
        functools.partial(forward_home_kernel, cols, len(shards)),
        grid=(tiles,),
        in_specs=[tile_spec(HEAD_DIM), held, tile_spec(1)] + [everywhere] * len(shards),
        out_specs=[tile_spec(HEAD_DIM), tile_spec(1), everywhere] + [everywhere] * len(shards),
        scratch_shapes=forward_scratch(keys_values.shape[0])
        + [
            pltpu.VMEM((tiles, HEAD_DIM, TILE), jnp.bfloat16),
            pltpu.SemaphoreType.DMA((tiles,)),
            pltpu.SemaphoreType.DMA((units,)),
            pltpu.SemaphoreType.DMA,
        ]
        + gather_sems(depths) * len(shards),
        out_shape=[
            jax.ShapeDtypeStruct((tiles, HEAD_DIM, TILE), jnp.float32),
            jax.ShapeDtypeStruct((tiles, 1, TILE), jnp.float32),
            jax.ShapeDtypeStruct((units, HEAD_DIM, TILE), jnp.bfloat16),
        ]
        + [gathered_shape(shard, depths) for shard in shards],
        compiler_params=pltpu.CompilerParams(
            collective_id=collective_id, has_side_effects=True, vmem_limit_bytes=48 * 2**20
        ),
    )(queries, keys_values, run, *shards)


def backward_tile(
    tile, core, width, queries, grads, exact, lse, run,
    kv_ref, key_rows, value_rows, dk_sum, dv_sum,
):
    full, start, steps, place = tile_reach(
        tile, core, width, BWD_WIDE, BWD_MASK, kv_ref.shape[0]
    )
    delta = jnp.sum(grads.astype(jnp.float32) * exact, axis=0, keepdims=True)
    over_queries = (((1,), (1,)), ((), ()))

    def fold(blocks, first, dq, masked):
        rows = wide_of(first, blocks)
        scores = jnp.dot(key_rows[rows, :], queries, preferred_element_type=jnp.float32)
        probs = jnp.exp2(scores * EXP_SCALE - lse)
        if masked:
            probs = jnp.where(in_reach(first, scores.shape, place, run), probs, 0.0)
        dp = jnp.dot(value_rows[rows, :], grads, preferred_element_type=jnp.float32)
        ds = (probs * (dp - delta)).astype(jnp.bfloat16)
        low = probs.astype(jnp.bfloat16)
        for j in range(blocks):
            part = slice(j * TILE, (j + 1) * TILE)
            dv_sum[first + j] += lax.dot_general(
                grads, low[part], over_queries, preferred_element_type=jnp.float32
            )
            dk_sum[first + j] += lax.dot_general(
                queries, ds[part], over_queries, preferred_element_type=jnp.float32
            )
            dq = dq + jnp.dot(
                kv_ref[first + j, 0:HEAD_DIM, :], ds[part], preferred_element_type=jnp.float32
            )
        return dq

    dq = jnp.zeros((HEAD_DIM, TILE), jnp.float32)
    dq = lax.fori_loop(0, full, lambda b, s: fold(BWD_WIDE, b * BWD_WIDE, s, False), dq)
    dq = lax.fori_loop(0, steps, lambda b, s: fold(BWD_MASK, start + b * BWD_MASK, s, True), dq)
    return (dq * SCORE_SCALE).astype(jnp.bfloat16)


def backward_begin(kv_ref, key_rows, value_rows, dk_sum, dv_sum):
    fill_rows(kv_ref, 0, key_rows)
    fill_rows(kv_ref, HEAD_DIM, value_rows)

    def clear(b):
        dk_sum[b] = jnp.zeros((HEAD_DIM, TILE), jnp.float32)
        dv_sum[b] = jnp.zeros((HEAD_DIM, TILE), jnp.float32)

    loop(0, kv_ref.shape[0], clear)


def backward_end(dk_sum, dv_sum, dkv, first, last):
    def drain(b):
        dkv[b, 0:HEAD_DIM, :] = (dk_sum[b] * SCORE_SCALE).astype(jnp.bfloat16)
        dkv[b, HEAD_DIM : 2 * HEAD_DIM, :] = dv_sum[b].astype(jnp.bfloat16)

    loop(first, last, drain)


def backward_scratch(blocks):
    return [pltpu.VMEM((blocks * TILE, HEAD_DIM), jnp.bfloat16)] * 2 + [
        pltpu.VMEM((blocks, HEAD_DIM, TILE), jnp.float32)
    ] * 2


NEAR_AT, MIDDLE_AT, FAR_AT = (0, 2, 4, 6), (2, 4, 6, 8), (3, 5, 7, 9)


def reduce_at(step, reduces, depths):
    quarter = depths // 4
    for name, places in (("far", FAR_AT), ("middle", MIDDLE_AT), ("near", NEAR_AT)):
        for part, place_at in enumerate(places):

            @pl.when(step == place_at)
            def _(name=name, part=part):
                for reduce in reduces:
                    getattr(reduce, name)(part * quarter, (part + 1) * quarter)


def backward_kernel(width, depths, count, *refs):
    q_ref, kv_ref, do_ref, o_ref, lse_ref, run_ref = refs[:6]
    parts, refs = refs[6 : 6 + count], refs[6 + count :]
    dq_ref, dkv_ref = refs[:2]
    totals, refs = refs[2 : 2 + count], refs[2 + count :]
    held = refs[:4]
    reduces = reduces_of(parts, totals, refs[4:], depths)
    tile, tiles = pl.program_id(0), pl.num_programs(0)
    _, core, _, holds, _ = my_unit()

    @pl.when(tile == 0)
    def _():
        greet_mesh(depths)
        for reduce in reduces:
            reduce.start()

    reduce_at(tile, reduces, depths)

    @pl.when(holds & (tile == 0))
    def _():
        backward_begin(kv_ref, *held)

    @pl.when(holds)
    def _():
        dq_ref[0] = backward_tile(
            tile, core, width, q_ref[0], do_ref[0], o_ref[0], lse_ref[0], run_ref[0],
            kv_ref, *held,
        )

    @pl.when(holds & (tile == tiles - 1))
    def _():
        backward_end(held[2], held[3], dkv_ref, 0, dkv_ref.shape[0])

    @pl.when(tile == tiles - 1)
    def _():
        for reduce in reduces:
            reduce.finish()


def attend_back(queries, keys_values, grads, exact, lse, run, width, parts, cols, collective_id):
    tiles, blocks = queries.shape[0], keys_values.shape[0]
    held = pl.BlockSpec(keys_values.shape, lambda i: (0, 0, 0))
    wide, flat = tile_spec(HEAD_DIM), tile_spec(1)
    depths = cols // 4
    return pl.pallas_call(
        functools.partial(backward_kernel, width, depths, len(parts)),
        grid=(tiles,),
        in_specs=[wide, held, wide, wide, flat, flat]
        + [pl.BlockSpec(memory_space=pl.ANY)] * len(parts),
        out_specs=[wide, held]
        + [pl.BlockSpec(part.shape[-2:], lambda i: (0, 0)) for part in parts],
        scratch_shapes=backward_scratch(blocks) + all_reduce_scratch(parts, depths),
        out_shape=[
            jax.ShapeDtypeStruct(queries.shape, jnp.bfloat16),
            jax.ShapeDtypeStruct(keys_values.shape, jnp.bfloat16),
        ]
        + [jax.ShapeDtypeStruct(part.shape[-2:], jnp.float32) for part in parts],
        compiler_params=pltpu.CompilerParams(
            collective_id=collective_id, has_side_effects=True, vmem_limit_bytes=52 * 2**20
        ),
    )(queries, keys_values, grads, exact, lse, run, *parts)


def backward_home_kernel(cols, depths, count, *refs):
    q_ref, kv_ref, o_ref, lse_ref, run_ref, do_source = refs[:6]
    parts, refs = refs[6 : 6 + count], refs[6 + count :]
    q_home, kv_home = refs[:2]
    totals, refs = refs[2 : 2 + count], refs[2 + count :]
    held, refs = refs[:4], refs[4:]
    grads, low, dkv, inbox, refs = refs[0], refs[1], refs[2], refs[3], refs[4:]
    in_send, in_recv, q_send, q_recv, kv_send, kv_recv, near_send, near_recv, own_sem = refs[:9]
    reduces = reduces_of(parts, totals, refs[9:], depths)
    step, pairs = pl.program_id(0), tiles_of(kv_ref)
    tile = pairs - 1 - step
    me, core, pair, holds, unit = my_unit()
    sibling = me + 1 - 2 * core
    last = tile == 0

    def do_out(u, holder):
        return remote(
            do_source.at[u], grads.at[pair], in_send.at[u], in_recv.at[pair], holder * 2 + core, cols
        )

    def do_in(t):
        return remote(
            do_source.at[unit], grads.at[t], in_send.at[unit], in_recv.at[t], t * 2 + core, cols
        )

    def q_away(t):
        return remote(low.at[t], q_home.at[unit], q_send.at[t], q_recv.at[unit], t * 2 + core, cols)

    def kv_away(t):
        return remote(
            inbox.at[t], kv_home.at[unit], kv_send.at[t], kv_recv.at[unit], t * 2 + core, cols
        )

    def near(t):
        return remote(
            dkv.at[t * 2 + 1 - core], inbox.at[t], near_send.at[t], near_recv.at[t], sibling, cols
        )

    do_own = pltpu.make_async_copy(do_source.at[unit], grads.at[pair], own_sem.at[0])
    q_stays = pltpu.make_async_copy(low.at[pair], q_home.at[unit], own_sem.at[1])
    kv_stays = pltpu.make_async_copy(inbox.at[pair], kv_home.at[unit], own_sem.at[2])

    def give(t):
        near(t).wait_recv()
        inbox[t] = dkv[t * 2 + core] + inbox[t]
        pl.when(t != pair)(lambda: kv_away(t).start())
        pl.when(t == pair)(lambda: kv_stays.start())

    @pl.when(step == 0)
    def _():
        loop(1, pairs, lambda s: greet(lax.rem(pair + s, pairs) * 2 + core, cols))
        greet(sibling, cols)
        pl.semaphore_wait(pltpu.get_barrier_semaphore(), pairs)
        other_units(pairs, pair, lambda u, holder: do_out(u, holder).start())
        pl.when(holds)(lambda: do_own.start())
        for reduce in reduces:
            reduce.start()

    @pl.when(holds & (step == 0))
    def _():
        backward_begin(kv_ref, *held)

    reduce_at(step, reduces, depths)

    @pl.when(holds)
    def _():
        pl.when(tile != pair)(lambda: do_in(tile).wait_recv())
        pl.when(tile == pair)(lambda: do_own.wait())
        low[tile] = backward_tile(
            tile, core, TILE, q_ref[0], grads[tile], o_ref[0], lse_ref[0], run_ref[0],
            kv_ref, *held,
        )
        pl.when(tile != pair)(lambda: q_away(tile).start())
        pl.when(tile == pair)(lambda: q_stays.start())
        backward_end(held[2], held[3], dkv, 2 * tile, 2 * tile + 2)
        near(tile).start()
        pl.when(step > 0)(lambda: give(tile + 1))
        pl.when(last)(lambda: give(tile))

    @pl.when(last)
    def _():
        for reduce in reduces:
            reduce.finish()

        def arrived(u, holder):
            target = holder * 2 + core
            remote(
                low.at[pair], q_home.at[u], q_send.at[pair], q_recv.at[u], target, cols
            ).wait_recv()
            remote(
                inbox.at[pair], kv_home.at[u], kv_send.at[pair], kv_recv.at[u], target, cols
            ).wait_recv()

        other_units(pairs, pair, arrived)
        other_units(pairs, pair, lambda u, holder: do_out(u, holder).wait_send())

        @pl.when(holds)
        def _():
            def sent(t):
                near(t).wait_send()

                @pl.when(t != pair)
                def _():
                    q_away(t).wait_send()
                    kv_away(t).wait_send()

            loop(0, pairs, sent)
            q_stays.wait()
            kv_stays.wait()


def attend_back_home(queries, keys_values, do_blocks, exact, lse, run, parts, cols, collective_id):
    tiles, blocks = queries.shape[0], keys_values.shape[0]
    units, depths = do_blocks.shape[0], cols // 4
    held = pl.BlockSpec(keys_values.shape, lambda i: (0, 0, 0))
    wide = pl.BlockSpec((1, HEAD_DIM, TILE), lambda i: (tiles - 1 - i, 0, 0))
    flat = pl.BlockSpec((1, 1, TILE), lambda i: (tiles - 1 - i, 0, 0))
    everywhere = pl.BlockSpec(memory_space=pl.ANY)
    by_tile, by_unit = pltpu.SemaphoreType.DMA((tiles,)), pltpu.SemaphoreType.DMA((units,))
    tile_rows = pltpu.VMEM((tiles, HEAD_DIM, TILE), jnp.bfloat16)
    return pl.pallas_call(
        functools.partial(backward_home_kernel, cols, depths, len(parts)),
        grid=(tiles,),
        in_specs=[wide, held, wide, flat, flat, everywhere] + [everywhere] * len(parts),
        out_specs=[everywhere, everywhere]
        + [pl.BlockSpec(part.shape[-2:], lambda i: (0, 0)) for part in parts],
        scratch_shapes=backward_scratch(blocks)
        + [
            tile_rows,
            tile_rows,
            pltpu.VMEM((blocks, 2 * HEAD_DIM, TILE), jnp.bfloat16),
            pltpu.VMEM((tiles, 2 * HEAD_DIM, TILE), jnp.bfloat16),
            by_unit,
            by_tile,
            by_tile,
            by_unit,
            by_tile,
            by_unit,
            by_tile,
            by_tile,
            pltpu.SemaphoreType.DMA((3,)),
        ]
        + all_reduce_scratch(parts, depths),
        out_shape=[
            jax.ShapeDtypeStruct((units, HEAD_DIM, TILE), jnp.bfloat16),
            jax.ShapeDtypeStruct((units, 2 * HEAD_DIM, TILE), jnp.bfloat16),
        ]
        + [jax.ShapeDtypeStruct(part.shape[-2:], jnp.float32) for part in parts],
        compiler_params=pltpu.CompilerParams(
            collective_id=collective_id, has_side_effects=True, vmem_limit_bytes=52 * 2**20
        ),
    )(queries, keys_values, exact, lse, run, do_blocks, *parts)


def to_tiles(blocks):
    count, rows, width = blocks.shape
    if width == TILE:
        return blocks
    joined = TILE // width
    return (
        blocks.reshape(count // joined, joined, rows, width)
        .transpose(0, 2, 1, 3)
        .reshape(count // joined, rows, TILE)
    )


def from_tiles(tiles, width):
    count, rows, _ = tiles.shape
    if width == TILE:
        return tiles
    joined = TILE // width
    return (
        tiles.reshape(count, rows, joined, width)
        .transpose(0, 2, 1, 3)
        .reshape(count * joined, rows, width)
    )


def dot(left, right, over):
    return lax.dot_general(
        left, right, (((over[0],), (over[1],)), ((), ())), preferred_element_type=jnp.float32
    )


STRIP = 512


def strips(total, body):
    width = min(total, STRIP)
    loop(0, total // width, lambda j: body(pl.ds(pl.multiple_of(j * width, width), width)))


def shared_forward(ins, outs, done):
    normed, wide, down = ins
    gate_in, up_in, hidden_low, total = outs
    hidden = down.shape[0]

    def strip(at):
        after = pl.ds(at.start + hidden, at.size)
        gate = dot(normed[...], wide[:, at], (1, 0))
        up = dot(normed[...], wide[:, after], (1, 0))
        gate_in[:, at] = gate.astype(jnp.bfloat16)
        up_in[:, at] = up.astype(jnp.bfloat16)
        hidden_low[:, at] = (apply_silu(gate) * up).astype(jnp.bfloat16)

    strips(hidden, strip)
    for start in done[:3]:
        start()
    total[...] = dot(hidden_low[...], down[...], (1, 0))
    done[3]()


def shared_backward(ins, outs, done):
    grads, normed, gate_in, up_in, hidden_low, wide, down = ins
    grad_wide, grad_down, back = outs
    hidden = down.shape[0]
    normed_t = normed[...].T
    back[...] = jnp.zeros_like(back)

    def strip(at):
        after = pl.ds(at.start + hidden, at.size)
        upstream = dot(grads[...], down[at, :], (1, 1))
        gate, up = gate_in[:, at].astype(jnp.float32), up_in[:, at].astype(jnp.float32)
        low_gate = (upstream * up * silu_slope(gate)).astype(jnp.bfloat16)
        low_up = (upstream * apply_silu(gate)).astype(jnp.bfloat16)
        back[...] += dot(low_gate, wide[:, at], (1, 1)) + dot(low_up, wide[:, after], (1, 1))
        grad_wide[:, at] = dot(normed_t, low_gate, (1, 0)).astype(jnp.bfloat16)
        grad_wide[:, after] = dot(normed_t, low_up, (1, 0)).astype(jnp.bfloat16)
        grad_down[at, :] = dot(hidden_low[:, at].T, grads[...], (1, 0)).astype(jnp.bfloat16)

    strips(hidden, strip)
    for start in done:
        start()


QUARTERS = 4


def quarter_order(pair, per):
    own = lax.div(pair, per)
    outer, inner = lax.div(own, 2), lax.rem(own, 2)
    return [own, (1 - outer) * 2 + inner, outer * 2 + 1 - inner, (1 - outer) * 2 + 1 - inner]


def expert_kernel(cols, step, final, work_first, work, shapes, *refs):
    held_in, held_out, extra = shapes
    sending, refs = refs[0], refs[1:]
    inputs, refs = refs[:held_in], refs[held_in:]
    extra_in = len(work.arrays)
    work_in, refs = refs[:extra_in], refs[extra_in:]
    returned, refs = refs[0], refs[1:]
    outputs, refs = refs[:held_out], refs[held_out:]
    work_out, refs = refs[: len(work.out_shape)], refs[len(work.out_shape) :]
    land, partial, inbox, refs = refs[0], refs[1], refs[2], refs[3:]
    send, recv, share_send, share_recv, near_send, near_recv, refs = refs[:6] + (refs[6:],)
    back_send, back_recv, own_sem, load_sem, refs = refs[:4] + (refs[4:],)
    held, refs = refs[:held_in], refs[held_in:]
    scratch, refs = refs[:extra], refs[extra:]
    begin, run, end = work.bind(work_in + work_out + refs)

    me = flat_index(cols)
    core, pair = lax.rem(me, 2), lax.div(me, 2)
    pairs = sending.shape[0]
    per = pairs // QUARTERS
    sibling = me + 1 - 2 * core
    order = quarter_order(pair, per)

    loads = [pltpu.make_async_copy(inputs[i], held[i], load_sem.at[i]) for i in range(held_in)]
    for copy in loads:
        copy.start()
    begin()

    loop(1, pairs, lambda s: greet(lax.rem(pair + s, pairs) * 2 + core, cols))
    greet(sibling, cols)
    pl.semaphore_wait(pltpu.get_barrier_semaphore(), pairs)

    def out(e):
        return remote(
            sending.at[e], land.at[pair, core], send.at[e], recv.at[pair], e * 2 + core, cols
        )

    def arrival(e):
        return remote(
            sending.at[e], land.at[e, core], send.at[e], recv.at[e], e * 2 + core, cols
        )

    def share(e):
        block = land.at[e, core]
        return remote(block, block, share_send.at[e], share_recv.at[e], sibling, cols)

    def near(quarter):
        rows = pl.ds(quarter * per, per)
        return remote(
            partial.at[rows, 1 - core],
            inbox.at[rows],
            near_send.at[quarter],
            near_recv.at[quarter],
            sibling,
            cols,
        )

    def back(e):
        return remote(
            inbox.at[e], returned.at[pair], back_send.at[e], back_recv.at[pair], e * 2 + core, cols
        )

    def back_arrival(e):
        return remote(
            inbox.at[e], returned.at[e], back_send.at[e], back_recv.at[e], e * 2 + core, cols
        )

    def others(quarter, action):
        def one(k):
            e = quarter * per + k
            pl.when(e != pair)(lambda: action(e))

        loop(0, per, one)

    own_in = pltpu.make_async_copy(sending.at[pair], land.at[pair, core], own_sem.at[0])
    own_back = pltpu.make_async_copy(inbox.at[pair], returned.at[pair], own_sem.at[1])

    for quarter in (order[2], order[0], order[1], order[3]):
        others(quarter, lambda e: out(e).start())
    own_in.start()
    own_in.wait()
    share(pair).start()
    if work_first:
        run()
    for copy in loads:
        copy.wait()

    def take(quarter):
        def one(e):
            arrival(e).wait_recv()
            share(e).start()

        others(quarter, one)
        loop(0, per, lambda k: share(quarter * per + k).wait_recv())
        step(quarter, per, land, partial, held, scratch)
        near(quarter).start()

    def give(quarter):
        near(quarter).wait_recv()

        def one(k):
            e = quarter * per + k
            inbox[e] = partial[e, core] + inbox[e]
            pl.when(e != pair)(lambda: back(e).start())

        loop(0, per, one)

    take(order[0])
    take(order[1])
    give(order[0])
    give(order[1])
    own_back.start()
    take(order[2])
    give(order[2])
    take(order[3])
    give(order[3])
    if not work_first:
        run()
    final(land, held, scratch, outputs)
    for quarter in order:
        others(quarter, lambda e: out(e).wait_send())
        others(quarter, lambda e: back(e).wait_send())
        others(quarter, lambda e: back_arrival(e).wait_recv())
        loop(0, per, lambda k: share(quarter * per + k).wait_send())
        near(quarter).wait_send()
    own_back.wait()
    end()


def expert_pass(sending, held, out_shape, extra, step, final, work, work_first, cols, collective_id):
    pairs, slots, width = sending.shape
    block = (pairs, slots, width)
    both = (pairs, 2, slots, width)
    sems = pltpu.SemaphoreType.DMA((pairs,))
    scratch = [
        pltpu.VMEM(both, sending.dtype),
        pltpu.VMEM(both, sending.dtype),
        pltpu.VMEM(block, sending.dtype),
    ]
    scratch += [sems] * 8 + [pltpu.SemaphoreType.DMA((2,)), pltpu.SemaphoreType.DMA((len(held),))]
    scratch += [pltpu.VMEM(a.shape, a.dtype) for a in held] + extra + work.scratch()
    out_shape = [jax.ShapeDtypeStruct(block, sending.dtype)] + out_shape
    shapes = (len(held), len(out_shape) - 1, len(extra))
    everywhere = pl.BlockSpec(memory_space=pl.ANY)
    return pl.pallas_call(
        functools.partial(expert_kernel, cols, step, final, work_first, work, shapes),
        out_shape=out_shape + work.out_shape,
        in_specs=[everywhere] * (1 + len(held) + len(work.arrays)),
        out_specs=[everywhere] * (len(out_shape) + len(work.out_shape)),
        scratch_shapes=scratch,
        compiler_params=pltpu.CompilerParams(
            collective_id=collective_id, has_side_effects=True, vmem_limit_bytes=52 * 2**20
        ),
    )(sending, *held, *work.arrays)


def forward_step(quarter, per, land, partial, held, scratch):
    gate, up, down = held
    gate_kept, up_kept, hidden_kept = scratch[:3]
    rows = land[pl.ds(quarter * per, per)].reshape(-1, land.shape[-1])

    def strip(at):
        inner_gate = dot(rows, gate[:, at], (1, 0))
        inner_up = dot(rows, up[:, at], (1, 0))
        gate_kept[quarter, :, at] = inner_gate.astype(jnp.bfloat16)
        up_kept[quarter, :, at] = inner_up.astype(jnp.bfloat16)
        hidden_kept[quarter, :, at] = (apply_silu(inner_gate) * inner_up).astype(jnp.bfloat16)

    strips(gate.shape[1], strip)
    total = dot(hidden_kept[quarter], down[...], (1, 0)).astype(jnp.bfloat16)
    partial[pl.ds(quarter * per, per)] = total.reshape((per,) + partial.shape[1:])


def forward_final(land, held, scratch, outputs):
    sems = scratch[3]
    copies = [
        pltpu.make_async_copy(source, outputs[i], sems.at[i])
        for i, source in enumerate((land,) + tuple(scratch[:3]))
    ]
    for copy in copies:
        copy.start()
    for copy in copies:
        copy.wait()


def expert_forward(sending, gate, up, down, work, cols, collective_id):
    pairs, slots, width = sending.shape
    kept = (QUARTERS, 2 * pairs * slots // QUARTERS, gate.shape[1])
    out_shape = [jax.ShapeDtypeStruct((pairs, 2, slots, width), sending.dtype)]
    out_shape += [jax.ShapeDtypeStruct(kept, sending.dtype)] * 3
    extra = [pltpu.VMEM(kept, sending.dtype)] * 3 + [pltpu.SemaphoreType.DMA((4,))]
    return expert_pass(
        sending, [gate, up, down], out_shape, extra, forward_step, forward_final, work, False,
        cols, collective_id,
    )


def backward_step(quarter, per, land, partial, held, scratch):
    gate, up, down, _, gate_kept, up_kept, _ = held
    grads = land[pl.ds(quarter * per, per)].reshape(-1, land.shape[-1])

    def strip(at):
        upstream = dot(grads, down[at, :], (1, 1))
        inner_gate = gate_kept[quarter, :, at].astype(jnp.float32)
        inner_up = up_kept[quarter, :, at].astype(jnp.float32)
        gate_kept[quarter, :, at] = (upstream * inner_up * silu_slope(inner_gate)).astype(
            jnp.bfloat16
        )
        up_kept[quarter, :, at] = (upstream * apply_silu(inner_gate)).astype(jnp.bfloat16)

    strips(gate.shape[1], strip)
    total = dot(gate_kept[quarter], gate[...], (1, 1)) + dot(up_kept[quarter], up[...], (1, 1))
    partial[pl.ds(quarter * per, per)] = total.astype(jnp.bfloat16).reshape(
        (per,) + partial.shape[1:]
    )


GRAD_STRIP = 256


def backward_final(land, held, scratch, outputs):
    _, _, _, rows, low_gate, low_up, hidden = held
    buffers, sems = scratch
    width, inner = land.shape[-1], hidden.shape[-1]
    row_count = low_gate.shape[0] * low_gate.shape[1]
    started = {}

    def flat(ref):
        return ref[...].reshape(row_count, ref.shape[-1])

    def turned(ref, at):
        lead = ref.shape[:-1]
        return ref[(slice(None),) * len(lead) + (at,)].reshape(row_count, GRAD_STRIP).T

    def store(slot, part, value, target):
        if (slot, part) in started:
            started[slot, part].wait()
        view = buffers.at[slot, part, :, pl.ds(0, value.shape[1])]
        buffers[slot, part, :, 0 : value.shape[1]] = value
        copy = pltpu.make_async_copy(view, target, sems.at[slot, part])
        copy.start()
        started[slot, part] = copy

    for j in range(width // GRAD_STRIP):
        at = slice(j * GRAD_STRIP, (j + 1) * GRAD_STRIP)
        left = turned(rows, at)
        store(j % 2, 0, dot(left, flat(low_gate), (1, 0)), outputs[0].at[at])
        store(j % 2, 1, dot(left, flat(low_up), (1, 0)), outputs[1].at[at])
    for j in range(inner // GRAD_STRIP):
        at = slice(j * GRAD_STRIP, (j + 1) * GRAD_STRIP)
        value = dot(turned(hidden, at), land[...].reshape(row_count, width), (1, 0))
        store(j % 2, j // 2 % 2, value, outputs[2].at[at])
    for copy in started.values():
        copy.wait()


def expert_backward(sending, gate, up, down, kept, work, cols, collective_id):
    out_shape = [jax.ShapeDtypeStruct(w.shape, jnp.float32) for w in (gate, up, down)]
    widest = max(gate.shape[1], down.shape[1])
    extra = [
        pltpu.VMEM((2, 2, GRAD_STRIP, widest), jnp.float32),
        pltpu.SemaphoreType.DMA((2, 2)),
    ]
    return expert_pass(
        sending, [gate, up, down] + list(kept), out_shape, extra, backward_step, backward_final,
        work, True, cols, collective_id,
    )


def on_device(
    hidden_in,
    w_query,
    w_key,
    w_value,
    w_out,
    norm_attn,
    norm_ffn,
    w_router,
    shared_gate,
    shared_up,
    shared_down,
    expert_gate,
    expert_up,
    expert_down,
    teacher,
    routes,
    cont_lengths,
    valid_mask,
):
    rows_dev, groups, model_width = hidden_in.shape
    tokens = rows_dev * groups
    head_count = lax.axis_size("head")
    cols = lax.axis_size("blk")
    devices = head_count * cols
    slices = devices // EXPERTS
    pairs = devices // 2
    shard = w_query.shape[0]
    hidden = shared_gate.shape[1]
    bf16, f32 = jnp.bfloat16, jnp.float32
    me = flat_index(cols)
    core, pair = lax.rem(me, 2), lax.div(me, 2)
    holds, unit = unit_place(pair)

    packed = jnp.concatenate([w_query, w_key, w_value], axis=1)
    router_size = shard * EXPERTS
    router_rows = -(-router_size // 128)
    router_pad = router_rows * 128 - router_size

    def in_rows(gains_first, gains_second, scalar, router):
        count = gains_first.shape[0]
        pieces = [
            jnp.pad(gains_first.astype(f32), ((0, 0), (0, 128 - shard))),
            jnp.pad(gains_second.astype(f32), ((0, 0), (0, 128 - shard))),
            jnp.broadcast_to(scalar, (count, 128)),
            jnp.pad(router.astype(f32), ((0, 0), (0, router_pad + (5 - router_rows) * 128))),
        ]
        return jnp.concatenate(pieces, axis=1).reshape(count, 8, 128)

    small = in_rows(
        norm_attn[None],
        norm_ffn[None],
        jnp.sum(valid_mask.astype(f32)),
        w_router.reshape(1, router_size),
    )[0]
    all_packed, all_small = gather_all([packed, small], cols, 0)
    proj_mat = all_packed.reshape(model_width, 3 * model_width)
    all_small = all_small.reshape(devices, 8, 128)
    gain_attn = all_small[:, 0, :shard].reshape(model_width)
    gain_ffn = all_small[:, 1, :shard].reshape(model_width)
    valid_total = jnp.sum(all_small[:, 2, 0])
    route_mat = (
        all_small[:, 3 : 3 + router_rows]
        .reshape(devices, router_rows * 128)[:, :router_size]
        .reshape(model_width, EXPERTS)
        .astype(bf16)
    )

    wide = jnp.concatenate([shared_gate, shared_up], axis=1)

    local_pos = me * rows_dev + jnp.arange(rows_dev, dtype=jnp.int32)
    local_begin = segment_starts(local_pos, cont_lengths)
    cosine, sine = rotary_tables(local_pos, local_begin)
    flat_in = hidden_in.reshape(tokens, model_width)
    def rotated(halves, sine_now):
        first, second = halves[:, 0], halves[:, 1]
        return jnp.concatenate(
            [first * cosine - second * sine_now, second * cosine + first * sine_now], axis=1
        )

    def by_unit(blocks):
        rows = blocks.shape[1]
        return (
            blocks.reshape(HEADS, rows, rows_dev, groups)
            .transpose(3, 0, 1, 2)
            .reshape(groups * HEADS, rows, rows_dev)
        )

    def by_head(blocks):
        rows = blocks.shape[1]
        return (
            blocks.reshape(groups, HEADS, rows, rows_dev)
            .transpose(1, 2, 3, 0)
            .reshape(HEADS, rows, tokens)
        )

    at_home = rows_dev == TILE and groups == 1
    if at_home:
        normed_attn, scaling_attn, q_blocks, kv_blocks = project(
            flat_in, gain_attn, proj_mat, cosine, sine, cols, 1
        )
    else:
        normed_exact, scaling_attn = root_norm(flat_in, gain_attn)
        normed_attn = normed_exact.astype(bf16)
        projected = dot(proj_mat, normed_attn, (0, 1)).reshape(
            3, HEADS, 2, HEAD_DIM // 2, tokens
        )
        qkv_blocks = jnp.concatenate(
            [
                rotated(projected[0], sine),
                rotated(projected[1], sine),
                projected[2].reshape(HEADS, HEAD_DIM, tokens),
            ],
            axis=1,
        ).astype(bf16)
        q_blocks, kv_blocks = to_units(by_unit(qkv_blocks), cols, True, 1)

    unit_lengths = lax.dynamic_slice_in_dim(
        cont_lengths, jnp.minimum(unit // HEADS, groups - 1), 1, axis=0
    )
    place = (
        (2 * jnp.arange(pairs, dtype=jnp.int32) + core)[:, None] * rows_dev
        + jnp.arange(rows_dev, dtype=jnp.int32)
    ).reshape(-1)
    run = segment_starts(place, unit_lengths).reshape(-1, 1, TILE)
    queries, keys_values = to_tiles(q_blocks), to_tiles(kv_blocks)
    if at_home:
        exact, lse, attended, out_mat, share_down, share_wide = attend_home(
            queries, keys_values, run, [w_out, shared_down, wide], cols, 2
        )
    else:
        exact, low, lse = attend(queries, keys_values, run, rows_dev)
        (attended,) = to_tokens([from_tiles(low, rows_dev)], cols, 2)
        out_mat, share_down, share_wide = gather_all([w_out, shared_down, wide], cols, 11)
    out_mat = out_mat.reshape(model_width, model_width)
    share_down = share_down.reshape(hidden, model_width)
    share_wide = share_wide.reshape(model_width, 2 * hidden)
    attended = by_head(attended).reshape(model_width, tokens)

    residual_mid = flat_in + dot(attended, out_mat, (0, 0))
    normed_mid, scaling_ffn = root_norm(residual_mid, gain_ffn)
    normed_ffn = normed_mid.astype(bf16)

    route_flat = routes.reshape(tokens, TOP)
    route_onehot = (route_flat[:, :, None] == jnp.arange(EXPERTS, dtype=jnp.int32)).astype(f32)
    flat_routes = route_flat.reshape(-1)
    route_hits = (flat_routes[:, None] == jnp.arange(EXPERTS, dtype=jnp.int32)).astype(bf16)
    order = jnp.arange(tokens * TOP, dtype=jnp.int32)
    before = dot((order[None, :] < order[:, None]).astype(bf16), route_hits, (1, 0))
    ranking = jnp.sum(before * route_hits.astype(f32), axis=1).astype(jnp.int32)
    slot_of = (flat_routes * CAP + ranking).reshape(tokens, TOP)
    slot_ids = jnp.arange(EXPERTS * CAP, dtype=jnp.int32)
    place_first = (slot_ids[:, None] == slot_of[None, :, 0]).astype(bf16)
    place_second = (slot_ids[:, None] == slot_of[None, :, 1]).astype(bf16)

    sending = dot(place_first + place_second, normed_ffn, (1, 0)).astype(bf16)
    sending = sending.reshape(EXPERTS, CAP, model_width)

    logits = dot(normed_ffn, route_mat, (1, 0))
    chosen = jnp.sum(route_onehot * logits[:, None, :], axis=-1)
    gate_probs = jax.nn.softmax(chosen, axis=1)
    out = jax.ShapeDtypeStruct
    shared_work = Work(
        [normed_ffn, share_wide, share_down],
        [
            out((tokens, hidden), bf16),
            out((tokens, hidden), bf16),
            out((tokens, hidden), bf16),
            out((tokens, model_width), f32),
        ],
        shared_forward,
    )
    if slices == 2:
        passed = expert_forward(
            sending, expert_gate, expert_up, expert_down, shared_work, cols, 3
        )
        returned, kept, shared_results = passed[0], passed[1:5], passed[5:]
    else:
        (arrived,) = spread([sending], cols, slices, EXPERTS, 3)
        arrived = arrived.reshape(devices * CAP, model_width)
        inner_gate = dot(arrived, expert_gate, (1, 0))
        inner_up = dot(arrived, expert_up, (1, 0))
        inner_hidden = (apply_silu(inner_gate) * inner_up).astype(bf16)
        partial_out = dot(inner_hidden, expert_down, (1, 0)).astype(bf16)
        returned, *shared_results = collect(
            [partial_out.reshape(slices, EXPERTS, CAP, model_width)], cols, 4, shared_work
        )
    shared_gate_in, shared_up_in, shared_hidden, shared_out = shared_results
    expert_rows = returned.reshape(EXPERTS * CAP, model_width)
    routed_first = dot(place_first, expert_rows, (0, 0))
    routed_second = dot(place_second, expert_rows, (0, 0))
    mixture = gate_probs[:, 0:1] * routed_first + gate_probs[:, 1:2] * routed_second
    layer_flat = residual_mid + shared_out + mixture

    keep_rows = valid_mask.reshape(tokens).astype(f32)[:, None]
    deviation = layer_flat - teacher.reshape(tokens, model_width)
    loss_local = jnp.sum(keep_rows * deviation * deviation)
    grad_rows = keep_rows * deviation * (tokens * devices / valid_total)
    back_first = (gate_probs[:, 0:1] * grad_rows).astype(bf16)
    back_second = (gate_probs[:, 1:2] * grad_rows).astype(bf16)
    back_send = (
        dot(place_first, back_first, (1, 0)) + dot(place_second, back_second, (1, 0))
    ).astype(bf16)
    shared_work = Work(
        [
            grad_rows.astype(bf16),
            normed_ffn,
            shared_gate_in,
            shared_up_in,
            shared_hidden,
            share_wide,
            share_down,
        ],
        [
            out(share_wide.shape, bf16),
            out(share_down.shape, bf16),
            out((tokens, model_width), f32),
        ],
        shared_backward,
        {0: 5, 1: 6},
    )
    back_send = back_send.reshape(EXPERTS, CAP, model_width)
    if slices == 2:
        passed = expert_backward(
            back_send, expert_gate, expert_up, expert_down, kept, shared_work, cols, 5
        )
        back_returned, grad_expert_gate, grad_expert_up, grad_expert_down = passed[:4]
        grad_share_wide, grad_share_down, shared_back = passed[4:]
    else:
        back_arrived, grad_share_wide, grad_share_down, shared_back = spread(
            [back_send], cols, slices, EXPERTS, 5, shared_work
        )
        back_arrived = back_arrived.reshape(devices * CAP, model_width)
        grad_inner = dot(back_arrived, expert_down, (1, 1))
        grad_inner_gate = (grad_inner * inner_up * silu_slope(inner_gate)).astype(bf16)
        grad_inner_up = (grad_inner * apply_silu(inner_gate)).astype(bf16)
        back_partial = (
            dot(grad_inner_gate, expert_gate, (1, 1)) + dot(grad_inner_up, expert_up, (1, 1))
        ).astype(bf16)
        (back_returned,) = collect(
            [back_partial.reshape(slices, EXPERTS, CAP, model_width)], cols, 6
        )
        grad_expert_down = dot(inner_hidden, back_arrived, (0, 0))
        grad_expert_gate = dot(arrived, grad_inner_gate, (0, 0))
        grad_expert_up = dot(arrived, grad_inner_up, (0, 0))

    grad_gate = jnp.stack(
        [jnp.sum(grad_rows * routed_first, axis=-1), jnp.sum(grad_rows * routed_second, axis=-1)],
        axis=1,
    )
    grad_chosen = gate_probs * (grad_gate - jnp.sum(gate_probs * grad_gate, axis=1, keepdims=True))
    grad_logits = jnp.sum(route_onehot * grad_chosen[:, :, None], axis=1).astype(bf16)
    grad_route_mat = dot(normed_ffn, grad_logits, (0, 0))

    back_rows = back_returned.reshape(EXPERTS * CAP, model_width)
    grad_normed = (
        dot(place_first + place_second, back_rows, (0, 0))
        + dot(grad_logits, route_mat, (1, 1))
        + shared_back
    )

    grad_mid_norm, grad_gain_ffn = root_norm_back(residual_mid, scaling_ffn, gain_ffn, grad_normed)
    grad_mid = grad_rows + grad_mid_norm
    grad_mid_low = grad_mid.astype(bf16)
    grad_attended = dot(out_mat, grad_mid_low, (1, 1)).astype(bf16)
    grad_out_mat = dot(attended, grad_mid_low, (1, 0))
    grad_blocks = by_unit(grad_attended.reshape(HEADS, HEAD_DIM, tokens))
    spots = (2, cols // 4, 2, 2)
    parts = [
        grad_share_wide.reshape(spots + (shard, 2 * hidden)),
        grad_share_down.reshape(spots + shared_down.shape),
        grad_out_mat.astype(bf16).reshape(spots + (shard, model_width)),
    ]
    if at_home:
        dq, dkv, share_sums, grad_share_down, grad_out_sum = attend_back_home(
            queries, keys_values, grad_blocks, exact, lse, run, parts, cols, 10
        )
    else:
        (grad_blocks,) = to_units(grad_blocks, cols, False, 7)
        dq, dkv, share_sums, grad_share_down, grad_out_sum = attend_back(
            queries, keys_values, to_tiles(grad_blocks), exact, lse, run, rows_dev, parts, cols, 10
        )
        dq, dkv = to_tokens([from_tiles(dq, rows_dev), from_tiles(dkv, rows_dev)], cols, 8)
    dq, dkv = by_head(dq).astype(f32), by_head(dkv)

    def halves_of(rows):
        return rows.reshape(HEADS, 2, HEAD_DIM // 2, tokens)

    grad_proj = jnp.concatenate(
        [
            rotated(halves_of(dq), -sine).astype(bf16).reshape(model_width, tokens),
            rotated(halves_of(dkv[:, :HEAD_DIM].astype(f32)), -sine)
            .astype(bf16)
            .reshape(model_width, tokens),
            dkv[:, HEAD_DIM:].reshape(model_width, tokens),
        ],
        axis=0,
    )
    grad_normed_attn = dot(grad_proj, proj_mat, (0, 1))
    grad_in_norm, grad_gain_attn = root_norm_back(
        flat_in, scaling_attn, gain_attn, grad_normed_attn
    )
    input_grad = (grad_mid + grad_in_norm).reshape(rows_dev, groups, model_width)

    grad_attn = dot(normed_attn, grad_proj, (0, 1)).astype(bf16)
    tail = in_rows(
        grad_gain_attn.reshape(devices, shard),
        grad_gain_ffn.reshape(devices, shard),
        loss_local,
        grad_route_mat.reshape(devices, router_size),
    )
    attn_sums, tail_sums = reduce_all(
        [grad_attn.reshape(spots + (shard, 3 * model_width)), tail.reshape(spots + (8, 128))],
        cols,
        9,
    )
    loss_value = tail_sums[2, 0] / (valid_total * model_width)
    return (
        layer_flat.reshape(rows_dev, groups, model_width),
        input_grad,
        loss_value,
        attn_sums[:, :model_width],
        attn_sums[:, model_width : 2 * model_width],
        attn_sums[:, 2 * model_width :],
        grad_out_sum,
        tail_sums[0, :shard],
        tail_sums[1, :shard],
        tail_sums[3 : 3 + router_rows].reshape(-1)[:router_size].reshape(shard, EXPERTS),
        share_sums[:, :hidden],
        share_sums[:, hidden:],
        grad_share_down,
        grad_expert_gate,
        grad_expert_up,
        grad_expert_down,
    )


def solution(mesh):
    placed = (
        P(("head", "blk"), None, None),
        P(("head", "blk"), None),
        P(("head", "blk"), None),
        P(("head", "blk"), None),
        P(("head", "blk"), None),
        P(("head", "blk")),
        P(("head", "blk")),
        P(("head", "blk"), None),
        P(("head", "blk"), None),
        P(("head", "blk"), None),
        P(("head", "blk"), None),
        P(None, ("head", "blk")),
        P(None, ("head", "blk")),
        P(("head", "blk"), None),
        P(("head", "blk"), None, None),
        P(("head", "blk"), None, None),
        P(),
        P(("head", "blk"), None),
    )
    return jax.shard_map(
        on_device,
        mesh=mesh,
        in_specs=placed,
        out_specs=(
            P(("head", "blk"), None, None),
            P(("head", "blk"), None, None),
            P(),
            P(("head", "blk"), None),
            P(("head", "blk"), None),
            P(("head", "blk"), None),
            P(("head", "blk"), None),
            P(("head", "blk")),
            P(("head", "blk")),
            P(("head", "blk"), None),
            P(("head", "blk"), None),
            P(("head", "blk"), None),
            P(("head", "blk"), None),
            P(None, ("head", "blk")),
            P(None, ("head", "blk")),
            P(("head", "blk"), None),
        ),
        check_vma=False,
    )
```

```python
import functools
import math

import jax
import jax.numpy as jnp
from jax import lax
from jax.experimental import pallas as pl
from jax.experimental.pallas import tpu as pltpu
from jax.sharding import PartitionSpec as P

HEADS = 12
HEAD_DIM = 64
EXPERTS = 16
TOP = 2
PROMPT = 4096
LONGEST = 768
CAP = 64

EPSILON = 1e-06
NEGATIVE = -1e30
SCORE_SCALE = HEAD_DIM ** (-0.5)
EXP_SCALE = SCORE_SCALE * math.log2(math.e)

TILE = 256
FWD_WIDE, FWD_MASK = 8, 4
BWD_WIDE, BWD_MASK = 4, 2

MESH_ID = pl.DeviceIdType.MESH
AXES = ("head", "blk")


def apply_silu(argument):
    return argument * jax.nn.sigmoid(argument)


def silu_slope(argument):
    sigmoid_val = jax.nn.sigmoid(argument)
    return sigmoid_val * (1.0 + argument * (1.0 - sigmoid_val))


def root_norm(inputs, gain_vec):
    scaling = lax.rsqrt(jnp.mean(inputs * inputs, axis=-1, keepdims=True) + EPSILON)
    return (inputs * scaling * gain_vec, scaling)


def root_norm_back(inputs, scaling, gain_vec, upstream):
    weighted = gain_vec * upstream
    through = scaling * weighted - inputs * scaling**3 * jnp.mean(
        weighted * inputs, axis=-1, keepdims=True
    )
    return (through, jnp.sum(upstream * inputs * scaling, axis=0))


def segment_starts(positions, cont_lengths):
    count = cont_lengths.shape[1]
    earlier = jnp.arange(count)[None, :] < jnp.arange(count)[:, None]
    begins = PROMPT + jnp.sum(jnp.where(earlier, cont_lengths[:, None, :], 0), axis=2)
    passed = begins[None, :, :] <= positions[:, None, None]
    return jnp.max(jnp.where(passed, begins[None], 0), axis=-1)


def rotary_tables(positions, run_begin):
    relative = jnp.where(
        positions[:, None] < PROMPT, positions[:, None], PROMPT + positions[:, None] - run_begin
    )
    angle_pos = relative.astype(jnp.float32).reshape(1, -1)
    half_dim = HEAD_DIM // 2
    frequency = jnp.exp(
        jnp.arange(half_dim, dtype=jnp.int32).astype(jnp.float32)
        * (-2.0 * math.log(10000.0) / HEAD_DIM)
    )
    angles = angle_pos * frequency[:, None]
    return (jnp.cos(angles), jnp.sin(angles))


def flat_index(cols):
    return lax.axis_index("head") * cols + lax.axis_index("blk")


def coords(flat, cols):
    return (lax.div(flat, cols), lax.rem(flat, cols))


def greet(flat, cols):
    pl.semaphore_signal(
        pltpu.get_barrier_semaphore(),
        inc=1,
        device_id=coords(flat, cols),
        device_id_type=MESH_ID,
    )


def remote(source, target, send_sem, recv_sem, flat, cols):
    return pltpu.make_async_remote_copy(
        src_ref=source,
        dst_ref=target,
        send_sem=send_sem,
        recv_sem=recv_sem,
        device_id=coords(flat, cols),
        device_id_type=MESH_ID,
    )


def loop(first, last, body):
    def step(index, carry):
        body(index)
        return carry

    lax.fori_loop(first, last, step, 0)


def greet_partners(cols, size, partners):
    me = flat_index(cols)
    mine, group = lax.rem(me, size), lax.div(me, size)
    loop(1, partners, lambda s: greet(lax.rem(group + s, partners) * size + mine, cols))
    for t in range(1, size):
        greet(group * size + lax.rem(mine + t, size), cols)
    pl.semaphore_wait(pltpu.get_barrier_semaphore(), partners + size - 2)
    return mine, group


class Work:
    def __init__(self, arrays, out_shape, body, reuse=None):
        self.arrays, self.out_shape, self.body = list(arrays), list(out_shape), body
        self.reuse = reuse or {}

    def own_buffers(self):
        return [i for i in range(len(self.out_shape)) if i not in self.reuse]

    def scratch(self):
        held = self.arrays + [self.out_shape[i] for i in self.own_buffers()]
        total = len(self.arrays) + len(self.out_shape)
        return [pltpu.VMEM(a.shape, a.dtype) for a in held] + [pltpu.SemaphoreType.DMA((max(total, 1),))]

    def bind(self, refs):
        count, total = len(self.arrays), len(self.arrays) + len(self.out_shape)
        inputs, outputs = refs[:count], refs[count:total]
        held_in, rest, sems = refs[total : total + count], refs[total + count : -1], refs[-1]
        held_out = [None] * len(outputs)
        for buffer, i in zip(rest, self.own_buffers()):
            held_out[i] = buffer
        for i, source in self.reuse.items():
            held_out[i] = held_in[source]
        loads = [
            pltpu.make_async_copy(inputs[i], held_in[i], sems.at[i]) for i in range(count)
        ]
        stores = [
            pltpu.make_async_copy(held_out[i], outputs[i], sems.at[count + i])
            for i in range(len(outputs))
        ]

        def begin():
            for copy in loads:
                copy.start()

        def run():
            for copy in loads:
                copy.wait()
            self.body(held_in, held_out, [copy.start for copy in stores])

        def end():
            for copy in stores:
                copy.wait()

        return begin, run, end


def split_refs(refs, count, work):
    extra_in = len(work.arrays) if work else 0
    extra_out = len(work.out_shape) if work else 0
    inputs, refs = refs[:count], refs[count:]
    work_in, refs = refs[:extra_in], refs[extra_in:]
    outputs, refs = refs[:count], refs[count:]
    work_out, refs = refs[:extra_out], refs[extra_out:]
    if not work:
        return inputs, outputs, refs, (lambda: None,) * 3
    held = extra_in + len(work.own_buffers()) + 1
    return inputs, outputs, refs[:-held], work.bind(work_in + work_out + refs[-held:])


def spread_kernel(cols, size, partners, work, count, *refs):
    inputs, outputs, sems, (begin, run, end) = split_refs(refs, count, work)
    begin()
    mine, group = greet_partners(cols, size, partners)

    def far(i, s):
        send, recv = sems[5 * i], sems[5 * i + 1]
        other = lax.rem(group + s, partners)
        return remote(
            inputs[i].at[other], outputs[i].at[mine, group], send.at[s], recv.at[s], other * size + mine, cols
        )

    def near(i, s, t):
        send, recv = sems[5 * i + 2], sems[5 * i + 3]
        block = outputs[i].at[mine, lax.rem(group - s + partners, partners)]
        target = group * size + lax.rem(mine + t, size)
        return remote(block, block, send.at[s, t], recv.at[s, t], target, cols)

    def own(i):
        return pltpu.make_async_copy(inputs[i].at[group], outputs[i].at[mine, group], sems[5 * i + 4])

    def each(action):
        for i in range(count):
            action(i)

    def near_all(s, action):
        for i in range(count):
            for t in range(1, size):
                action(near(i, s, t))

    each(lambda i: own(i).start())
    loop(1, partners, lambda s: each(lambda i: far(i, s).start()))
    each(lambda i: own(i).wait())
    near_all(0, lambda copy: copy.start())
    run()

    def relay(s):
        each(lambda i: far(i, s).wait_recv())
        near_all(s, lambda copy: copy.start())

    loop(1, partners, relay)
    loop(1, partners, lambda s: each(lambda i: far(i, s).wait_send()))
    loop(0, partners, lambda s: near_all(s, lambda copy: copy.wait()))
    end()


def spread(arrays, cols, size, partners, collective_id, work=None):
    count = len(arrays)
    out_shape, scratch = [], []
    for array in arrays:
        block = array.shape[1:]
        out_shape.append(jax.ShapeDtypeStruct((size, partners) + block, array.dtype))
        scratch += [
            pltpu.SemaphoreType.DMA((partners,)),
            pltpu.SemaphoreType.DMA((partners,)),
            pltpu.SemaphoreType.DMA((partners, size)),
            pltpu.SemaphoreType.DMA((partners, size)),
            pltpu.SemaphoreType.DMA,
        ]
    extra = []
    if work:
        extra, out_shape, scratch = work.arrays, out_shape + work.out_shape, scratch + work.scratch()
    return pl.pallas_call(
        functools.partial(spread_kernel, cols, size, partners, work, count),
        out_shape=out_shape,
        in_specs=[pl.BlockSpec(memory_space=pl.ANY)] * (count + len(extra)),
        out_specs=[pl.BlockSpec(memory_space=pl.ANY)] * len(out_shape),
        scratch_shapes=scratch,
        compiler_params=pltpu.CompilerParams(
            collective_id=collective_id, has_side_effects=True, vmem_limit_bytes=52 * 2**20
        ),
    )(*arrays, *extra)


def collect_kernel(cols, size, partners, work, count, *refs):
    inputs, outputs, scratch, (begin, run, end) = split_refs(refs, count, work)
    begin()
    mine, group = greet_partners(cols, size, partners)

    def near(i, s, t):
        inbox, send, recv = scratch[7 * i + 1], scratch[7 * i + 2], scratch[7 * i + 3]
        other = lax.rem(group + s, partners)
        member = lax.rem(mine + t, size)
        return remote(
            inputs[i].at[member, other],
            inbox.at[t - 1, other],
            send.at[s, t],
            recv.at[s, t],
            group * size + member,
            cols,
        )

    def far(i, s):
        stage, send, recv = scratch[7 * i], scratch[7 * i + 4], scratch[7 * i + 5]
        other = lax.rem(group + s, partners)
        return remote(
            stage.at[other], outputs[i].at[group], send.at[s], recv.at[s], other * size + mine, cols
        )

    def own(i):
        return pltpu.make_async_copy(
            scratch[7 * i].at[group], outputs[i].at[group], scratch[7 * i + 6]
        )

    def each(action):
        for i in range(count):
            action(i)

    def near_all(s, action):
        for i in range(count):
            for t in range(1, size):
                action(near(i, s, t))

    def add(s):
        other = lax.rem(group + s, partners)
        for i in range(count):
            stage, inbox = scratch[7 * i], scratch[7 * i + 1]
            total = inputs[i][mine, other].astype(jnp.float32)
            for t in range(1, size):
                total = total + inbox[t - 1, other].astype(jnp.float32)
            stage[other] = total.astype(stage.dtype)

    loop(1, partners, lambda s: near_all(s, lambda copy: copy.start()))
    near_all(0, lambda copy: copy.start())

    def relay(s):
        near_all(s, lambda copy: copy.wait_recv())
        add(s)
        each(lambda i: far(i, s).start())

    loop(1, partners, relay)
    near_all(0, lambda copy: copy.wait_recv())
    add(0)
    each(lambda i: own(i).start())
    run()
    loop(0, partners, lambda s: near_all(s, lambda copy: copy.wait_send()))
    loop(1, partners, lambda s: each(lambda i: far(i, s).wait()))
    each(lambda i: own(i).wait())
    end()


def collect(arrays, cols, collective_id, work=None):
    count = len(arrays)
    size, partners = arrays[0].shape[:2]
    out_shape, scratch = [], []
    for array in arrays:
        block = array.shape[2:]
        out_shape.append(jax.ShapeDtypeStruct((partners,) + block, array.dtype))
        scratch += [
            pltpu.VMEM((partners,) + block, array.dtype),
            pltpu.VMEM((size - 1, partners) + block, array.dtype),
            pltpu.SemaphoreType.DMA((partners, size)),
            pltpu.SemaphoreType.DMA((partners, size)),
            pltpu.SemaphoreType.DMA((partners,)),
            pltpu.SemaphoreType.DMA((partners,)),
            pltpu.SemaphoreType.DMA,
        ]
    extra = []
    if work:
        extra, out_shape, scratch = work.arrays, out_shape + work.out_shape, scratch + work.scratch()
    return pl.pallas_call(
        functools.partial(collect_kernel, cols, size, partners, work, count),
        out_shape=out_shape,
        in_specs=[pl.BlockSpec(memory_space=pltpu.VMEM)] * count
        + [pl.BlockSpec(memory_space=pl.ANY)] * len(extra),
        out_specs=[pl.BlockSpec(memory_space=pl.ANY)] * len(out_shape),
        scratch_shapes=scratch,
        compiler_params=pltpu.CompilerParams(
            collective_id=collective_id, has_side_effects=True, vmem_limit_bytes=52 * 2**20
        ),
    )(*arrays, *extra)


def spot():
    column = lax.axis_index("blk")
    return (
        lax.axis_index("head"),
        lax.div(column, 4),
        lax.rem(lax.div(column, 2), 2),
        lax.rem(column, 2),
    )


def at_spot(head, depth, x, core):
    return (head, depth * 4 + x * 2 + core)


def push(source, target, send_sem, recv_sem, device):
    return pltpu.make_async_remote_copy(
        src_ref=source,
        dst_ref=target,
        send_sem=send_sem,
        recv_sem=recv_sem,
        device_id=device,
        device_id_type=MESH_ID,
    )


def greet_mesh(depths):
    head, depth, x, core = spot()
    barrier = pltpu.get_barrier_semaphore()

    def signal(device):
        pl.semaphore_signal(barrier, inc=1, device_id=device, device_id_type=MESH_ID)

    loop(1, depths, lambda s: signal(at_spot(head, lax.rem(depth + s, depths), x, core)))
    signal(at_spot(head, depth, 1 - x, core))
    signal(at_spot(1 - head, depth, x, core))
    signal(at_spot(head, depth, x, 1 - core))
    pl.semaphore_wait(barrier, depths + 2)


GATHER_SEMS = 13


def gather_sems(depths):
    row, square = pltpu.SemaphoreType.DMA((depths,)), pltpu.SemaphoreType.DMA((4, depths))
    return [row] * 10 + [square] * 2 + [pltpu.SemaphoreType.DMA]


class Gather:
    def __init__(self, source, result, sems, depths, cut):
        self.source, self.result, self.sems = source, result, sems
        self.depths, self.cut = depths, cut
        self.width = source.shape[-1]

    def along(self, s):
        head, depth, x, core = spot()
        device = at_spot(head, lax.rem(depth + s, self.depths), x, core)
        target = self.result.at[head, depth, x, core]
        return push(self.source, target, self.sems[0].at[s], self.sems[1].at[s], device)

    def block(self, s, far_head, far_x):
        head, depth, x, core = spot()
        return self.result.at[
            1 - head if far_head else head,
            lax.rem(depth - s + self.depths, self.depths),
            1 - x if far_x else x,
            core,
        ]

    def hop(self, kind, s):
        head, depth, x, core = spot()
        if kind in (0, 3):
            device = at_spot(head, depth, 1 - x, core)
        else:
            device = at_spot(1 - head, depth, x, core)
        view = self.block(s, kind == 3, kind == 2)
        if kind == 2:
            view = view.at[:, pl.ds(0, self.cut)]
        if kind == 3:
            view = view.at[:, pl.ds(self.cut, self.width - self.cut)]
        sems = self.sems
        return push(view, view, sems[2 + 2 * kind].at[s], sems[3 + 2 * kind].at[s], device)

    def kinds(self):
        return (2, 3) if self.cut < self.width else (2,)

    def share(self, part, s):
        head, depth, x, core = spot()
        view = self.block(s, part // 2 == 1, part % 2 == 1)
        device = at_spot(head, depth, x, 1 - core)
        return push(view, view, self.sems[10].at[part, s], self.sems[11].at[part, s], device)

    def own(self):
        return pltpu.make_async_copy(self.source, self.result.at[spot()], self.sems[12])

    def start(self):
        self.own().start()
        loop(1, self.depths, lambda s: self.along(s).start())

    def begin_near(self, s):
        self.hop(0, s).start()
        self.hop(1, s).start()
        self.share(0, s).start()

    def start_own(self):
        self.own().wait()
        self.begin_near(0)

    def spread_near(self):
        def step(s):
            self.along(s).wait_recv()
            self.begin_near(s)

        loop(1, self.depths, step)

    def spread_far(self):
        def step(s):
            self.hop(0, s).wait_recv()
            self.hop(2, s).start()
            self.share(1, s).start()
            self.hop(1, s).wait_recv()
            if self.cut < self.width:
                self.hop(3, s).start()
            self.share(2, s).start()

        loop(0, self.depths, step)

    def settle(self):
        def step(s):
            for kind in self.kinds():
                self.hop(kind, s).wait_recv()
            self.share(3, s).start()

        loop(0, self.depths, step)

    def finish(self):
        loop(1, self.depths, lambda s: self.along(s).wait_send())

        def step(s):
            for kind in (0, 1) + self.kinds():
                self.hop(kind, s).wait_send()
            for part in range(4):
                self.share(part, s).wait()

        loop(0, self.depths, step)


class DepthGather:
    def __init__(self, source, result, sems, depths):
        self.source, self.result, self.sems, self.depths = source, result, sems, depths

    def along(self, s):
        head, depth, x, core = spot()
        device = at_spot(head, lax.rem(depth + s, self.depths), x, core)
        return push(
            self.source, self.result.at[depth], self.sems[0].at[s], self.sems[1].at[s], device
        )

    def own(self):
        return pltpu.make_async_copy(self.source, self.result.at[spot()[1]], self.sems[2])

    def start(self):
        self.own().start()
        loop(1, self.depths, lambda s: self.along(s).start())

    def finish(self):
        self.own().wait()
        loop(1, self.depths, lambda s: self.along(s).wait())


def depth_sems(depths):
    return [pltpu.SemaphoreType.DMA((depths,))] * 2 + [pltpu.SemaphoreType.DMA]


class PlaneGather(Gather):
    def near_copy(self, s, device, send_sem, recv_sem):
        head, depth, x, core = spot()
        goal = lax.rem(depth - s + self.depths, self.depths)
        target = self.result.at[head, goal, x, core]
        return push(self.source.at[goal], target, send_sem, recv_sem, device)

    def hop(self, kind, s):
        if kind > 1:
            return super().hop(kind, s)
        head, depth, x, core = spot()
        device = at_spot(head, depth, 1 - x, core) if kind == 0 else at_spot(1 - head, depth, x, core)
        return self.near_copy(
            s, device, self.sems[2 + 2 * kind].at[s], self.sems[3 + 2 * kind].at[s]
        )

    def share(self, part, s):
        if part > 0:
            return super().share(part, s)
        head, depth, x, core = spot()
        device = at_spot(head, depth, x, 1 - core)
        return self.near_copy(s, device, self.sems[10].at[part, s], self.sems[11].at[part, s])

    def own(self):
        head, _, x, core = spot()
        return pltpu.make_async_copy(
            self.source, self.result.at[head, :, x, core], self.sems[12]
        )

    def start(self):
        self.own().start()
        loop(0, self.depths, self.begin_near)

    def finish(self):
        self.own().wait()

        def step(s):
            for kind in (0, 1) + self.kinds():
                self.hop(kind, s).wait_send()
            for part in range(4):
                self.share(part, s).wait()

        loop(0, self.depths, step)


def cut_of(width):
    return width // 256 * 128 if width >= 256 else width


def gathered_shape(shard, depths):
    return jax.ShapeDtypeStruct((2, depths, 2, 2) + shard.shape, shard.dtype)


def gather_kernel(depths, count, *refs):
    gathers = gathers_of(refs[:count], refs[count : 2 * count], refs[2 * count :], depths)
    greet_mesh(depths)
    for step in ("start", "start_own", "spread_near", "spread_far", "settle", "finish"):
        for gather in gathers:
            getattr(gather, step)()


def gather_all(arrays, cols, collective_id):
    depths, count = cols // 4, len(arrays)
    return pl.pallas_call(
        functools.partial(gather_kernel, depths, count),
        out_shape=[gathered_shape(array, depths) for array in arrays],
        in_specs=[pl.BlockSpec(memory_space=pl.ANY)] * count,
        out_specs=[pl.BlockSpec(memory_space=pl.ANY)] * count,
        scratch_shapes=gather_sems(depths) * count,
        compiler_params=pltpu.CompilerParams(collective_id=collective_id, has_side_effects=True),
    )(*arrays)


REDUCE_SCRATCH = 20


class Reduce:
    def __init__(self, parts, total, scratch, depths, cut):
        self.parts, self.total = parts, total
        self.sums, self.core_in, self.a1, self.b1, self.a2, self.b2, self.z_in = scratch[:7]
        self.sems = scratch[7:]
        self.depths, self.cut = depths, cut
        self.width = parts.shape[-1]
        self.two = cut < self.width
        self.first = pl.ds(0, cut)
        self.rest = pl.ds(cut, self.width - cut)

    def goal(self, s):
        return lax.rem(spot()[1] + s, self.depths)

    def to_core(self, s):
        head, depth, x, core = spot()
        goal = self.goal(s)
        return push(
            self.parts.at[:, goal, :, 1 - core],
            self.core_in.at[:, goal],
            self.sems[0].at[s],
            self.sems[1].at[s],
            at_spot(head, depth, x, 1 - core),
        )

    def hop(self, kind, s):
        head, depth, x, core = spot()
        goal = self.goal(s)
        over_x = at_spot(head, depth, 1 - x, core)
        over_head = at_spot(1 - head, depth, x, core)
        if kind == 0:
            view = self.sums.at[1 - head, goal, :, :, self.first]
            target, device = self.a1.at[goal], over_head
        elif kind == 1:
            view = self.sums.at[:, goal, 1 - x, :, self.rest]
            target, device = self.b1.at[goal], over_x
        elif kind == 2:
            view = self.sums.at[head, goal, 1 - x, :, self.first]
            target, device = self.a2.at[goal], over_x
        else:
            view = self.sums.at[1 - head, goal, x, :, self.rest]
            target, device = self.b2.at[goal], over_head
        send, recv = self.sems[2 + 2 * kind], self.sems[3 + 2 * kind]
        return push(view, target, send.at[s], recv.at[s], device)

    def along(self, s):
        head, depth, x, core = spot()
        goal = self.goal(s)
        return push(
            self.sums.at[head, goal, x],
            self.z_in.at[s],
            self.sems[10].at[s],
            self.sems[11].at[s],
            at_spot(head, goal, x, core),
        )

    def own(self, s):
        goal = self.goal(s)
        return pltpu.make_async_copy(
            self.parts.at[:, goal, :, spot()[3]], self.sums.at[:, goal], self.sems[12].at[s]
        )

    def start(self):
        def step(s):
            self.to_core(s).start()
            self.own(s).start()

        self.each(step, 0, self.depths)

    def each(self, step, first, last):
        loop(first, last, lambda i: step(lax.rem(i + 1, self.depths)))

    def add(self, where, columns, arrived):
        place = where + (slice(None), columns)
        self.sums[place] = self.sums[place] + arrived

    def near(self, first, last):
        def step(s):
            goal = self.goal(s)
            self.own(s).wait()
            self.to_core(s).wait_recv()
            whole = pl.ds(0, self.width)
            for k in range(4):
                self.add((k // 2, goal, k % 2), whole, self.core_in[k // 2, goal, k % 2])
            self.hop(0, s).start()
            if self.two:
                self.hop(1, s).start()

        self.each(step, first, last)

    def middle(self, first, last):
        head, _, x, _ = spot()

        def step(s):
            goal = self.goal(s)
            self.hop(0, s).wait_recv()
            for k in range(2):
                self.add((head, goal, k), self.first, self.a1[goal, k])
            self.hop(2, s).start()
            if self.two:
                self.hop(1, s).wait_recv()
                for k in range(2):
                    self.add((k, goal, x), self.rest, self.b1[goal, k])
                self.hop(3, s).start()

        self.each(step, first, last)

    def far(self, first, last):
        head, _, x, _ = spot()

        def step(s):
            goal = self.goal(s)
            self.hop(2, s).wait_recv()
            self.add((head, goal, x), self.first, self.a2[goal])
            if self.two:
                self.hop(3, s).wait_recv()
                self.add((head, goal, x), self.rest, self.b2[goal])
            pl.when(s > 0)(lambda: self.along(s).start())

        self.each(step, first, last)

    def finish(self):
        head, depth, x, _ = spot()
        self.total[...] = self.sums[head, depth, x].astype(jnp.float32)

        def step(s):
            self.along(s).wait_recv()
            self.total[...] += self.z_in[s].astype(jnp.float32)

        loop(1, self.depths, step)

        def sent(s):
            self.to_core(s).wait_send()
            for kind in (0, 1, 2, 3) if self.two else (0, 2):
                self.hop(kind, s).wait_send()

        loop(0, self.depths, sent)
        loop(1, self.depths, lambda s: self.along(s).wait_send())


def reduce_scratch(shape, dtype, depths, cut):
    rows, width = shape[-2:]
    rest = max(width - cut, 128)
    row = pltpu.SemaphoreType.DMA((depths,))
    return [
        pltpu.VMEM((2, depths, 2, rows, width), dtype),
        pltpu.VMEM((2, depths, 2, rows, width), dtype),
        pltpu.VMEM((depths, 2, rows, cut), dtype),
        pltpu.VMEM((depths, 2, rows, rest), dtype),
        pltpu.VMEM((depths, rows, cut), dtype),
        pltpu.VMEM((depths, rows, rest), dtype),
        pltpu.VMEM((depths, rows, width), dtype),
    ] + [row] * 13


def reduces_of(parts, totals, scratch, depths):
    return [
        Reduce(
            part,
            totals[i],
            scratch[REDUCE_SCRATCH * i : REDUCE_SCRATCH * (i + 1)],
            depths,
            cut_of(part.shape[-1]),
        )
        for i, part in enumerate(parts)
    ]


def reduce_kernel(depths, count, *refs):
    reduces = reduces_of(refs[:count], refs[count : 2 * count], refs[2 * count :], depths)
    greet_mesh(depths)
    for reduce in reduces:
        reduce.start()
    for step in ("near", "middle", "far"):
        for reduce in reduces:
            getattr(reduce, step)(0, depths)
    for reduce in reduces:
        reduce.finish()


def all_reduce_scratch(arrays, depths):
    scratch = []
    for array in arrays:
        scratch += reduce_scratch(array.shape, array.dtype, depths, cut_of(array.shape[-1]))
    return scratch


def reduce_all(arrays, cols, collective_id):
    depths, count = cols // 4, len(arrays)
    return pl.pallas_call(
        functools.partial(reduce_kernel, depths, count),
        out_shape=[jax.ShapeDtypeStruct(array.shape[-2:], jnp.float32) for array in arrays],
        in_specs=[pl.BlockSpec(memory_space=pl.ANY)] * count,
        out_specs=[pl.BlockSpec(memory_space=pltpu.VMEM)] * count,
        scratch_shapes=all_reduce_scratch(arrays, depths),
        compiler_params=pltpu.CompilerParams(
            collective_id=collective_id, has_side_effects=True, vmem_limit_bytes=52 * 2**20
        ),
    )(*arrays)


def unit_place(pair):
    return lax.rem(pair, 4) != 3, lax.div(pair, 4) * 3 + lax.rem(pair, 4)


def greet_units(cols, pairs, sibling, to_units):
    me = flat_index(cols)
    core, pair = lax.rem(me, 2), lax.div(me, 2)
    holds, unit = unit_place(pair)
    barrier = pltpu.get_barrier_semaphore()
    units = pairs // 4 * 3
    extra = 1 if sibling else 0
    if sibling:
        pl.when(holds)(lambda: greet(me + 1 - 2 * core, cols))
    if to_units:

        @pl.when(holds)
        def _():
            loop(1, pairs, lambda s: greet(lax.rem(pair + s, pairs) * 2 + core, cols))
            pl.semaphore_wait(barrier, units - 1 + extra)

        pl.when(jnp.logical_not(holds))(lambda: pl.semaphore_wait(barrier, units))
    else:

        def to_unit(s):
            other = lax.rem(pair + s, pairs)
            pl.when(unit_place(other)[0])(lambda: greet(other * 2 + core, cols))

        loop(1, pairs, to_unit)
        pl.when(holds)(lambda: pl.semaphore_wait(barrier, pairs - 1 + extra))
    return me, core, pair, holds, unit


def to_units_kernel(cols, pairs, with_kv, *refs):
    if with_kv:
        source, q_out, kv_out, send, recv, own_sem, kv_send, kv_recv, fwd_send, fwd_recv = refs
    else:
        source, q_out, send, recv, own_sem = refs
    me, core, pair, holds, _ = greet_units(cols, pairs, with_kv, True)
    q_rows = pl.ds(0, HEAD_DIM)
    kv_rows = pl.ds(HEAD_DIM, 2 * HEAD_DIM)

    def far(s):
        other = lax.rem(pair + s, pairs)
        unit = unit_place(other)[1]
        target = other * 2 + core
        copies = [
            remote(
                source.at[unit, q_rows] if with_kv else source.at[unit],
                q_out.at[pair],
                send.at[s],
                recv.at[s],
                target,
                cols,
            )
        ]
        if with_kv:
            copies.append(
                remote(
                    source.at[unit, kv_rows],
                    kv_out.at[me],
                    kv_send.at[s],
                    kv_recv.at[s],
                    target,
                    cols,
                )
            )
        return copies

    def own():
        unit = unit_place(pair)[1]
        copies = [
            pltpu.make_async_copy(
                source.at[unit, q_rows] if with_kv else source.at[unit],
                q_out.at[pair],
                own_sem.at[0],
            )
        ]
        if with_kv:
            copies.append(
                pltpu.make_async_copy(source.at[unit, kv_rows], kv_out.at[me], own_sem.at[1])
            )
        return copies

    def forward(s):
        block = kv_out.at[lax.rem(pair - s + pairs, pairs) * 2 + core]
        return remote(block, block, fwd_send.at[s], fwd_recv.at[s], me + 1 - 2 * core, cols)

    def sends(s, action):
        def run():
            for copy in far(s):
                action(copy)

        pl.when(unit_place(lax.rem(pair + s, pairs))[0])(run)

    loop(1, pairs, lambda s: sends(s, lambda copy: copy.start()))

    @pl.when(holds)
    def _():
        for copy in own():
            copy.start()
        for copy in own():
            copy.wait()
        if with_kv:
            forward(0).start()

        def take(s):
            for copy in far(s):
                copy.wait_recv()
            if with_kv:
                forward(s).start()

        loop(1, pairs, take)
        if with_kv:
            loop(0, pairs, lambda s: forward(s).wait())

    loop(1, pairs, lambda s: sends(s, lambda copy: copy.wait_send()))


def to_units(blocks, cols, with_kv, collective_id):
    units, rows, width = blocks.shape
    pairs = units // 3 * 4
    out_shape = [jax.ShapeDtypeStruct((pairs, HEAD_DIM, width), blocks.dtype)]
    scratch = [
        pltpu.SemaphoreType.DMA((pairs,)),
        pltpu.SemaphoreType.DMA((pairs,)),
        pltpu.SemaphoreType.DMA((2,)),
    ]
    if with_kv:
        out_shape.append(jax.ShapeDtypeStruct((2 * pairs, 2 * HEAD_DIM, width), blocks.dtype))
        scratch += [pltpu.SemaphoreType.DMA((pairs,))] * 4
    return pl.pallas_call(
        functools.partial(to_units_kernel, cols, pairs, with_kv),
        out_shape=out_shape,
        in_specs=[pl.BlockSpec(memory_space=pl.ANY)],
        out_specs=[pl.BlockSpec(memory_space=pl.ANY)] * len(out_shape),
        scratch_shapes=scratch,
        compiler_params=pltpu.CompilerParams(collective_id=collective_id, has_side_effects=True),
    )(blocks)


def project_kernel(
    cols, x_ref, gain_ref, cos_ref, sin_ref, w_far, normed_ref, scale_ref, q_out, kv_out,
    stage, w_ref, q_send, q_recv, kv_send, kv_recv, fwd_send, fwd_recv, own_sem,
):
    me = flat_index(cols)
    core, pair = lax.rem(me, 2), lax.div(me, 2)
    holds, unit = unit_place(pair)
    sibling = me + 1 - 2 * core
    pairs, heads = q_out.shape[0], stage.shape[0]
    barrier = pltpu.get_barrier_semaphore()
    width = heads * HEAD_DIM
    weights = pltpu.make_async_copy(w_far, w_ref, own_sem.at[2])
    weights.start()

    @pl.when(holds)
    def _():
        loop(1, pairs, lambda s: greet(lax.rem(pair + s, pairs) * 2 + core, cols))
        greet(sibling, cols)

    rows = x_ref[...]
    scale = lax.rsqrt(jnp.mean(rows * rows, axis=-1, keepdims=True) + EPSILON)
    normed = (rows * scale * gain_ref[...]).astype(jnp.bfloat16)
    scale_ref[...] = scale
    normed_ref[...] = normed
    cosine, sine = cos_ref[...], sin_ref[...]
    half = HEAD_DIM // 2
    q_rows, kv_rows = pl.ds(0, HEAD_DIM), pl.ds(HEAD_DIM, 2 * HEAD_DIM)

    def q_far(u, holder):
        return remote(
            stage.at[u, q_rows], q_out.at[pair], q_send.at[u], q_recv.at[pair], holder * 2 + core,
            cols,
        )

    def kv_far(u, holder):
        return remote(
            stage.at[u, kv_rows], kv_out.at[me], kv_send.at[u], kv_recv.at[pair],
            holder * 2 + core, cols,
        )

    q_own = pltpu.make_async_copy(stage.at[unit, q_rows], q_out.at[pair], own_sem.at[0])
    kv_own = pltpu.make_async_copy(stage.at[unit, kv_rows], kv_out.at[me], own_sem.at[1])

    def forward(source):
        block = kv_out.at[source * 2 + core]
        return remote(block, block, fwd_send.at[source], fwd_recv.at[source], sibling, cols)

    weights.wait()
    per = TILE // HEAD_DIM
    for group in range(heads // per):
        for part in range(3):
            at = pl.ds(part * width + group * TILE, TILE)
            turned = dot(normed, w_ref[:, at], (1, 0)).T
            for k in range(per):
                head = group * per + k
                low = part * HEAD_DIM
                block = turned[k * HEAD_DIM : (k + 1) * HEAD_DIM]
                if part < 2:
                    first, second = block[:half], block[half:]
                    block = jnp.concatenate(
                        [first * cosine - second * sine, second * cosine + first * sine], axis=0
                    )
                stage[head, low : low + HEAD_DIM, :] = block.astype(jnp.bfloat16)
        if group == 0:
            pl.when(holds)(lambda: pl.semaphore_wait(barrier, heads))
            pl.when(jnp.logical_not(holds))(lambda: pl.semaphore_wait(barrier, heads))
        for k in range(per):
            u = group * per + k
            holder = u // 3 * 4 + u % 3

            @pl.when(pair != holder)
            def _(u=u, holder=holder):
                kv_far(u, holder).start()
                q_far(u, holder).start()

            @pl.when(pair == holder)
            def _():
                kv_own.start()
                q_own.start()

    @pl.when(holds)
    def _():
        kv_own.wait()
        forward(pair).start()

        def take(s):
            source = lax.rem(pair - s + pairs, pairs)
            arrival = remote(
                stage.at[unit, kv_rows], kv_out.at[source * 2 + core], kv_send.at[unit],
                kv_recv.at[source], source * 2 + core, cols,
            )
            arrival.wait_recv()
            forward(source).start()

        loop(1, pairs, take)

        def take_q(s):
            source = lax.rem(pair - s + pairs, pairs)
            remote(
                stage.at[unit, q_rows], q_out.at[source], q_send.at[unit], q_recv.at[source],
                source * 2 + core, cols,
            ).wait_recv()

        loop(1, pairs, take_q)
        loop(0, pairs, lambda source: forward(source).wait())
        q_own.wait()

    def sent(u, holder):
        kv_far(u, holder).wait_send()
        q_far(u, holder).wait_send()

    other_units(pairs, pair, sent)


def project(rows, gain, weights, cosine, sine, cols, collective_id):
    tokens, width = rows.shape
    heads = width // HEAD_DIM
    pairs = heads // 3 * 4
    by_pair, by_unit = pltpu.SemaphoreType.DMA((pairs,)), pltpu.SemaphoreType.DMA((heads,))
    vmem = pl.BlockSpec(memory_space=pltpu.VMEM)
    everywhere = pl.BlockSpec(memory_space=pl.ANY)
    return pl.pallas_call(
        functools.partial(project_kernel, cols),
        out_shape=[
            jax.ShapeDtypeStruct((tokens, width), jnp.bfloat16),
            jax.ShapeDtypeStruct((tokens, 1), jnp.float32),
            jax.ShapeDtypeStruct((pairs, HEAD_DIM, tokens), jnp.bfloat16),
            jax.ShapeDtypeStruct((2 * pairs, 2 * HEAD_DIM, tokens), jnp.bfloat16),
        ],
        in_specs=[vmem] * 4 + [everywhere],
        out_specs=[vmem, vmem, everywhere, everywhere],
        scratch_shapes=[
            pltpu.VMEM((heads, 3 * HEAD_DIM, tokens), jnp.bfloat16),
            pltpu.VMEM(weights.shape, weights.dtype),
            by_unit,
            by_pair,
            by_unit,
            by_pair,
            by_pair,
            by_pair,
            pltpu.SemaphoreType.DMA((3,)),
        ],
        compiler_params=pltpu.CompilerParams(
            collective_id=collective_id, has_side_effects=True, vmem_limit_bytes=40 * 2**20
        ),
    )(rows, gain.reshape(1, width), cosine, sine, weights)


def to_tokens_kernel(cols, pairs, with_kv, *refs):
    if with_kv:
        q_in, kv_in, q_out, kv_out, send, recv, own_sem = refs[:7]
        stage, inbox, kv_send, kv_recv, near_send, near_recv = refs[7:]
    else:
        q_in, q_out, send, recv, own_sem = refs
    me, core, pair, holds, unit = greet_units(cols, pairs, with_kv, False)

    def far(s):
        other = lax.rem(pair + s, pairs)
        target = other * 2 + core
        copies = [remote(q_in.at[other], q_out.at[unit], send.at[s], recv.at[s], target, cols)]
        if with_kv:
            copies.append(
                remote(
                    stage.at[other], kv_out.at[unit], kv_send.at[s], kv_recv.at[s], target, cols
                )
            )
        return copies

    def own():
        copies = [pltpu.make_async_copy(q_in.at[pair], q_out.at[unit], own_sem.at[0])]
        if with_kv:
            copies.append(pltpu.make_async_copy(stage.at[pair], kv_out.at[unit], own_sem.at[1]))
        return copies

    def near(s):
        other = lax.rem(pair + s, pairs)
        return remote(
            kv_in.at[other * 2 + 1 - core],
            inbox.at[other],
            near_send.at[s],
            near_recv.at[s],
            me + 1 - 2 * core,
            cols,
        )

    def add(s):
        other = lax.rem(pair + s, pairs)
        total = kv_in[other * 2 + core].astype(jnp.float32) + inbox[other].astype(jnp.float32)
        stage[other] = total.astype(stage.dtype)

    @pl.when(holds)
    def _():
        if with_kv:
            loop(1, pairs, lambda s: near(s).start())
            near(0).start()

        def give(s):
            if with_kv:
                near(s).wait_recv()
                add(s)
            for copy in far(s):
                copy.start()

        loop(1, pairs, give)
        if with_kv:
            near(0).wait_recv()
            add(0)
        for copy in own():
            copy.start()
        for copy in own():
            copy.wait()

    def take(s):
        def run():
            for copy in far(s):
                copy.wait_recv()

        pl.when(unit_place(lax.rem(pair - s + pairs, pairs))[0])(run)

    loop(1, pairs, take)

    @pl.when(holds)
    def _():
        def sent(s):
            for copy in far(s):
                copy.wait_send()

        loop(1, pairs, sent)
        if with_kv:
            loop(0, pairs, lambda s: near(s).wait_send())


def to_tokens(arrays, cols, collective_id):
    with_kv = len(arrays) == 2
    pairs, _, width = arrays[0].shape
    units = pairs // 4 * 3
    out_shape = [jax.ShapeDtypeStruct((units, HEAD_DIM, width), arrays[0].dtype)]
    in_specs = [pl.BlockSpec(memory_space=pl.ANY)]
    scratch = [
        pltpu.SemaphoreType.DMA((pairs,)),
        pltpu.SemaphoreType.DMA((pairs,)),
        pltpu.SemaphoreType.DMA((2,)),
    ]
    if with_kv:
        out_shape.append(jax.ShapeDtypeStruct((units, 2 * HEAD_DIM, width), arrays[1].dtype))
        in_specs.append(pl.BlockSpec(memory_space=pltpu.VMEM))
        scratch += [pltpu.VMEM((pairs, 2 * HEAD_DIM, width), arrays[1].dtype)] * 2
        scratch += [pltpu.SemaphoreType.DMA((pairs,))] * 4
    return pl.pallas_call(
        functools.partial(to_tokens_kernel, cols, pairs, with_kv),
        out_shape=out_shape,
        in_specs=in_specs,
        out_specs=[pl.BlockSpec(memory_space=pl.ANY)] * len(out_shape),
        scratch_shapes=scratch,
        compiler_params=pltpu.CompilerParams(
            collective_id=collective_id, has_side_effects=True, vmem_limit_bytes=48 * 2**20
        ),
    )(*arrays)


def wide_of(first, blocks):
    return pl.ds(pl.multiple_of(first * TILE, TILE), blocks * TILE)


def in_reach(first, shape, place, run):
    key_pos = first * TILE + lax.broadcasted_iota(jnp.int32, shape, 0)
    return (key_pos <= place) & (key_pos >= run)


def tile_reach(tile, core, width, wide, masked, blocks):
    joined = TILE // width
    low = (2 * tile * joined + core) * width
    high = low + (2 * joined - 1) * width - 1
    prompt = low < PROMPT
    full = jnp.where(prompt, low // (TILE * wide), PROMPT // (TILE * wide))
    back = jnp.maximum((low - LONGEST + 1) // TILE, PROMPT // TILE)
    first = jnp.where(prompt, full * wide, back)
    steps = (high // TILE + masked - first) // masked
    first = jnp.minimum(first, blocks - steps * masked)
    lane = lax.broadcasted_iota(jnp.int32, (1, TILE), 1)
    place = low + lane + lane // width * width
    return full, first, steps, place


CHUNK = 64


def fill_rows(kv_ref, first_row, rows):
    def fill(b):
        rows[wide_of(b, 1), :] = kv_ref[b, first_row : first_row + HEAD_DIM, :].T

    loop(0, kv_ref.shape[0], fill)


def forward_tile(tile, core, width, queries, run, kv_ref, key_rows, kept):
    full, start, steps, place = tile_reach(
        tile, core, width, FWD_WIDE, FWD_MASK, kv_ref.shape[0]
    )

    def by_eight(value):
        return value.reshape(-1, 8, TILE)

    def fold(blocks, first, state, masked):
        top, total, gathered = state
        base = pl.multiple_of(first * TILE, TILE)
        highest = top
        for c in range(blocks * TILE // CHUNK):
            scores = jnp.dot(
                key_rows[pl.ds(base + c * CHUNK, CHUNK), :],
                queries,
                preferred_element_type=jnp.float32,
            )
            if masked:
                key_pos = base + c * CHUNK + lax.broadcasted_iota(jnp.int32, scores.shape, 0)
                scores = jnp.where((key_pos <= place) & (key_pos >= run), scores, NEGATIVE)
            kept[c * CHUNK : (c + 1) * CHUNK, :] = scores
            highest = jnp.maximum(highest, jnp.max(by_eight(scores), axis=0))
        new_top = jnp.broadcast_to(jnp.max(highest, axis=0, keepdims=True), (8, TILE))
        shrink = jnp.exp2((top - new_top) * EXP_SCALE)
        total = total * shrink
        gathered = (by_eight(gathered) * shrink[None]).reshape(HEAD_DIM, TILE)
        for j in range(blocks):
            low = []
            for c in range(j * TILE // CHUNK, (j + 1) * TILE // CHUNK):
                scores = by_eight(kept[c * CHUNK : (c + 1) * CHUNK, :])
                weights = jnp.exp2((scores - new_top[None]) * EXP_SCALE)
                total = total + jnp.sum(weights, axis=0)
                low.append(weights.reshape(CHUNK, TILE).astype(jnp.bfloat16))
            gathered = gathered + jnp.dot(
                kv_ref[first + j, HEAD_DIM : 2 * HEAD_DIM, :],
                jnp.concatenate(low, axis=0),
                preferred_element_type=jnp.float32,
            )
        return (new_top, total, gathered)

    state = (
        jnp.full((8, TILE), NEGATIVE, jnp.float32),
        jnp.zeros((8, TILE), jnp.float32),
        jnp.zeros((HEAD_DIM, TILE), jnp.float32),
    )
    state = lax.fori_loop(0, full, lambda b, s: fold(FWD_WIDE, b * FWD_WIDE, s, False), state)
    top, total, gathered = lax.fori_loop(
        0, steps, lambda b, s: fold(FWD_MASK, start + b * FWD_MASK, s, True), state
    )
    total = jnp.sum(total, axis=0, keepdims=True)
    exact = gathered / total
    return exact, exact.astype(jnp.bfloat16), top[0:1] * EXP_SCALE + jnp.log2(total)


def forward_scratch(blocks):
    return [
        pltpu.VMEM((blocks * TILE, HEAD_DIM), jnp.bfloat16),
        pltpu.VMEM((max(FWD_WIDE, FWD_MASK) * TILE, TILE), jnp.float32),
    ]


def my_unit():
    me = flat_index(lax.axis_size("blk"))
    pair = lax.div(me, 2)
    holds, unit = unit_place(pair)
    return me, lax.rem(me, 2), pair, holds, unit


def forward_kernel(width, q_ref, kv_ref, run_ref, o_ref, ob_ref, lse_ref, key_rows, kept):
    tile = pl.program_id(0)
    _, core, _, holds, _ = my_unit()

    @pl.when(holds & (tile == 0))
    def _():
        fill_rows(kv_ref, 0, key_rows)

    @pl.when(holds)
    def _():
        o_ref[0], ob_ref[0], lse_ref[0] = forward_tile(
            tile, core, width, q_ref[0], run_ref[0], kv_ref, key_rows, kept
        )


def tile_spec(rows):
    return pl.BlockSpec((1, rows, TILE), lambda i: (i, 0, 0))


def attend(queries, keys_values, run, width):
    tiles = queries.shape[0]
    held = pl.BlockSpec(keys_values.shape, lambda i: (0, 0, 0))
    return pl.pallas_call(
        functools.partial(forward_kernel, width),
        grid=(tiles,),
        in_specs=[tile_spec(HEAD_DIM), held, tile_spec(1)],
        out_specs=[tile_spec(HEAD_DIM), tile_spec(HEAD_DIM), tile_spec(1)],
        scratch_shapes=forward_scratch(keys_values.shape[0]),
        out_shape=[
            jax.ShapeDtypeStruct((tiles, HEAD_DIM, TILE), jnp.float32),
            jax.ShapeDtypeStruct((tiles, HEAD_DIM, TILE), jnp.bfloat16),
            jax.ShapeDtypeStruct((tiles, 1, TILE), jnp.float32),
        ],
        compiler_params=pltpu.CompilerParams(vmem_limit_bytes=48 * 2**20),
    )(queries, keys_values, run)


def other_units(pairs, pair, action):
    def one(u):
        holder = lax.div(u, 3) * 4 + lax.rem(u, 3)
        pl.when(holder != pair)(lambda: action(u, holder))

    loop(0, pairs // 4 * 3, one)


def gathers_of(sources, results, sems, depths):
    return [
        Gather(
            source,
            results[i],
            sems[GATHER_SEMS * i : GATHER_SEMS * (i + 1)],
            depths,
            cut_of(source.shape[-1]),
        )
        for i, source in enumerate(sources)
    ]


GATHER_AT = {"start": 0, "start_own": 0, "spread_near": 8, "spread_far": 12, "settle": 15}


def forward_home_kernel(cols, count, deep, *refs):
    q_ref, kv_ref, run_ref = refs[:3]
    sources, refs = refs[3 : 3 + count + deep], refs[3 + count + deep :]
    o_ref, lse_ref, home = refs[:3]
    results, refs = refs[3 : 3 + count + deep], refs[3 + count + deep :]
    key_rows, kept, low, send, recv, own_sem = refs[:6]
    refs, deep_sems = refs[6 : 6 + GATHER_SEMS * count], refs[6 + GATHER_SEMS * count :]
    gathers = gathers_of(sources[:count], results[:count], refs, cols // 4)
    depth_gathers = [
        DepthGather(sources[count + i], results[count + i], deep_sems[3 * i : 3 * i + 3], cols // 4)
        for i in range(deep)
    ]
    tile, tiles = pl.program_id(0), tiles_of(kv_ref)
    me, core, pair, holds, unit = my_unit()

    @pl.when(tile == 0)
    def _():
        loop(1, tiles, lambda s: greet(lax.rem(pair + s, tiles) * 2 + core, cols))
        greet(me + 1 - 2 * core, cols)

    @pl.when(holds & (tile == 0))
    def _():
        fill_rows(kv_ref, 0, key_rows)

    @pl.when(tile == 0)
    def _():
        pl.semaphore_wait(pltpu.get_barrier_semaphore(), tiles)

    for name, place_at in GATHER_AT.items():

        @pl.when(tile == place_at)
        def _(name=name):
            for gather in gathers:
                getattr(gather, name)()

    @pl.when(tile == GATHER_AT["spread_near"])
    def _():
        for gather in depth_gathers:
            gather.start()

    def away(t):
        return remote(
            low.at[t], home.at[unit], send.at[t], recv.at[unit], t * 2 + core, cols
        )

    stays = pltpu.make_async_copy(low.at[pair], home.at[unit], own_sem)

    @pl.when(holds)
    def _():
        o_ref[0], low[tile], lse_ref[0] = forward_tile(
            tile, core, TILE, q_ref[0], run_ref[0], kv_ref, key_rows, kept
        )
        pl.when(tile != pair)(lambda: away(tile).start())
        pl.when(tile == pair)(lambda: stays.start())

    @pl.when(tile == tiles - 1)
    def _():
        for gather in gathers + depth_gathers:
            gather.finish()

        def arrived(u, holder):
            remote(
                low.at[pair], home.at[u], send.at[pair], recv.at[u], holder * 2 + core, cols
            ).wait_recv()

        other_units(tiles, pair, arrived)

        @pl.when(holds)
        def _():
            def sent(t):
                pl.when(t != pair)(lambda: away(t).wait_send())

            loop(0, tiles, sent)
            stays.wait()


def tiles_of(kv_ref):
    return kv_ref.shape[0] // 2


def attend_home(queries, keys_values, run, shards, deep, cols, collective_id):
    tiles, units, depths = queries.shape[0], queries.shape[0] // 4 * 3, cols // 4
    held = pl.BlockSpec(keys_values.shape, lambda i: (0, 0, 0))
    everywhere = pl.BlockSpec(memory_space=pl.ANY)
    return pl.pallas_call(
        functools.partial(forward_home_kernel, cols, len(shards), len(deep)),
        grid=(tiles,),
        in_specs=[tile_spec(HEAD_DIM), held, tile_spec(1)] + [everywhere] * (len(shards) + len(deep)),
        out_specs=[tile_spec(HEAD_DIM), tile_spec(1), everywhere] + [everywhere] * (len(shards) + len(deep)),
        scratch_shapes=forward_scratch(keys_values.shape[0])
        + [
            pltpu.VMEM((tiles, HEAD_DIM, TILE), jnp.bfloat16),
            pltpu.SemaphoreType.DMA((tiles,)),
            pltpu.SemaphoreType.DMA((units,)),
            pltpu.SemaphoreType.DMA,
        ]
        + gather_sems(depths) * len(shards)
        + depth_sems(depths) * len(deep),
        out_shape=[
            jax.ShapeDtypeStruct((tiles, HEAD_DIM, TILE), jnp.float32),
            jax.ShapeDtypeStruct((tiles, 1, TILE), jnp.float32),
            jax.ShapeDtypeStruct((units, HEAD_DIM, TILE), jnp.bfloat16),
        ]
        + [gathered_shape(shard, depths) for shard in shards]
        + [jax.ShapeDtypeStruct((depths,) + shard.shape, shard.dtype) for shard in deep],
        compiler_params=pltpu.CompilerParams(
            collective_id=collective_id, has_side_effects=True, vmem_limit_bytes=48 * 2**20
        ),
    )(queries, keys_values, run, *shards, *deep)


def backward_tile(
    tile, core, width, queries, grads, exact, lse, run,
    kv_ref, key_rows, value_rows, dk_sum, dv_sum,
):
    full, start, steps, place = tile_reach(
        tile, core, width, BWD_WIDE, BWD_MASK, kv_ref.shape[0]
    )
    delta = jnp.sum(grads.astype(jnp.float32) * exact, axis=0, keepdims=True)
    over_queries = (((1,), (1,)), ((), ()))

    def fold(blocks, first, dq, masked):
        rows = wide_of(first, blocks)
        scores = jnp.dot(key_rows[rows, :], queries, preferred_element_type=jnp.float32)
        probs = jnp.exp2(scores * EXP_SCALE - lse)
        if masked:
            probs = jnp.where(in_reach(first, scores.shape, place, run), probs, 0.0)
        dp = jnp.dot(value_rows[rows, :], grads, preferred_element_type=jnp.float32)
        ds = (probs * (dp - delta)).astype(jnp.bfloat16)
        low = probs.astype(jnp.bfloat16)
        for j in range(blocks):
            part = slice(j * TILE, (j + 1) * TILE)
            dv_sum[first + j] += lax.dot_general(
                grads, low[part], over_queries, preferred_element_type=jnp.float32
            )
            dk_sum[first + j] += lax.dot_general(
                queries, ds[part], over_queries, preferred_element_type=jnp.float32
            )
            dq = dq + jnp.dot(
                kv_ref[first + j, 0:HEAD_DIM, :], ds[part], preferred_element_type=jnp.float32
            )
        return dq

    dq = jnp.zeros((HEAD_DIM, TILE), jnp.float32)
    dq = lax.fori_loop(0, full, lambda b, s: fold(BWD_WIDE, b * BWD_WIDE, s, False), dq)
    dq = lax.fori_loop(0, steps, lambda b, s: fold(BWD_MASK, start + b * BWD_MASK, s, True), dq)
    return (dq * SCORE_SCALE).astype(jnp.bfloat16)


def backward_begin(kv_ref, key_rows, value_rows, dk_sum, dv_sum):
    fill_rows(kv_ref, 0, key_rows)
    fill_rows(kv_ref, HEAD_DIM, value_rows)

    def clear(b):
        dk_sum[b] = jnp.zeros((HEAD_DIM, TILE), jnp.float32)
        dv_sum[b] = jnp.zeros((HEAD_DIM, TILE), jnp.float32)

    loop(0, kv_ref.shape[0], clear)


def backward_end(dk_sum, dv_sum, dkv, first, last):
    def drain(b):
        dkv[b, 0:HEAD_DIM, :] = (dk_sum[b] * SCORE_SCALE).astype(jnp.bfloat16)
        dkv[b, HEAD_DIM : 2 * HEAD_DIM, :] = dv_sum[b].astype(jnp.bfloat16)

    loop(first, last, drain)


def backward_scratch(blocks):
    return [pltpu.VMEM((blocks * TILE, HEAD_DIM), jnp.bfloat16)] * 2 + [
        pltpu.VMEM((blocks, HEAD_DIM, TILE), jnp.float32)
    ] * 2


NEAR_AT, MIDDLE_AT, FAR_AT = (0, 2, 4, 6), (2, 4, 6, 8), (3, 5, 7, 9)


def reduce_at(step, reduces, depths):
    quarter = depths // 4
    for name, places in (("far", FAR_AT), ("middle", MIDDLE_AT), ("near", NEAR_AT)):
        for part, place_at in enumerate(places):

            @pl.when(step == place_at)
            def _(name=name, part=part):
                for reduce in reduces:
                    getattr(reduce, name)(part * quarter, (part + 1) * quarter)


def backward_kernel(width, depths, count, *refs):
    q_ref, kv_ref, do_ref, o_ref, lse_ref, run_ref = refs[:6]
    parts, refs = refs[6 : 6 + count], refs[6 + count :]
    dq_ref, dkv_ref = refs[:2]
    totals, refs = refs[2 : 2 + count], refs[2 + count :]
    held = refs[:4]
    reduces = reduces_of(parts, totals, refs[4:], depths)
    tile, tiles = pl.program_id(0), pl.num_programs(0)
    _, core, _, holds, _ = my_unit()

    @pl.when(tile == 0)
    def _():
        greet_mesh(depths)
        for reduce in reduces:
            reduce.start()

    reduce_at(tile, reduces, depths)

    @pl.when(holds & (tile == 0))
    def _():
        backward_begin(kv_ref, *held)

    @pl.when(holds)
    def _():
        dq_ref[0] = backward_tile(
            tile, core, width, q_ref[0], do_ref[0], o_ref[0], lse_ref[0], run_ref[0],
            kv_ref, *held,
        )

    @pl.when(holds & (tile == tiles - 1))
    def _():
        backward_end(held[2], held[3], dkv_ref, 0, dkv_ref.shape[0])

    @pl.when(tile == tiles - 1)
    def _():
        for reduce in reduces:
            reduce.finish()


def attend_back(queries, keys_values, grads, exact, lse, run, width, parts, cols, collective_id):
    tiles, blocks = queries.shape[0], keys_values.shape[0]
    held = pl.BlockSpec(keys_values.shape, lambda i: (0, 0, 0))
    wide, flat = tile_spec(HEAD_DIM), tile_spec(1)
    depths = cols // 4
    return pl.pallas_call(
        functools.partial(backward_kernel, width, depths, len(parts)),
        grid=(tiles,),
        in_specs=[wide, held, wide, wide, flat, flat]
        + [pl.BlockSpec(memory_space=pl.ANY)] * len(parts),
        out_specs=[wide, held]
        + [pl.BlockSpec(part.shape[-2:], lambda i: (0, 0)) for part in parts],
        scratch_shapes=backward_scratch(blocks) + all_reduce_scratch(parts, depths),
        out_shape=[
            jax.ShapeDtypeStruct(queries.shape, jnp.bfloat16),
            jax.ShapeDtypeStruct(keys_values.shape, jnp.bfloat16),
        ]
        + [jax.ShapeDtypeStruct(part.shape[-2:], jnp.float32) for part in parts],
        compiler_params=pltpu.CompilerParams(
            collective_id=collective_id, has_side_effects=True, vmem_limit_bytes=52 * 2**20
        ),
    )(queries, keys_values, grads, exact, lse, run, *parts)


def backward_home_kernel(cols, depths, count, *refs):
    q_ref, kv_ref, o_ref, lse_ref, run_ref, do_source = refs[:6]
    parts, refs = refs[6 : 6 + count], refs[6 + count :]
    q_home, kv_home = refs[:2]
    totals, refs = refs[2 : 2 + count], refs[2 + count :]
    held, refs = refs[:4], refs[4:]
    grads, low, dkv, inbox, refs = refs[0], refs[1], refs[2], refs[3], refs[4:]
    in_send, in_recv, q_send, q_recv, kv_send, kv_recv, near_send, near_recv, own_sem = refs[:9]
    reduces = reduces_of(parts, totals, refs[9:], depths)
    step, pairs = pl.program_id(0), tiles_of(kv_ref)
    tile = pairs - 1 - step
    me, core, pair, holds, unit = my_unit()
    sibling = me + 1 - 2 * core
    last = tile == 0

    def do_out(u, holder):
        return remote(
            do_source.at[u], grads.at[pair], in_send.at[u], in_recv.at[pair], holder * 2 + core, cols
        )

    def do_in(t):
        return remote(
            do_source.at[unit], grads.at[t], in_send.at[unit], in_recv.at[t], t * 2 + core, cols
        )

    def q_away(t):
        return remote(low.at[t], q_home.at[unit], q_send.at[t], q_recv.at[unit], t * 2 + core, cols)

    def kv_away(t):
        return remote(
            inbox.at[t], kv_home.at[unit], kv_send.at[t], kv_recv.at[unit], t * 2 + core, cols
        )

    def near(t):
        return remote(
            dkv.at[t * 2 + 1 - core], inbox.at[t], near_send.at[t], near_recv.at[t], sibling, cols
        )

    do_own = pltpu.make_async_copy(do_source.at[unit], grads.at[pair], own_sem.at[0])
    q_stays = pltpu.make_async_copy(low.at[pair], q_home.at[unit], own_sem.at[1])
    kv_stays = pltpu.make_async_copy(inbox.at[pair], kv_home.at[unit], own_sem.at[2])

    def give(t):
        near(t).wait_recv()
        inbox[t] = dkv[t * 2 + core] + inbox[t]
        pl.when(t != pair)(lambda: kv_away(t).start())
        pl.when(t == pair)(lambda: kv_stays.start())

    @pl.when(step == 0)
    def _():
        loop(1, pairs, lambda s: greet(lax.rem(pair + s, pairs) * 2 + core, cols))
        greet(sibling, cols)
        pl.semaphore_wait(pltpu.get_barrier_semaphore(), pairs)
        other_units(pairs, pair, lambda u, holder: do_out(u, holder).start())
        pl.when(holds)(lambda: do_own.start())
        for reduce in reduces:
            reduce.start()

    @pl.when(holds & (step == 0))
    def _():
        backward_begin(kv_ref, *held)

    reduce_at(step, reduces, depths)

    @pl.when(holds)
    def _():
        pl.when(tile != pair)(lambda: do_in(tile).wait_recv())
        pl.when(tile == pair)(lambda: do_own.wait())
        low[tile] = backward_tile(
            tile, core, TILE, q_ref[0], grads[tile], o_ref[0], lse_ref[0], run_ref[0],
            kv_ref, *held,
        )
        pl.when(tile != pair)(lambda: q_away(tile).start())
        pl.when(tile == pair)(lambda: q_stays.start())
        backward_end(held[2], held[3], dkv, 2 * tile, 2 * tile + 2)
        near(tile).start()
        pl.when(step > 0)(lambda: give(tile + 1))
        pl.when(last)(lambda: give(tile))

    @pl.when(last)
    def _():
        for reduce in reduces:
            reduce.finish()

        def arrived(u, holder):
            target = holder * 2 + core
            remote(
                low.at[pair], q_home.at[u], q_send.at[pair], q_recv.at[u], target, cols
            ).wait_recv()
            remote(
                inbox.at[pair], kv_home.at[u], kv_send.at[pair], kv_recv.at[u], target, cols
            ).wait_recv()

        other_units(pairs, pair, arrived)
        other_units(pairs, pair, lambda u, holder: do_out(u, holder).wait_send())

        @pl.when(holds)
        def _():
            def sent(t):
                near(t).wait_send()

                @pl.when(t != pair)
                def _():
                    q_away(t).wait_send()
                    kv_away(t).wait_send()

            loop(0, pairs, sent)
            q_stays.wait()
            kv_stays.wait()


def attend_back_home(queries, keys_values, do_blocks, exact, lse, run, parts, cols, collective_id):
    tiles, blocks = queries.shape[0], keys_values.shape[0]
    units, depths = do_blocks.shape[0], cols // 4
    held = pl.BlockSpec(keys_values.shape, lambda i: (0, 0, 0))
    wide = pl.BlockSpec((1, HEAD_DIM, TILE), lambda i: (tiles - 1 - i, 0, 0))
    flat = pl.BlockSpec((1, 1, TILE), lambda i: (tiles - 1 - i, 0, 0))
    everywhere = pl.BlockSpec(memory_space=pl.ANY)
    by_tile, by_unit = pltpu.SemaphoreType.DMA((tiles,)), pltpu.SemaphoreType.DMA((units,))
    tile_rows = pltpu.VMEM((tiles, HEAD_DIM, TILE), jnp.bfloat16)
    return pl.pallas_call(
        functools.partial(backward_home_kernel, cols, depths, len(parts)),
        grid=(tiles,),
        in_specs=[wide, held, wide, flat, flat, everywhere] + [everywhere] * len(parts),
        out_specs=[everywhere, everywhere]
        + [pl.BlockSpec(part.shape[-2:], lambda i: (0, 0)) for part in parts],
        scratch_shapes=backward_scratch(blocks)
        + [
            tile_rows,
            tile_rows,
            pltpu.VMEM((blocks, 2 * HEAD_DIM, TILE), jnp.bfloat16),
            pltpu.VMEM((tiles, 2 * HEAD_DIM, TILE), jnp.bfloat16),
            by_unit,
            by_tile,
            by_tile,
            by_unit,
            by_tile,
            by_unit,
            by_tile,
            by_tile,
            pltpu.SemaphoreType.DMA((3,)),
        ]
        + all_reduce_scratch(parts, depths),
        out_shape=[
            jax.ShapeDtypeStruct((units, HEAD_DIM, TILE), jnp.bfloat16),
            jax.ShapeDtypeStruct((units, 2 * HEAD_DIM, TILE), jnp.bfloat16),
        ]
        + [jax.ShapeDtypeStruct(part.shape[-2:], jnp.float32) for part in parts],
        compiler_params=pltpu.CompilerParams(
            collective_id=collective_id, has_side_effects=True, vmem_limit_bytes=52 * 2**20
        ),
    )(queries, keys_values, exact, lse, run, do_blocks, *parts)


def to_tiles(blocks):
    count, rows, width = blocks.shape
    if width == TILE:
        return blocks
    joined = TILE // width
    return (
        blocks.reshape(count // joined, joined, rows, width)
        .transpose(0, 2, 1, 3)
        .reshape(count // joined, rows, TILE)
    )


def from_tiles(tiles, width):
    count, rows, _ = tiles.shape
    if width == TILE:
        return tiles
    joined = TILE // width
    return (
        tiles.reshape(count, rows, joined, width)
        .transpose(0, 2, 1, 3)
        .reshape(count * joined, rows, width)
    )


def dot(left, right, over):
    return lax.dot_general(
        left, right, (((over[0],), (over[1],)), ((), ())), preferred_element_type=jnp.float32
    )


STRIP = 512


def strips(total, body):
    width = min(total, STRIP)
    loop(0, total // width, lambda j: body(pl.ds(pl.multiple_of(j * width, width), width)))


def shared_forward(ins, outs, done):
    normed, wide, down = ins
    gate_in, up_in, hidden_low, total = outs
    hidden = down.shape[0]

    def strip(at):
        after = pl.ds(at.start + hidden, at.size)
        gate = dot(normed[...], wide[:, at], (1, 0))
        up = dot(normed[...], wide[:, after], (1, 0))
        gate_in[:, at] = gate.astype(jnp.bfloat16)
        up_in[:, at] = up.astype(jnp.bfloat16)
        hidden_low[:, at] = (apply_silu(gate) * up).astype(jnp.bfloat16)

    strips(hidden, strip)
    for start in done[:3]:
        start()
    total[...] = dot(hidden_low[...], down[...], (1, 0))
    done[3]()


def shared_backward(ins, outs, done):
    grads, normed, gate_in, up_in, hidden_low, wide, down = ins
    grad_wide, grad_down, back = outs
    hidden = down.shape[0]
    normed_t = normed[...].T
    back[...] = jnp.zeros_like(back)

    def strip(at):
        after = pl.ds(at.start + hidden, at.size)
        upstream = dot(grads[...], down[at, :], (1, 1))
        gate, up = gate_in[:, at].astype(jnp.float32), up_in[:, at].astype(jnp.float32)
        low_gate = (upstream * up * silu_slope(gate)).astype(jnp.bfloat16)
        low_up = (upstream * apply_silu(gate)).astype(jnp.bfloat16)
        back[...] += dot(low_gate, wide[:, at], (1, 1)) + dot(low_up, wide[:, after], (1, 1))
        grad_wide[:, at] = dot(normed_t, low_gate, (1, 0)).astype(jnp.bfloat16)
        grad_wide[:, after] = dot(normed_t, low_up, (1, 0)).astype(jnp.bfloat16)
        grad_down[at, :] = dot(hidden_low[:, at].T, grads[...], (1, 0)).astype(jnp.bfloat16)

    strips(hidden, strip)
    for start in done:
        start()


QUARTERS = 4


def quarter_order(pair, per):
    own = lax.div(pair, per)
    outer, inner = lax.div(own, 2), lax.rem(own, 2)
    return [own, (1 - outer) * 2 + inner, outer * 2 + 1 - inner, (1 - outer) * 2 + 1 - inner]


def expert_kernel(cols, step, final, work_first, work, shapes, *refs):
    held_in, held_out, extra, plane = shapes
    sending, refs = refs[0], refs[1:]
    plane_in, refs = refs[:plane], refs[plane:]
    inputs, refs = refs[:held_in], refs[held_in:]
    extra_in = len(work.arrays)
    work_in, refs = refs[:extra_in], refs[extra_in:]
    returned, refs = refs[0], refs[1:]
    plane_out, refs = refs[:plane], refs[plane:]
    outputs, refs = refs[:held_out], refs[held_out:]
    work_out, refs = refs[: len(work.out_shape)], refs[len(work.out_shape) :]
    land, partial, inbox, refs = refs[0], refs[1], refs[2], refs[3:]
    send, recv, share_send, share_recv, near_send, near_recv, refs = refs[:6] + (refs[6:],)
    back_send, back_recv, own_sem, load_sem, refs = refs[:4] + (refs[4:],)
    held, refs = refs[:held_in], refs[held_in:]
    scratch, refs = refs[:extra], refs[extra:]
    plane_sems, refs = refs[: GATHER_SEMS * plane], refs[GATHER_SEMS * plane :]
    planes = [
        PlaneGather(
            plane_in[i],
            plane_out[i],
            plane_sems[GATHER_SEMS * i : GATHER_SEMS * (i + 1)],
            cols // 4,
            cut_of(plane_in[i].shape[-1]),
        )
        for i in range(plane)
    ]
    begin, run, end = work.bind(work_in + work_out + refs)

    me = flat_index(cols)
    core, pair = lax.rem(me, 2), lax.div(me, 2)
    pairs = sending.shape[0]
    per = pairs // QUARTERS
    sibling = me + 1 - 2 * core
    order = quarter_order(pair, per)

    loads = [pltpu.make_async_copy(inputs[i], held[i], load_sem.at[i]) for i in range(held_in)]
    for copy in loads:
        copy.start()
    begin()

    loop(1, pairs, lambda s: greet(lax.rem(pair + s, pairs) * 2 + core, cols))
    greet(sibling, cols)
    pl.semaphore_wait(pltpu.get_barrier_semaphore(), pairs)

    def out(e):
        return remote(
            sending.at[e], land.at[pair, core], send.at[e], recv.at[pair], e * 2 + core, cols
        )

    def arrival(e):
        return remote(
            sending.at[e], land.at[e, core], send.at[e], recv.at[e], e * 2 + core, cols
        )

    def share(e):
        block = land.at[e, core]
        return remote(block, block, share_send.at[e], share_recv.at[e], sibling, cols)

    def near(quarter):
        rows = pl.ds(quarter * per, per)
        return remote(
            partial.at[rows, 1 - core],
            inbox.at[rows],
            near_send.at[quarter],
            near_recv.at[quarter],
            sibling,
            cols,
        )

    def back(e):
        return remote(
            inbox.at[e], returned.at[pair], back_send.at[e], back_recv.at[pair], e * 2 + core, cols
        )

    def back_arrival(e):
        return remote(
            inbox.at[e], returned.at[e], back_send.at[e], back_recv.at[e], e * 2 + core, cols
        )

    def others(quarter, action):
        def one(k):
            e = quarter * per + k
            pl.when(e != pair)(lambda: action(e))

        loop(0, per, one)

    own_in = pltpu.make_async_copy(sending.at[pair], land.at[pair, core], own_sem.at[0])
    own_back = pltpu.make_async_copy(inbox.at[pair], returned.at[pair], own_sem.at[1])

    for quarter in (order[2], order[0], order[1], order[3]):
        others(quarter, lambda e: out(e).start())
    own_in.start()
    for gather in planes:
        gather.start()
    own_in.wait()
    share(pair).start()
    if work_first:
        run()
    for copy in loads:
        copy.wait()

    def take(quarter):
        def one(e):
            arrival(e).wait_recv()
            share(e).start()

        others(quarter, one)
        loop(0, per, lambda k: share(quarter * per + k).wait_recv())
        step(quarter, per, land, partial, held, scratch)
        near(quarter).start()

    def give(quarter):
        near(quarter).wait_recv()

        def one(k):
            e = quarter * per + k
            inbox[e] = partial[e, core] + inbox[e]
            pl.when(e != pair)(lambda: back(e).start())

        loop(0, per, one)

    take(order[0])
    take(order[1])
    give(order[0])
    give(order[1])
    own_back.start()
    take(order[2])
    give(order[2])
    for gather in planes:
        gather.spread_far()
    take(order[3])
    give(order[3])
    for gather in planes:
        gather.settle()
    if not work_first:
        run()
    final(land, held, scratch, outputs)
    for quarter in order:
        others(quarter, lambda e: out(e).wait_send())
        others(quarter, lambda e: back(e).wait_send())
        others(quarter, lambda e: back_arrival(e).wait_recv())
        loop(0, per, lambda k: share(quarter * per + k).wait_send())
        near(quarter).wait_send()
    own_back.wait()
    for gather in planes:
        gather.finish()
    end()


def expert_pass(
    sending, held, out_shape, extra, step, final, work, work_first, cols, collective_id, plane=()
):
    pairs, slots, width = sending.shape
    block = (pairs, slots, width)
    both = (pairs, 2, slots, width)
    sems = pltpu.SemaphoreType.DMA((pairs,))
    scratch = [
        pltpu.VMEM(both, sending.dtype),
        pltpu.VMEM(both, sending.dtype),
        pltpu.VMEM(block, sending.dtype),
    ]
    scratch += [sems] * 8 + [pltpu.SemaphoreType.DMA((2,)), pltpu.SemaphoreType.DMA((len(held),))]
    scratch += [pltpu.VMEM(a.shape, a.dtype) for a in held] + extra
    scratch += gather_sems(cols // 4) * len(plane) + work.scratch()
    shapes = (len(held), len(out_shape), len(extra), len(plane))
    whole = [gathered_shape(jax.ShapeDtypeStruct(a.shape[1:], a.dtype), cols // 4) for a in plane]
    out_shape = [jax.ShapeDtypeStruct(block, sending.dtype)] + whole + out_shape
    everywhere = pl.BlockSpec(memory_space=pl.ANY)
    return pl.pallas_call(
        functools.partial(expert_kernel, cols, step, final, work_first, work, shapes),
        out_shape=out_shape + work.out_shape,
        in_specs=[everywhere] * (1 + len(plane) + len(held) + len(work.arrays)),
        out_specs=[everywhere] * (len(out_shape) + len(work.out_shape)),
        scratch_shapes=scratch,
        compiler_params=pltpu.CompilerParams(
            collective_id=collective_id, has_side_effects=True, vmem_limit_bytes=52 * 2**20
        ),
    )(sending, *plane, *held, *work.arrays)


def forward_step(quarter, per, land, partial, held, scratch):
    gate, up, down = held
    gate_kept, up_kept, hidden_kept = scratch[:3]
    rows = land[pl.ds(quarter * per, per)].reshape(-1, land.shape[-1])

    def strip(at):
        inner_gate = dot(rows, gate[:, at], (1, 0))
        inner_up = dot(rows, up[:, at], (1, 0))
        gate_kept[quarter, :, at] = inner_gate.astype(jnp.bfloat16)
        up_kept[quarter, :, at] = inner_up.astype(jnp.bfloat16)
        hidden_kept[quarter, :, at] = (apply_silu(inner_gate) * inner_up).astype(jnp.bfloat16)

    strips(gate.shape[1], strip)
    total = dot(hidden_kept[quarter], down[...], (1, 0)).astype(jnp.bfloat16)
    partial[pl.ds(quarter * per, per)] = total.reshape((per,) + partial.shape[1:])


def forward_final(land, held, scratch, outputs):
    sems = scratch[3]
    copies = [
        pltpu.make_async_copy(source, outputs[i], sems.at[i])
        for i, source in enumerate((land,) + tuple(scratch[:3]))
    ]
    for copy in copies:
        copy.start()
    for copy in copies:
        copy.wait()


def expert_forward(sending, gate, up, down, plane, cols, collective_id):
    pairs, slots, width = sending.shape
    kept = (QUARTERS, 2 * pairs * slots // QUARTERS, gate.shape[1])
    out_shape = [jax.ShapeDtypeStruct((pairs, 2, slots, width), sending.dtype)]
    out_shape += [jax.ShapeDtypeStruct(kept, sending.dtype)] * 3
    extra = [pltpu.VMEM(kept, sending.dtype)] * 3 + [pltpu.SemaphoreType.DMA((4,))]
    return expert_pass(
        sending, [gate, up, down], out_shape, extra, forward_step, forward_final,
        Work([], [], lambda ins, outs, done: None), False, cols, collective_id, plane,
    )


def backward_step(quarter, per, land, partial, held, scratch):
    gate, up, down, _, gate_kept, up_kept, _ = held
    grads = land[pl.ds(quarter * per, per)].reshape(-1, land.shape[-1])

    def strip(at):
        upstream = dot(grads, down[at, :], (1, 1))
        inner_gate = gate_kept[quarter, :, at].astype(jnp.float32)
        inner_up = up_kept[quarter, :, at].astype(jnp.float32)
        gate_kept[quarter, :, at] = (upstream * inner_up * silu_slope(inner_gate)).astype(
            jnp.bfloat16
        )
        up_kept[quarter, :, at] = (upstream * apply_silu(inner_gate)).astype(jnp.bfloat16)

    strips(gate.shape[1], strip)
    total = dot(gate_kept[quarter], gate[...], (1, 1)) + dot(up_kept[quarter], up[...], (1, 1))
    partial[pl.ds(quarter * per, per)] = total.astype(jnp.bfloat16).reshape(
        (per,) + partial.shape[1:]
    )


GRAD_STRIP = 256


def backward_final(land, held, scratch, outputs):
    _, _, _, rows, low_gate, low_up, hidden = held
    buffers, sems = scratch
    width, inner = land.shape[-1], hidden.shape[-1]
    row_count = low_gate.shape[0] * low_gate.shape[1]
    started = {}

    def flat(ref):
        return ref[...].reshape(row_count, ref.shape[-1])

    def turned(ref, at):
        lead = ref.shape[:-1]
        return ref[(slice(None),) * len(lead) + (at,)].reshape(row_count, GRAD_STRIP).T

    def store(slot, part, value, target):
        if (slot, part) in started:
            started[slot, part].wait()
        view = buffers.at[slot, part, :, pl.ds(0, value.shape[1])]
        buffers[slot, part, :, 0 : value.shape[1]] = value
        copy = pltpu.make_async_copy(view, target, sems.at[slot, part])
        copy.start()
        started[slot, part] = copy

    for j in range(width // GRAD_STRIP):
        at = slice(j * GRAD_STRIP, (j + 1) * GRAD_STRIP)
        left = turned(rows, at)
        store(j % 2, 0, dot(left, flat(low_gate), (1, 0)), outputs[0].at[at])
        store(j % 2, 1, dot(left, flat(low_up), (1, 0)), outputs[1].at[at])
    for j in range(inner // GRAD_STRIP):
        at = slice(j * GRAD_STRIP, (j + 1) * GRAD_STRIP)
        value = dot(turned(hidden, at), land[...].reshape(row_count, width), (1, 0))
        store(j % 2, j // 2 % 2, value, outputs[2].at[at])
    for copy in started.values():
        copy.wait()


def expert_backward(sending, gate, up, down, kept, work, cols, collective_id):
    out_shape = [jax.ShapeDtypeStruct(w.shape, jnp.float32) for w in (gate, up, down)]
    widest = max(gate.shape[1], down.shape[1])
    extra = [
        pltpu.VMEM((2, 2, GRAD_STRIP, widest), jnp.float32),
        pltpu.SemaphoreType.DMA((2, 2)),
    ]
    return expert_pass(
        sending, [gate, up, down] + list(kept), out_shape, extra, backward_step, backward_final,
        work, True, cols, collective_id,
    )


def on_device(
    hidden_in,
    w_query,
    w_key,
    w_value,
    w_out,
    norm_attn,
    norm_ffn,
    w_router,
    shared_gate,
    shared_up,
    shared_down,
    expert_gate,
    expert_up,
    expert_down,
    teacher,
    routes,
    cont_lengths,
    valid_mask,
):
    rows_dev, groups, model_width = hidden_in.shape
    tokens = rows_dev * groups
    head_count = lax.axis_size("head")
    cols = lax.axis_size("blk")
    devices = head_count * cols
    slices = devices // EXPERTS
    pairs = devices // 2
    shard = w_query.shape[0]
    hidden = shared_gate.shape[1]
    bf16, f32 = jnp.bfloat16, jnp.float32
    me = flat_index(cols)
    core, pair = lax.rem(me, 2), lax.div(me, 2)
    holds, unit = unit_place(pair)

    packed = jnp.concatenate([w_query, w_key, w_value], axis=1)
    router_size = shard * EXPERTS
    router_rows = -(-router_size // 128)
    router_pad = router_rows * 128 - router_size

    def in_rows(gains_first, gains_second, scalar, router):
        count = gains_first.shape[0]
        pieces = [
            jnp.pad(gains_first.astype(f32), ((0, 0), (0, 128 - shard))),
            jnp.pad(gains_second.astype(f32), ((0, 0), (0, 128 - shard))),
            jnp.broadcast_to(scalar, (count, 128)),
            jnp.pad(router.astype(f32), ((0, 0), (0, router_pad + (5 - router_rows) * 128))),
        ]
        return jnp.concatenate(pieces, axis=1).reshape(count, 8, 128)

    small = in_rows(
        norm_attn[None],
        norm_ffn[None],
        jnp.sum(valid_mask.astype(f32)),
        w_router.reshape(1, router_size),
    )[0]
    all_packed, all_small = gather_all([packed, small], cols, 0)
    proj_mat = all_packed.reshape(model_width, 3 * model_width)
    all_small = all_small.reshape(devices, 8, 128)
    gain_attn = all_small[:, 0, :shard].reshape(model_width)
    gain_ffn = all_small[:, 1, :shard].reshape(model_width)
    valid_total = jnp.sum(all_small[:, 2, 0])
    route_mat = (
        all_small[:, 3 : 3 + router_rows]
        .reshape(devices, router_rows * 128)[:, :router_size]
        .reshape(model_width, EXPERTS)
        .astype(bf16)
    )

    wide = jnp.concatenate([shared_gate, shared_up], axis=1)

    local_pos = me * rows_dev + jnp.arange(rows_dev, dtype=jnp.int32)
    local_begin = segment_starts(local_pos, cont_lengths)
    cosine, sine = rotary_tables(local_pos, local_begin)
    flat_in = hidden_in.reshape(tokens, model_width)
    def rotated(halves, sine_now):
        first, second = halves[:, 0], halves[:, 1]
        return jnp.concatenate(
            [first * cosine - second * sine_now, second * cosine + first * sine_now], axis=1
        )

    def by_unit(blocks):
        rows = blocks.shape[1]
        return (
            blocks.reshape(HEADS, rows, rows_dev, groups)
            .transpose(3, 0, 1, 2)
            .reshape(groups * HEADS, rows, rows_dev)
        )

    def by_head(blocks):
        rows = blocks.shape[1]
        return (
            blocks.reshape(groups, HEADS, rows, rows_dev)
            .transpose(1, 2, 3, 0)
            .reshape(HEADS, rows, tokens)
        )

    at_home = rows_dev == TILE and groups == 1 and slices == 2
    if at_home:
        normed_attn, scaling_attn, q_blocks, kv_blocks = project(
            flat_in, gain_attn, proj_mat, cosine, sine, cols, 1
        )
    else:
        normed_exact, scaling_attn = root_norm(flat_in, gain_attn)
        normed_attn = normed_exact.astype(bf16)
        projected = dot(proj_mat, normed_attn, (0, 1)).reshape(
            3, HEADS, 2, HEAD_DIM // 2, tokens
        )
        qkv_blocks = jnp.concatenate(
            [
                rotated(projected[0], sine),
                rotated(projected[1], sine),
                projected[2].reshape(HEADS, HEAD_DIM, tokens),
            ],
            axis=1,
        ).astype(bf16)
        q_blocks, kv_blocks = to_units(by_unit(qkv_blocks), cols, True, 1)

    unit_lengths = lax.dynamic_slice_in_dim(
        cont_lengths, jnp.minimum(unit // HEADS, groups - 1), 1, axis=0
    )
    place = (
        (2 * jnp.arange(pairs, dtype=jnp.int32) + core)[:, None] * rows_dev
        + jnp.arange(rows_dev, dtype=jnp.int32)
    ).reshape(-1)
    run = segment_starts(place, unit_lengths).reshape(-1, 1, TILE)
    queries, keys_values = to_tiles(q_blocks), to_tiles(kv_blocks)
    if at_home:
        exact, lse, attended, out_mat, share_down, wide = attend_home(
            queries, keys_values, run, [w_out, shared_down], [wide], cols, 2
        )
    else:
        exact, low, lse = attend(queries, keys_values, run, rows_dev)
        (attended,) = to_tokens([from_tiles(low, rows_dev)], cols, 2)
        out_mat, share_down, share_wide = gather_all([w_out, shared_down, wide], cols, 11)
        share_wide = share_wide.reshape(model_width, 2 * hidden)
    out_mat = out_mat.reshape(model_width, model_width)
    share_down = share_down.reshape(hidden, model_width)
    attended = by_head(attended).reshape(model_width, tokens)

    residual_mid = flat_in + dot(attended, out_mat, (0, 0))
    normed_mid, scaling_ffn = root_norm(residual_mid, gain_ffn)
    normed_ffn = normed_mid.astype(bf16)

    route_flat = routes.reshape(tokens, TOP)
    route_onehot = (route_flat[:, :, None] == jnp.arange(EXPERTS, dtype=jnp.int32)).astype(f32)
    flat_routes = route_flat.reshape(-1)
    route_hits = (flat_routes[:, None] == jnp.arange(EXPERTS, dtype=jnp.int32)).astype(bf16)
    order = jnp.arange(tokens * TOP, dtype=jnp.int32)
    before = dot((order[None, :] < order[:, None]).astype(bf16), route_hits, (1, 0))
    ranking = jnp.sum(before * route_hits.astype(f32), axis=1).astype(jnp.int32)
    slot_of = (flat_routes * CAP + ranking).reshape(tokens, TOP)
    slot_ids = jnp.arange(EXPERTS * CAP, dtype=jnp.int32)
    place_first = (slot_ids[:, None] == slot_of[None, :, 0]).astype(bf16)
    place_second = (slot_ids[:, None] == slot_of[None, :, 1]).astype(bf16)

    sending = dot(place_first + place_second, normed_ffn, (1, 0)).astype(bf16)
    sending = sending.reshape(EXPERTS, CAP, model_width)

    logits = dot(normed_ffn, route_mat, (1, 0))
    chosen = jnp.sum(route_onehot * logits[:, None, :], axis=-1)
    gate_probs = jax.nn.softmax(chosen, axis=1)
    out = jax.ShapeDtypeStruct
    if at_home:
        returned, share_wide, *kept = expert_forward(
            sending, expert_gate, expert_up, expert_down, [wide], cols, 3
        )
        share_wide = share_wide.reshape(model_width, 2 * hidden)
        shared_in = dot(normed_ffn, share_wide, (1, 0))
        shared_hidden = (apply_silu(shared_in[:, :hidden]) * shared_in[:, hidden:]).astype(bf16)
        shared_results = [
            shared_in[:, :hidden].astype(bf16),
            shared_in[:, hidden:].astype(bf16),
            shared_hidden,
            dot(shared_hidden, share_down, (1, 0)),
        ]
    else:
        shared_work = Work(
            [normed_ffn, share_wide, share_down],
            [
                out((tokens, hidden), bf16),
                out((tokens, hidden), bf16),
                out((tokens, hidden), bf16),
                out((tokens, model_width), f32),
            ],
            shared_forward,
        )
        (arrived,) = spread([sending], cols, slices, EXPERTS, 3)
        arrived = arrived.reshape(devices * CAP, model_width)
        inner_gate = dot(arrived, expert_gate, (1, 0))
        inner_up = dot(arrived, expert_up, (1, 0))
        inner_hidden = (apply_silu(inner_gate) * inner_up).astype(bf16)
        partial_out = dot(inner_hidden, expert_down, (1, 0)).astype(bf16)
        returned, *shared_results = collect(
            [partial_out.reshape(slices, EXPERTS, CAP, model_width)], cols, 4, shared_work
        )
    shared_gate_in, shared_up_in, shared_hidden, shared_out = shared_results
    expert_rows = returned.reshape(EXPERTS * CAP, model_width)
    routed_first = dot(place_first, expert_rows, (0, 0))
    routed_second = dot(place_second, expert_rows, (0, 0))
    mixture = gate_probs[:, 0:1] * routed_first + gate_probs[:, 1:2] * routed_second
    layer_flat = residual_mid + shared_out + mixture

    keep_rows = valid_mask.reshape(tokens).astype(f32)[:, None]
    deviation = layer_flat - teacher.reshape(tokens, model_width)
    loss_local = jnp.sum(keep_rows * deviation * deviation)
    grad_rows = keep_rows * deviation * (tokens * devices / valid_total)
    back_first = (gate_probs[:, 0:1] * grad_rows).astype(bf16)
    back_second = (gate_probs[:, 1:2] * grad_rows).astype(bf16)
    back_send = (
        dot(place_first, back_first, (1, 0)) + dot(place_second, back_second, (1, 0))
    ).astype(bf16)
    shared_work = Work(
        [
            grad_rows.astype(bf16),
            normed_ffn,
            shared_gate_in,
            shared_up_in,
            shared_hidden,
            share_wide,
            share_down,
        ],
        [
            out(share_wide.shape, bf16),
            out(share_down.shape, bf16),
            out((tokens, model_width), f32),
        ],
        shared_backward,
        {0: 5, 1: 6},
    )
    back_send = back_send.reshape(EXPERTS, CAP, model_width)
    if at_home:
        passed = expert_backward(
            back_send, expert_gate, expert_up, expert_down, kept, shared_work, cols, 5
        )
        back_returned, grad_expert_gate, grad_expert_up, grad_expert_down = passed[:4]
        grad_share_wide, grad_share_down, shared_back = passed[4:]
    else:
        back_arrived, grad_share_wide, grad_share_down, shared_back = spread(
            [back_send], cols, slices, EXPERTS, 5, shared_work
        )
        back_arrived = back_arrived.reshape(devices * CAP, model_width)
        grad_inner = dot(back_arrived, expert_down, (1, 1))
        grad_inner_gate = (grad_inner * inner_up * silu_slope(inner_gate)).astype(bf16)
        grad_inner_up = (grad_inner * apply_silu(inner_gate)).astype(bf16)
        back_partial = (
            dot(grad_inner_gate, expert_gate, (1, 1)) + dot(grad_inner_up, expert_up, (1, 1))
        ).astype(bf16)
        (back_returned,) = collect(
            [back_partial.reshape(slices, EXPERTS, CAP, model_width)], cols, 6
        )
        grad_expert_down = dot(inner_hidden, back_arrived, (0, 0))
        grad_expert_gate = dot(arrived, grad_inner_gate, (0, 0))
        grad_expert_up = dot(arrived, grad_inner_up, (0, 0))

    grad_gate = jnp.stack(
        [jnp.sum(grad_rows * routed_first, axis=-1), jnp.sum(grad_rows * routed_second, axis=-1)],
        axis=1,
    )
    grad_chosen = gate_probs * (grad_gate - jnp.sum(gate_probs * grad_gate, axis=1, keepdims=True))
    grad_logits = jnp.sum(route_onehot * grad_chosen[:, :, None], axis=1).astype(bf16)
    grad_route_mat = dot(normed_ffn, grad_logits, (0, 0))

    back_rows = back_returned.reshape(EXPERTS * CAP, model_width)
    grad_normed = (
        dot(place_first + place_second, back_rows, (0, 0))
        + dot(grad_logits, route_mat, (1, 1))
        + shared_back
    )

    grad_mid_norm, grad_gain_ffn = root_norm_back(residual_mid, scaling_ffn, gain_ffn, grad_normed)
    grad_mid = grad_rows + grad_mid_norm
    grad_mid_low = grad_mid.astype(bf16)
    grad_attended = dot(out_mat, grad_mid_low, (1, 1)).astype(bf16)
    grad_out_mat = dot(attended, grad_mid_low, (1, 0))
    grad_blocks = by_unit(grad_attended.reshape(HEADS, HEAD_DIM, tokens))
    spots = (2, cols // 4, 2, 2)
    parts = [
        grad_share_wide.reshape(spots + (shard, 2 * hidden)),
        grad_share_down.reshape(spots + shared_down.shape),
        grad_out_mat.astype(bf16).reshape(spots + (shard, model_width)),
    ]
    if at_home:
        dq, dkv, share_sums, grad_share_down, grad_out_sum = attend_back_home(
            queries, keys_values, grad_blocks, exact, lse, run, parts, cols, 10
        )
    else:
        (grad_blocks,) = to_units(grad_blocks, cols, False, 7)
        dq, dkv, share_sums, grad_share_down, grad_out_sum = attend_back(
            queries, keys_values, to_tiles(grad_blocks), exact, lse, run, rows_dev, parts, cols, 10
        )
        dq, dkv = to_tokens([from_tiles(dq, rows_dev), from_tiles(dkv, rows_dev)], cols, 8)
    dq, dkv = by_head(dq).astype(f32), by_head(dkv)

    def halves_of(rows):
        return rows.reshape(HEADS, 2, HEAD_DIM // 2, tokens)

    grad_proj = jnp.concatenate(
        [
            rotated(halves_of(dq), -sine).astype(bf16).reshape(model_width, tokens),
            rotated(halves_of(dkv[:, :HEAD_DIM].astype(f32)), -sine)
            .astype(bf16)
            .reshape(model_width, tokens),
            dkv[:, HEAD_DIM:].reshape(model_width, tokens),
        ],
        axis=0,
    )
    grad_normed_attn = dot(grad_proj, proj_mat, (0, 1))
    grad_in_norm, grad_gain_attn = root_norm_back(
        flat_in, scaling_attn, gain_attn, grad_normed_attn
    )
    input_grad = (grad_mid + grad_in_norm).reshape(rows_dev, groups, model_width)

    grad_attn = dot(normed_attn, grad_proj, (0, 1)).astype(bf16)
    tail = in_rows(
        grad_gain_attn.reshape(devices, shard),
        grad_gain_ffn.reshape(devices, shard),
        loss_local,
        grad_route_mat.reshape(devices, router_size),
    )
    attn_sums, tail_sums = reduce_all(
        [grad_attn.reshape(spots + (shard, 3 * model_width)), tail.reshape(spots + (8, 128))],
        cols,
        9,
    )
    loss_value = tail_sums[2, 0] / (valid_total * model_width)
    return (
        layer_flat.reshape(rows_dev, groups, model_width),
        input_grad,
        loss_value,
        attn_sums[:, :model_width],
        attn_sums[:, model_width : 2 * model_width],
        attn_sums[:, 2 * model_width :],
        grad_out_sum,
        tail_sums[0, :shard],
        tail_sums[1, :shard],
        tail_sums[3 : 3 + router_rows].reshape(-1)[:router_size].reshape(shard, EXPERTS),
        share_sums[:, :hidden],
        share_sums[:, hidden:],
        grad_share_down,
        grad_expert_gate,
        grad_expert_up,
        grad_expert_down,
    )


def solution(mesh):
    placed = (
        P(("head", "blk"), None, None),
        P(("head", "blk"), None),
        P(("head", "blk"), None),
        P(("head", "blk"), None),
        P(("head", "blk"), None),
        P(("head", "blk")),
        P(("head", "blk")),
        P(("head", "blk"), None),
        P(("head", "blk"), None),
        P(("head", "blk"), None),
        P(("head", "blk"), None),
        P(None, ("head", "blk")),
        P(None, ("head", "blk")),
        P(("head", "blk"), None),
        P(("head", "blk"), None, None),
        P(("head", "blk"), None, None),
        P(),
        P(("head", "blk"), None),
    )
    return jax.shard_map(
        on_device,
        mesh=mesh,
        in_specs=placed,
        out_specs=(
            P(("head", "blk"), None, None),
            P(("head", "blk"), None, None),
            P(),
            P(("head", "blk"), None),
            P(("head", "blk"), None),
            P(("head", "blk"), None),
            P(("head", "blk"), None),
            P(("head", "blk")),
            P(("head", "blk")),
            P(("head", "blk"), None),
            P(("head", "blk"), None),
            P(("head", "blk"), None),
            P(("head", "blk"), None),
            P(None, ("head", "blk")),
            P(None, ("head", "blk")),
            P(("head", "blk"), None),
        ),
        check_vma=False,
    )
```
